32 devices in a mesh: dp: 4 (over y, x), seq: 8 (over z, core).
Axes of the slice: x: 2, y: 2, z: 4, core: 2. Of those that a mesh axis runs over, the one named last changes fastest.
Arguments:
- tokens: bfloat16 [4, 2048, 1024], P('dp', 'seq'), may hold values from -6 to 6
- segments: int32 [4, 2048], P('dp'), may hold values from 0 to 2047, as said below
- cotangent: bfloat16 [4, 2048, 1024], P('dp', 'seq'), may hold values from -6 to 6
- in_weight: float32 [1024, 3072], P(('dp', 'seq')), may hold values from -0.1875 to 0.1875
- out_weight: float32 [1024, 1024], P(('dp', 'seq')), may hold values from -0.1875 to 0.1875
- gate_weight: float32 [1024, 4608], P(('dp', 'seq')), may hold values from -0.1875 to 0.1875
- up_weight: float32 [1024, 4608], P(('dp', 'seq')), may hold values from -0.1875 to 0.1875
- down_weight: float32 [4608, 1024], P(('dp', 'seq')), may hold values from -0.09375 to 0.09375
- norm_one: float32 [1024], P(('dp', 'seq')), may hold values from 0.1 to 1.9
- norm_two: float32 [1024], P(('dp', 'seq')), may hold values from 0.1 to 1.9
- kernel: float32 [3, 1024], P(None, ('dp', 'seq')), may hold values from -3.5 to 3.5
Outputs:
- output: bfloat16 [4, 2048, 1024], P('dp', 'seq')
- grad_tokens: bfloat16 [4, 2048, 1024], P('dp', 'seq')
- grad_in: float32 [1024, 3072], P(('dp', 'seq'))
- grad_out: float32 [1024, 1024], P(('dp', 'seq'))
- grad_gate: float32 [1024, 4608], P(('dp', 'seq'))
- grad_up: float32 [1024, 4608], P(('dp', 'seq'))
- grad_down: float32 [4608, 1024], P(('dp', 'seq'))
- grad_norm_one: float32 [1024], P(('dp', 'seq'))
- grad_norm_two: float32 [1024], P(('dp', 'seq'))
- grad_kernel: float32 [3, 1024], P(None, ('dp', 'seq'))
The draws below stay inside these ranges and needn't reach their ends.
Inputs may be any that keep to these rules, and one draw needn't show every extreme that they name: `segments`: within a sequence document numbers never fall and differ between documents; a document's number is the position of its first token in the sequence, except that the last document of each sequence is numbered 2048 - 1; documents hold about 200 to 2000 tokens; no document but the first begins at the first two positions of a block of 256 tokens.
All inputs are finite; a program needn't handle non-finite values.
Results may differ from the reference program's by a relative error of at most 0.014.
The reference program's roundings to bfloat16 on the way count: a program that leaves them out, or rounds other values in their place, can miss the bound.
Values may be sent and summed in bfloat16 or wider, within the bound.
A program may use at most 192 MiB of HBM per device.

```python
import jax
import jax.numpy as jnp
from jax import lax

D = 1024
FF = 4608
TOK_DEV = 256
DOC_MIN = 200
DOC_MAX = 2000
SEQS = 4
LENGTH = 2048


def draw_segments(key, part):
    key = jax.random.fold_in(key, 11)
    count_docs = LENGTH // DOC_MIN + 2
    doc_lengths = jax.random.randint(key, (SEQS, count_docs), DOC_MIN, DOC_MAX + 1)
    doc_ends = jnp.cumsum(doc_lengths, axis=1)
    doc_starts = doc_ends - doc_lengths
    at_edge = (doc_starts % TOK_DEV < 2) & (doc_starts > 0)
    moved = (doc_starts + 2 * at_edge.astype(jnp.int32)).astype(jnp.int32)
    places = jnp.arange(LENGTH, dtype=jnp.int32)
    begun = jnp.sum((moved[:, None, :] <= places[None, :, None]).astype(jnp.int32), axis=2) - 1
    first_place = jnp.take_along_axis(moved, begun, axis=1)
    last_doc = begun[:, LENGTH - 1:LENGTH]
    numbered = jnp.where(begun == last_doc, LENGTH - 1, first_place)
    return numbered.astype(jnp.int32)


def levels(rng, shape, pieces, smallest, high):
    def one(dim, parts):
        steps = jax.random.uniform(jax.random.fold_in(jax.random.fold_in(rng, 6), dim), (parts,), jnp.float32, smallest / len(pieces), high / len(pieces))
        return jnp.repeat(jnp.exp(steps), shape[dim] // parts).reshape((-1,) + (1,) * (len(shape) - dim - 1))

    loudness = one(*pieces[0])
    for cut in pieces[1:]:
        loudness = loudness * one(*cut)
    return loudness


def normal_values(rng, shape, deviation, limit, split=(), kind=jnp.bfloat16):
    entries = jax.random.normal(rng, shape, jnp.float32) * deviation
    if len(split) > 0:
        entries = levels(rng, shape, split, -0.22, 0.18) * entries
    return jnp.clip(entries, min=-limit, max=limit).astype(kind)


def setup_inputs(seed: int = 0) -> dict:
    key_of = jax.random.split(jax.random.key(seed), 12)
    tokens = normal_values(key_of[0], (SEQS, LENGTH, D), 1.0, 6.0, ((0, 4), (1, 8)))
    segments = draw_segments(jax.random.fold_in(key_of[11], 71), 0)
    cotangent = normal_values(key_of[2], (SEQS, LENGTH, D), 1.0, 6.0, ((0, 4), (1, 8)))
    in_weight = normal_values(key_of[3], (D, 3 * D), D ** -0.5, 0.1875, ((0, 32),), jnp.float32)
    out_weight = normal_values(key_of[4], (D, D), D ** -0.5, 0.1875, ((0, 32),), jnp.float32)
    gate_weight = normal_values(key_of[5], (D, FF), D ** -0.5, 0.1875, ((0, 32),), jnp.float32)
    up_weight = normal_values(key_of[6], (D, FF), D ** -0.5, 0.1875, ((0, 32),), jnp.float32)
    down_weight = normal_values(key_of[7], (FF, D), FF ** -0.5, 0.09375, ((0, 32),), jnp.float32)
    norm_one = jnp.clip(1.0 + 0.18 * jax.random.normal(key_of[8], (D,), jnp.float32), 0.1, 1.9)
    norm_two = jnp.clip(1.0 + 0.18 * jax.random.normal(key_of[9], (D,), jnp.float32), 0.1, 1.9)
    kernel = normal_values(key_of[10], (3, D), 3 ** -0.5, 3.5, ((1, 32),), jnp.float32)
    return {"tokens": tokens, "segments": segments, "cotangent": cotangent, "in_weight": in_weight, "out_weight": out_weight, "gate_weight": gate_weight, "up_weight": up_weight, "down_weight": down_weight, "norm_one": norm_one, "norm_two": norm_two, "kernel": kernel}


epsilon = 1e-05

@jax.custom_vjp
def low(v):
    return lax.optimization_barrier(v.astype(jnp.bfloat16)).astype(jnp.float32)

@jax.custom_vjp
def low_back(v):
    return v

def low_keep(v):
    return (low(v), None)

def low_pass(kept, grad):
    return (grad,)

def back_keep(v):
    return (v, None)

def back_low(kept, grad):
    return (low(grad),)
low.defvjp(low_keep, low_pass)
low_back.defvjp(back_keep, back_low)

def product_hi(left, right):
    return jnp.dot(left, right, precision=lax.Precision.HIGHEST)

def rms_unit(values):
    return values * lax.rsqrt(lax.optimization_barrier(jnp.mean(values * values, axis=1, keepdims=True)) + epsilon)

def forward(resident, doc_ids, params):
    in_mat, out_mat, gate_mat, up_mat, down_mat, gain_a, gain_b, kernel_f = params
    feature_width = resident.shape[1]
    normed_a = low(rms_unit(resident) * low(gain_a))
    mixed = low_back(product_hi(normed_a, low(in_mat)))
    b_part = mixed[:, :feature_width]
    c_part = mixed[:, feature_width:2 * feature_width]
    x_part = mixed[:, 2 * feature_width:]
    conv_in = low(b_part * x_part)
    taps = low(kernel_f)
    zero_one = jnp.zeros((1, feature_width), jnp.float32)
    zero_two = jnp.zeros((2, feature_width), jnp.float32)
    prev_one = jnp.concatenate([zero_one, conv_in[:-1]], axis=0)
    prev_two = jnp.concatenate([zero_two, conv_in[:-2]], axis=0)
    mask_one = jnp.concatenate([jnp.zeros((1,), jnp.float32), (doc_ids[1:] == doc_ids[:-1]).astype(jnp.float32)])[:, None]
    mask_two = jnp.concatenate([jnp.zeros((2,), jnp.float32), (doc_ids[2:] == doc_ids[:-2]).astype(jnp.float32)])[:, None]
    convolved = taps[0] * conv_in + taps[1] * (prev_one * mask_one) + taps[2] * (prev_two * mask_two)
    gated = low(c_part * convolved)
    hidden = resident + low_back(product_hi(gated, low(out_mat)))
    normed_b = low(rms_unit(hidden) * low(gain_b))
    gate_pre = low_back(product_hi(normed_b, low(gate_mat)))
    up_pre = low_back(product_hi(normed_b, low(up_mat)))
    active = low(jax.nn.silu(gate_pre) * up_pre)
    return hidden + low_back(product_hi(active, low(down_mat)))

def reference(tokens, segments, cotangent, in_weight, out_weight, gate_weight, up_weight, down_weight, norm_one, norm_two, kernel):
    weights = (in_weight, out_weight, gate_weight, up_weight, down_weight, norm_one, norm_two, kernel)

    def one_sequence(totals, items):
        resident, doc_ids, grad_seed = items

        def apply(resident_f, params):
            return forward(resident_f, doc_ids, params)
        result, pullback = jax.vjp(apply, resident.astype(jnp.float32), weights)
        grad_resident, grad_params = pullback(grad_seed.astype(jnp.float32))
        totals = jax.tree.map(lambda first, second: first + second, totals, grad_params)
        return (totals, (result.astype(jnp.bfloat16), grad_resident.astype(jnp.bfloat16)))
    starting = jax.tree.map(lambda array: jnp.zeros(array.shape, jnp.float32), weights)
    totals, stacked = lax.scan(one_sequence, starting, (tokens, segments, cotangent))
    return (stacked[0], stacked[1], totals[0], totals[1], totals[2], totals[3], totals[4], totals[5], totals[6], totals[7])
```

```python
import functools

import jax
import jax.numpy as jnp
from jax import lax
from jax.experimental import pallas as pl
from jax.experimental.pallas import tpu as pltpu
from jax.sharding import PartitionSpec as P

epsilon = 1e-05
MESH = pl.DeviceIdType.MESH
BF = jnp.bfloat16
F32 = jnp.float32


def dot_nn(a, b):
    return jnp.dot(a, b, preferred_element_type=F32)


def dot_nt(a, b):
    return lax.dot_general(a, b, (((1,), (1,)), ((), ())), preferred_element_type=F32)


def dot_tn(a, b):
    return lax.dot_general(a, b, (((0,), (0,)), ((), ())), preferred_element_type=F32)


def when(pred, body):
    if pred is True:
        body()
    else:
        pl.when(pred)(body)


GAIN, IN, OUT, GU0, DOWN, GU1, GU2 = range(7)
UNITS = (GAIN, IN, OUT, GU0, DOWN, GU1, GU2)
SLOT = {IN: 0, GU0: 1, GU1: 2, GU2: 3}
AX, AZ, AO, AR = range(4)


def block_kernel(
    dims,
    x_ref, do_ref, mask_ref, gain_ref, win_ref, wout_ref, wg_ref, wu_ref, wdn_ref,
    out_ref, gtok_ref, rbuf, gout_ref, gdown_ref, gsmall_ref,
    stage, wall, wo, wd, gb, gv, xa, ma, za, oa, ra, big, mbuf, pbuf, ybuf, halo_p, halo_q,
    sb_a, rx_a, ry_a, fx_a, fy_a, rx_b, ry_b, fx_b, fy_b, hid, own, dh,
    gw, gd, go, dd_g, dd_d, dd_o, up_g, up_d, up_o, dn_g, dn_d, dn_o,
    gvec, sg, sgx, s2, dd_s, up_s, dn_s,
    zs, zr, ws, wr, gs, gr, ms, mr, hs, hr, ags, agr, rss, rsr, ds_, dr_, us, ur, vs, vr, qs, qr, ss, sr, ins,
):
    tok, wid, nz, rows, ch, fs, cj, uw, drows = dims
    half = tok // 2
    d = lax.axis_index("dp")
    s = lax.axis_index("seq")
    x = lax.rem(d, 2)
    y = lax.div(d, 2)
    z = lax.div(s, 2)
    c = lax.rem(s, 2)
    xn = 2 * y + (1 - x)
    yn = 2 * (1 - y) + x
    dg = 2 * (1 - y) + (1 - x)
    oc = 1 - c
    top = nz - 1
    to_x, to_y, to_g = (xn, s), (yn, s), (dg, s)
    to_sib = (d, 2 * z + oc)
    to_up, to_dn = (d, s + 2), (d, s - 2)
    to_next, to_prev = (d, s + 1), (d, s - 1)
    pending = []

    def copy(src, dst, ssem, rsem, tgt):
        return pltpu.make_async_remote_copy(
            src_ref=src(), dst_ref=dst(), send_sem=ssem(), recv_sem=rsem(), device_id=tgt, device_id_type=MESH
        )

    def send(tag, pred, src, dst, ssem, rsem, tgt):
        when(pred, lambda: copy(src, dst, ssem, rsem, tgt).start())
        pending.append((tag, pred, src, dst, ssem, rsem, tgt))

    def recv(pred, dst, rsem):
        when(pred, lambda: copy(dst, dst, rsem, rsem, to_sib).wait_recv())

    def drain(tag=None):
        keep = []
        for item in pending:
            if tag is None or item[0] == tag:
                when(item[1], lambda item=item: copy(*item[2:]).wait_send())
            else:
                keep.append(item)
        pending[:] = keep

    barrier = pltpu.get_barrier_semaphore()

    def greet(tgt):
        pl.semaphore_signal(barrier, inc=1, device_id=tgt, device_id_type=MESH)

    for tgt in (to_x, to_y, to_g, to_sib):
        greet(tgt)
    has_up, has_dn = z < top, z > 0
    pl.when(has_up)(lambda: greet(to_up))
    pl.when(has_dn)(lambda: greet(to_dn))
    cross_next = jnp.logical_and(c == 1, z < top)
    cross_prev = jnp.logical_and(c == 0, z > 0)
    pl.when(cross_next)(lambda: greet(to_next))
    pl.when(cross_prev)(lambda: greet(to_prev))
    ones = [jnp.where(p, 1, 0) for p in (has_up, has_dn, cross_next, cross_prev)]
    pl.semaphore_wait(barrier, 4 + ones[0] + ones[1] + ones[2] + ones[3])

    def cols(unit):
        return pl.ds(SLOT[unit] * uw, uw)

    def w_block(unit, zz, cc):
        if unit == GAIN:
            return gb.at[d, zz, cc]
        if unit == OUT:
            return wo.at[pl.ds(pl.multiple_of((2 * zz + cc) * rows, rows), rows), :]
        if unit == DOWN:
            return wd.at[pl.ds(pl.multiple_of((2 * zz + cc) * drows, drows), drows), :]
        return wall.at[:, zz, cc, :, cols(unit)]

    def z_send(unit, pred, zz, ssem, tgt):
        blk = lambda: w_block(unit, zz, c)
        send("w", pred, blk, blk, lambda: zs.at[unit * 13 + ssem], lambda: zr.at[unit * 2 * nz + 2 * zz + c], tgt)

    def z_own(unit):
        z_send(unit, has_up, z, 0, to_up)
        z_send(unit, has_dn, z, 3, to_dn)
        z_send(unit, True, z, 6, to_sib)

    def z_fwd(unit, k):
        low, high = z - k, z + k
        has_low, has_high = z >= k, z + k <= top
        recv(has_low, lambda: w_block(unit, low, c), lambda: zr.at[unit * 2 * nz + 2 * low + c])
        if k < top:
            z_send(unit, jnp.logical_and(has_low, has_up), low, k, to_up)
        z_send(unit, has_low, low, 6 + k, to_sib)
        recv(has_high, lambda: w_block(unit, high, c), lambda: zr.at[unit * 2 * nz + 2 * high + c])
        if k < top:
            z_send(unit, jnp.logical_and(has_high, has_dn), high, 3 + k, to_dn)
        z_send(unit, has_high, high, 9 + k, to_sib)

    def z_finish(unit):
        for zz in range(nz):
            recv(True, lambda zz=zz: w_block(unit, zz, oc), lambda zz=zz: zr.at[unit * 2 * nz + 2 * zz + oc])

    peers = ((xn, to_x), (yn, to_y), (dg, to_g))

    def w_slice(unit):
        u = SLOT[unit]
        wall[d, z, c, :, cols(unit)] = stage[d, :, cols(unit)]
        for k, (idx, tgt) in enumerate(peers):
            send(
                "stage", True,
                lambda idx=idx: stage.at[idx, :, cols(unit)],
                lambda: wall.at[d, z, c, :, cols(unit)],
                lambda k=k: ws.at[u * 3 + k], lambda k=k: wr.at[u * 3 + k], tgt,
            )

    def w_slice_wait(unit):
        u = SLOT[unit]
        for k, (idx, _) in enumerate(peers):
            recv(True, lambda idx=idx: wall.at[idx, z, c, :, cols(unit)], lambda k=k: wr.at[u * 3 + k])

    lo, hi = pl.ds(0, half), pl.ds(half, half)

    def ag_send(a, buf, idx, part, k, rk, tgt):
        blk = lambda: buf.at[idx, part, :]
        send("ag", True, blk, blk, lambda: ags.at[a * 6 + k], lambda: agr.at[a * 6 + rk], tgt)

    def ag_start(a, buf):
        ag_send(a, buf, d, hi, 0, 1, to_x)
        ag_send(a, buf, d, lo, 1, 2, to_y)
        ag_send(a, buf, d, lo, 2, 0, to_x)
        ag_send(a, buf, d, hi, 3, 3, to_y)

    def ag_recv(a, buf, idx, part, rk):
        recv(True, lambda: buf.at[idx, part, :], lambda: agr.at[a * 6 + rk])

    def ag_fwd(a, buf):
        ag_recv(a, buf, yn, lo, 2)
        ag_send(a, buf, yn, lo, 4, 4, to_x)
        ag_recv(a, buf, xn, hi, 1)
        ag_send(a, buf, xn, hi, 5, 5, to_y)

    def ag_near(a, buf):
        ag_recv(a, buf, xn, lo, 0)
        ag_recv(a, buf, yn, hi, 3)

    def ag_far(a, buf):
        ag_recv(a, buf, dg, lo, 4)
        ag_recv(a, buf, dg, hi, 5)

    def rs_send(r, tag, src, dst, k, tgt):
        send(tag, True, src, dst, lambda: rss.at[r * 6 + k], lambda: rsr.at[r * 6 + k], tgt)

    def rs_run(r, sb, bufs, tile, tag, first=0):
        wide = pl.ds(first, wid)
        rx, ry, fx, fy = bufs
        sb[dg, :, wide] = tile(dg).astype(BF)
        rs_send(r, tag, lambda: sb.at[dg, lo, wide], lambda: fx, 0, to_x)
        rs_send(r, tag, lambda: sb.at[dg, hi, wide], lambda: fy, 1, to_y)
        sb[xn, :, wide] = tile(xn).astype(BF)
        rs_send(r, tag, lambda: sb.at[xn, lo, wide], lambda: rx.at[lo, :], 2, to_x)
        sb[yn, :, wide] = tile(yn).astype(BF)
        rs_send(r, tag, lambda: sb.at[yn, hi, wide], lambda: ry.at[hi, :], 3, to_y)

    def rs_pass(r, sb, bufs, tag, first=0):
        wide = pl.ds(first, wid)
        rx, ry, fx, fy = bufs
        recv(True, lambda: fx, lambda: rsr.at[r * 6 + 0])
        sb[yn, lo, wide] = (sb[yn, lo, wide].astype(F32) + fx[...].astype(F32)).astype(BF)
        rs_send(r, tag, lambda: sb.at[yn, lo, wide], lambda: ry.at[lo, :], 4, to_y)
        recv(True, lambda: fy, lambda: rsr.at[r * 6 + 1])
        sb[xn, hi, wide] = (sb[xn, hi, wide].astype(F32) + fy[...].astype(F32)).astype(BF)
        rs_send(r, tag, lambda: sb.at[xn, hi, wide], lambda: rx.at[hi, :], 5, to_x)

    def rs_wait(r, bufs):
        rx, ry, fx, fy = bufs
        recv(True, lambda: rx.at[lo, :], lambda: rsr.at[r * 6 + 2])
        recv(True, lambda: ry.at[hi, :], lambda: rsr.at[r * 6 + 3])
        recv(True, lambda: ry.at[lo, :], lambda: rsr.at[r * 6 + 4])
        recv(True, lambda: rx.at[hi, :], lambda: rsr.at[r * 6 + 5])

    bufs_a = (rx_a, ry_a, fx_a, fy_a)
    bufs_b = (rx_b, ry_b, fx_b, fy_b)

    def g_own(unit, zz, cc):
        if unit == GAIN:
            return s2.at[zz, cc]
        if unit == OUT:
            return go.at[pl.ds(pl.multiple_of((2 * zz + cc) * rows, rows), rows), :]
        if unit == DOWN:
            return gd.at[pl.ds(pl.multiple_of((2 * zz + cc) * drows, drows), drows), :]
        return gw.at[:, zz, cc, :, cols(unit)]

    def g_in(unit, trio, zz):
        buf = trio[{GAIN: 3, OUT: 2, DOWN: 1}.get(unit, 0)]
        if unit in SLOT:
            return buf.at[zz, :, :, cols(unit)]
        return buf.at[zz]

    t_dd = (dd_g, dd_d, dd_o, dd_s)
    t_up = (up_g, up_d, up_o, up_s)
    t_dn = (dn_g, dn_d, dn_o, dn_s)

    def g_pair(unit):
        for zz in range(nz):
            send(
                "g", True, lambda zz=zz: g_own(unit, zz, oc), lambda zz=zz: g_in(unit, t_dd, zz),
                lambda zz=zz: ds_.at[unit * nz + zz], lambda zz=zz: dr_.at[unit * nz + zz], to_sib,
            )

    def g_pair_wait(unit):
        for zz in range(nz):
            recv(True, lambda zz=zz: g_in(unit, t_dd, zz), lambda zz=zz: dr_.at[unit * nz + zz])

    def g_add(unit, dst, parts):
        shape = dst.shape
        if len(shape) == 3:
            for k in range(shape[0]):
                dst[k] = sum(p[k].astype(F32) for p in parts).astype(dst.dtype)
        else:
            dst[...] = sum(p[...].astype(F32) for p in parts).astype(dst.dtype)

    def g_up(unit, cond):
        for zt in range(top, 0, -1):
            pred = jnp.logical_and(cond, z < zt)
            mine, pair, came = (lambda: g_own(unit, zt, c)), (lambda: g_in(unit, t_dd, zt)), (lambda: g_in(unit, t_up, zt - 1))

            def first():
                g_add(unit, mine(), (mine(), pair()))

            def later():
                g_add(unit, mine(), (mine(), pair(), came()))

            recv(jnp.logical_and(pred, z > 0), came, lambda: ur.at[unit * top + zt - 1])
            pl.when(jnp.logical_and(pred, z == 0))(first)
            pl.when(jnp.logical_and(pred, z > 0))(later)
            send("g", pred, lambda zt=zt: g_own(unit, zt, c), lambda zt=zt: g_in(unit, t_up, zt - 1),
                 lambda zt=zt: us.at[(unit * top + zt - 1) * 2 + (0 if cond is low_z else 1)],
                 lambda zt=zt: ur.at[unit * top + zt - 1], to_up)

    def g_down(unit):
        for zt in range(top):
            pred = z > zt
            mine, pair, came = (lambda: g_own(unit, zt, c)), (lambda: g_in(unit, t_dd, zt)), (lambda: g_in(unit, t_dn, zt))

            def first():
                g_add(unit, mine(), (mine(), pair()))

            def later():
                g_add(unit, mine(), (mine(), pair(), came()))

            recv(jnp.logical_and(pred, z < top), came, lambda: vr.at[unit * top + zt])
            pl.when(jnp.logical_and(pred, z == top))(first)
            pl.when(jnp.logical_and(pred, z < top))(later)
            send("g", pred, lambda zt=zt: g_own(unit, zt, c), lambda zt=zt: g_in(unit, t_dn, zt),
                 lambda zt=zt: vs.at[unit * top + zt], lambda zt=zt: vr.at[unit * top + zt], to_dn)

    low_z = z < nz // 2
    high_z = z >= nz // 2

    def g_line(unit):
        g_up(unit, low_z)
        g_down(unit)
        g_up(unit, high_z)

    def g_last(unit, acc):
        up_ref = lambda: g_in(unit, t_up, z - 1)
        dn_ref = lambda: g_in(unit, t_dn, z)
        recv(has_dn, up_ref, lambda: ur.at[unit * top + z - 1])
        recv(has_up, dn_ref, lambda: vr.at[unit * top + z])
        g_add(unit, acc, (g_own(unit, z, c), g_in(unit, t_dd, z)))
        pl.when(has_dn)(lambda: g_add(unit, acc, (acc, up_ref())))
        pl.when(has_up)(lambda: g_add(unit, acc, (acc, dn_ref())))

    def g_rows(unit):
        facc = mbuf.at[:, pl.ds(0, rows), :]
        g_last(unit, facc)
        u = SLOT[unit]
        for k in range(4):
            stage[k, :, cols(unit)] = facc[k].astype(BF)
        rbuf[d, :, cols(unit)] = facc[d].astype(BF)
        for k, (idx, tgt) in enumerate(peers):
            send(
                "stage", True,
                lambda idx=idx: stage.at[idx, :, cols(unit)],
                lambda: rbuf.at[d, :, cols(unit)],
                lambda k=k: qs.at[u * 3 + k], lambda k=k: qr.at[u * 3 + k], tgt,
            )

    def g_rows_wait(unit):
        u = SLOT[unit]
        for k, (idx, _) in enumerate(peers):
            recv(True, lambda idx=idx: rbuf.at[idx, :, cols(unit)], lambda k=k: qr.at[u * 3 + k])

    count = 4 * fs // uw

    def wide_in(i):
        ref = wg_ref if i < count else wu_ref
        return pltpu.make_async_copy(
            ref.at[:, pl.ds((i % count) * uw, uw)], mbuf.at[i // 8, pl.ds((i % 8) * rows, rows), :], ins.at[i]
        )

    def wide_read(i, first, n):
        b = i * count + first // uw
        return mbuf[b // 8, pl.ds((b % 8) * rows, rows), pl.ds(first % uw, n)]

    for i in range(2 * count):
        wide_in(i).start()
    for k in range(4):
        for p in range(3):
            stage[k, :, pl.ds(p * ch, ch)] = win_ref[:, pl.ds(p * wid + k * ch, ch)].astype(BF)
    w_slice(IN)
    gb[d, z, c] = gain_ref[...]
    z_own(GAIN)
    xa[d] = x_ref[...]
    ag_start(AX, xa)
    ma[d] = mask_ref[...]
    for k, (idx, tgt) in enumerate(peers):
        send("ag", True, lambda: ma.at[d], lambda: ma.at[d], lambda k=k: ms.at[k], lambda k=k: mr.at[k], tgt)
    wo[pl.ds(pl.multiple_of(s * rows, rows), rows), :] = wout_ref[...].astype(BF)
    for i in range(2 * count):
        wide_in(i).wait()
    for k in range(4):
        for j in range(3):
            stage[k, :, pl.ds((1 + j) * uw, cj)] = wide_read(0, k * fs + j * cj, cj).astype(BF)
            stage[k, :, pl.ds((1 + j) * uw + cj, cj)] = wide_read(1, k * fs + j * cj, cj).astype(BF)
    w_slice_wait(IN)
    z_own(IN)
    z_own(OUT)
    for unit in (GU0, GU1, GU2):
        w_slice(unit)
    wd[pl.ds(pl.multiple_of(s * drows, drows), drows), :] = wdn_ref[...].astype(BF)
    z_fwd(GAIN, 1)
    z_fwd(IN, 1)
    ag_fwd(AX, xa)
    z_fwd(GAIN, 2)
    z_fwd(IN, 2)
    z_fwd(OUT, 1)
    w_slice_wait(GU0)
    z_own(GU0)
    z_fwd(GAIN, 3)
    z_finish(GAIN)
    for k, (idx, tgt) in enumerate(peers):
        send("w", True, lambda: gb.at[d], lambda: gb.at[d], lambda k=k: gs.at[k], lambda k=k: gr.at[k], tgt)
    z_fwd(IN, 3)
    z_fwd(OUT, 2)
    ag_near(AX, xa)
    for k, (idx, _) in enumerate(peers):
        recv(True, lambda idx=idx: gb.at[idx], lambda k=k: gr.at[k])
    per = 128 // rows
    for g in range(wid // 128):
        tot = None
        for i in range(g * per, (g + 1) * per):
            dd, q = i // (2 * nz), i % (2 * nz)
            piece = gb[dd, q // 2, q % 2].astype(F32)
            tot = piece if tot is None else tot + piece
        gv[:, pl.ds(g * 128, 128)] = tot
    ag_far(AX, xa)

    step = 32

    def norm_rows(xv):
        return lax.rsqrt(jnp.mean(xv * xv, axis=1, keepdims=True) + epsilon)

    zcol = pl.ds(0, wid)

    def make_z1():
        @pl.loop(0, 4 * tok // step)
        def _(i):
            dd = lax.div(i, tok // step)
            rr = pl.ds(pl.multiple_of(lax.rem(i, tok // step) * step, step), step)
            xv = xa[dd, rr, :].astype(F32)
            big[dd, rr, zcol] = (xv * norm_rows(xv) * gv[0:1, :]).astype(BF)

    make_z1()
    z_finish(IN)
    z_own(DOWN)
    z_fwd(GU0, 1)
    for k, (idx, _) in enumerate(peers):
        recv(True, lambda idx=idx: ma.at[idx], lambda k=k: mr.at[k])

    def unit_w(lo_col, n):
        return wall[:, :, :, :, pl.ds(lo_col, n)].reshape(wid, n)

    @pl.loop(0, 4)
    def _(dd):
        m = dot_nn(big[dd, :, zcol], unit_w(0, uw))
        mbuf[dd] = m
        pbuf[dd] = (m[:, :ch] * m[:, 2 * ch :]).astype(BF)

    tail = 16
    send("halo", s < 2 * nz - 1, lambda: pbuf.at[:, pl.ds(tok - tail, tail), :], lambda: halo_p,
         lambda: hs.at[0], lambda: hr.at[0], to_next)

    @pl.when(s == 0)
    def _():
        halo_p[...] = jnp.zeros_like(halo_p)

    z_fwd(OUT, 3)
    z_finish(OUT)
    recv(s > 0, lambda: halo_p, lambda: hr.at[0])
    tap_cols = pl.ds(pl.multiple_of(d * ch, ch), ch)
    row = lax.broadcasted_iota(jnp.int32, (tok, ch), 0)

    def past(dd):
        cur = pbuf[dd].astype(F32)
        old = halo_p[dd].astype(F32)
        masks = ma[dd].astype(F32)
        one = jnp.where(row == 0, old[tail - 1 : tail], pltpu.roll(cur, 1, 0)) * masks[:, 0:1]
        two = jnp.where(row == 0, old[tail - 2 : tail - 1], jnp.where(row == 1, old[tail - 1 : tail], pltpu.roll(cur, 2, 0)))
        return cur, one, two * masks[:, 1:2], masks

    def convolve(cur, one, two):
        return gv[2:3, tap_cols] * cur + gv[3:4, tap_cols] * one + gv[4:5, tap_cols] * two

    @pl.loop(0, 4)
    def _(dd):
        cur, one, two, _ = past(dd)
        ybuf[dd] = (mbuf[dd, :, pl.ds(ch, ch)] * convolve(cur, one, two)).astype(BF)

    def h_tile(dd):
        return dot_nn(ybuf[dd], wo[...])

    rs_run(0, sb_a, bufs_a, h_tile, "rs0")
    own[...] = h_tile(d)
    w_slice_wait(GU1)
    z_own(GU1)
    z_fwd(GU0, 2)
    rs_pass(0, sb_a, bufs_a, "rs0")
    z_fwd(DOWN, 1)
    z_fwd(GU0, 3)
    w_slice_wait(GU2)
    z_own(GU2)
    z_fwd(GU1, 1)
    z_fwd(DOWN, 2)
    rs_wait(0, bufs_a)

    @pl.loop(0, tok // step)
    def _(i):
        rr = pl.ds(pl.multiple_of(i * step, step), step)
        h = xa[d, rr, :].astype(F32) + own[rr, :] + rx_a[rr, :].astype(F32) + ry_a[rr, :].astype(F32)
        hid[rr, :] = h
        za[d, rr, :] = (h * norm_rows(h) * gv[1:2, :]).astype(BF)

    ag_start(AZ, za)
    oa[d] = do_ref[...]
    ag_start(AO, oa)
    z_fwd(GU1, 2)
    z_fwd(DOWN, 3)
    z_fwd(GU2, 1)
    ag_fwd(AZ, za)
    z_fwd(GU1, 3)
    z_fwd(GU2, 2)
    z_finish(GU0)
    ag_near(AZ, za)
    ag_far(AZ, za)
    ag_fwd(AO, oa)
    z_finish(DOWN)
    ag_near(AO, oa)
    ag_far(AO, oa)

    def gated(j):
        acol = pl.ds(j * cj, cj)
        gcol = pl.ds(fs + j * uw, cj)
        ucol = pl.ds(fs + j * uw + cj, cj)

        @pl.loop(0, 4)
        def _(dd):
            gu = dot_nn(za[dd], unit_w((1 + j) * uw, uw))
            da = dot_nt(oa[dd], wd[pl.ds(j * cj, cj), :])
            g, u = gu[:, :cj], gu[:, cj:]
            sig = jax.nn.sigmoid(g)
            sw = g * sig
            big[dd, :, acol] = (sw * u).astype(BF)
            big[dd, :, gcol] = (da * u * sig * (1.0 + g * (1.0 - sig))).astype(BF)
            big[dd, :, ucol] = (da * sw).astype(BF)

    def grad_gu(j):
        @pl.loop(0, 4)
        def _(dd):
            left = za[:, :, pl.ds(pl.multiple_of(dd * ch, ch), ch)].reshape(4 * tok, ch)
            right = big[:, :, pl.ds(fs + j * uw, uw)].reshape(4 * tok, uw)
            res = dot_tn(left, right).astype(BF)
            gw[dd, :, :, :, pl.ds((1 + j) * uw, uw)] = res.reshape(nz, 2, rows, uw)

    gated(0)
    grad_gu(0)
    g_pair(GU0)
    z_fwd(GU2, 3)
    z_finish(GU1)
    gated(1)
    z_finish(GU2)
    gated(2)

    drain("rs0")

    def dz2_tile(dd):
        return dot_nt(big[dd, :, pl.ds(fs, 3 * uw)], unit_w(uw, 3 * uw))

    rs_run(1, sb_a, bufs_a, dz2_tile, "rs1")
    own[...] = dz2_tile(d)
    rs_pass(1, sb_a, bufs_a, "rs1")
    g_pair_wait(GU0)
    g_line(GU0)
    grad_gu(1)
    g_pair(GU1)

    def grad_down(j):
        left = big[:, :, pl.ds(j * cj, cj)].reshape(4 * tok, cj)
        gd[pl.ds(j * cj, cj), :] = dot_tn(left, oa[...].reshape(4 * tok, wid)).astype(BF)

    rs_wait(1, bufs_a)
    gvec[...] = jnp.zeros_like(gvec)
    zero_row = jnp.zeros((8, wid), F32)

    def fold(v):
        return v.reshape(step // 8, 8, wid).sum(axis=0)

    def back_two(i, acc):
        rr = pl.ds(pl.multiple_of(i * step, step), step)
        dz = own[rr, :] + rx_a[rr, :].astype(F32) + ry_a[rr, :].astype(F32)
        h = hid[rr, :]
        inv = norm_rows(h)
        unit = h * inv
        e = dz * gv[1:2, :]
        g = oa[d, rr, :].astype(F32) + inv * (e - unit * jnp.mean(e * unit, axis=1, keepdims=True))
        dh[rr, :] = g
        ra[d, rr, :] = g.astype(BF)
        return acc + fold(dz * unit)

    gain2 = lax.fori_loop(0, tok // step, back_two, zero_row)
    gvec[1:2, :] = jnp.sum(gain2, axis=0, keepdims=True)
    ag_start(AR, ra)
    g_pair_wait(GU1)
    g_line(GU1)
    grad_gu(2)
    g_pair(GU2)
    ag_fwd(AR, ra)
    for j in range(3):
        grad_down(j)
    g_pair(DOWN)
    g_pair_wait(GU2)
    g_line(GU2)

    def out_tile(dd):
        return dot_nn(big[dd, :, pl.ds(0, fs)], wd[...])

    ag_near(AR, ra)
    ag_far(AR, ra)

    mcol = fs

    @pl.loop(0, 4)
    def _(dd):
        dy = dot_nt(ra[dd], wo[...])
        cur, one, two, _ = past(dd)
        q = dy * mbuf[dd, :, pl.ds(ch, ch)]
        mbuf[dd, :, pl.ds(ch, ch)] = q
        big[dd, :, pl.ds(mcol + ch, ch)] = (dy * convolve(cur, one, two)).astype(BF)
        gvec[2:3, tap_cols] = gvec[2:3, tap_cols] + jnp.sum(q * cur, axis=0, keepdims=True)
        gvec[3:4, tap_cols] = gvec[3:4, tap_cols] + jnp.sum(q * one, axis=0, keepdims=True)
        gvec[4:5, tap_cols] = gvec[4:5, tap_cols] + jnp.sum(q * two, axis=0, keepdims=True)

    head = 8
    send("halo", s > 0, lambda: mbuf.at[:, pl.ds(0, head), pl.ds(ch, ch)], lambda: halo_q, lambda: hs.at[1], lambda: hr.at[1], to_prev)

    @pl.when(s == 2 * nz - 1)
    def _():
        halo_q[...] = jnp.zeros_like(halo_q)

    rs_run(2, big, bufs_b, out_tile, "rs2", 2 * fs)
    own[...] = out_tile(d)
    rs_pass(2, big, bufs_b, "rs2", 2 * fs)
    make_z1()
    go[...] = dot_tn(ybuf[...].reshape(4 * tok, ch), ra[...].reshape(4 * tok, wid)).astype(BF)
    g_pair(OUT)
    g_pair_wait(DOWN)
    g_line(DOWN)
    recv(s < 2 * nz - 1, lambda: halo_q, lambda: hr.at[1])
    @pl.loop(0, 4)
    def _(dd):
        q = mbuf[dd, :, pl.ds(ch, ch)]
        new = halo_q[dd]
        masks = ma[dd].astype(F32)
        one = jnp.where(row == tok - 1, new[0:1], pltpu.roll(q, tok - 1, 0)) * masks[:, 2:3]
        two = jnp.where(row == tok - 2, new[0:1], jnp.where(row == tok - 1, new[1:2], pltpu.roll(q, tok - 2, 0)))
        dp = gv[2:3, tap_cols] * q + gv[3:4, tap_cols] * one + gv[4:5, tap_cols] * (two * masks[:, 3:4])
        big[dd, :, pl.ds(mcol, ch)] = (dp * mbuf[dd, :, pl.ds(2 * ch, ch)]).astype(BF)
        big[dd, :, pl.ds(mcol + 2 * ch, ch)] = (dp * mbuf[dd, :, pl.ds(0, ch)]).astype(BF)

    rs_wait(2, bufs_b)

    @pl.loop(0, tok // step)
    def _(i):
        rr = pl.ds(pl.multiple_of(i * step, step), step)
        out_ref[rr, :] = (hid[rr, :] + own[rr, :] + rx_b[rr, :].astype(F32) + ry_b[rr, :].astype(F32)).astype(BF)

    drain("rs1")

    def dz1_tile(dd):
        return dot_nt(big[dd, :, pl.ds(mcol, uw)], unit_w(0, uw))

    rs_run(3, sb_a, bufs_a, dz1_tile, "rs3")
    own[...] = dz1_tile(d)

    @pl.loop(0, 4)
    def _(dd):
        left = big[:, :, pl.ds(pl.multiple_of(dd * ch, ch), ch)].reshape(4 * tok, ch)
        right = big[:, :, pl.ds(mcol, uw)].reshape(4 * tok, uw)
        gw[dd, :, :, :, pl.ds(0, uw)] = dot_tn(left, right).astype(BF).reshape(nz, 2, rows, uw)

    g_pair(IN)
    rs_pass(3, sb_a, bufs_a, "rs3")
    g_pair_wait(OUT)
    g_line(OUT)
    g_pair_wait(IN)
    g_line(IN)
    drain("halo")
    drain("stage")
    g_rows(GU0)
    g_rows(GU1)
    g_rows(GU2)
    rs_wait(3, bufs_a)

    def back_one(i, acc):
        rr = pl.ds(pl.multiple_of(i * step, step), step)
        dz = own[rr, :] + rx_a[rr, :].astype(F32) + ry_a[rr, :].astype(F32)
        xv = xa[d, rr, :].astype(F32)
        inv = norm_rows(xv)
        unit = xv * inv
        e = dz * gv[0:1, :]
        g = dh[rr, :] + inv * (e - unit * jnp.mean(e * unit, axis=1, keepdims=True))
        gtok_ref[rr, :] = g.astype(BF)
        return acc + fold(dz * unit)

    gain1 = lax.fori_loop(0, tok // step, back_one, zero_row)
    gvec[0:1, :] = jnp.sum(gain1, axis=0, keepdims=True)
    for g in range(wid // 128):
        val = gvec[:, pl.ds(g * 128, 128)].astype(BF)
        for i in range(g * per, (g + 1) * per):
            dd, q = i // (2 * nz), i % (2 * nz)
            sg[dd, q // 2, q % 2] = val
    for k, (idx, tgt) in enumerate(peers):
        send("g", True, lambda idx=idx: sg.at[idx], lambda k=k: sgx.at[k], lambda k=k: ss.at[k], lambda k=k: sr.at[k], tgt)
    g_rows(IN)
    for unit in (GU0, GU1, GU2):
        g_rows_wait(unit)
    g_last(DOWN, gdown_ref)
    g_last(OUT, gout_ref)
    for k in range(3):
        recv(True, lambda k=k: sgx.at[k], lambda k=k: sr.at[k])
    for zz in range(nz):
        for cc in range(2):
            tot = sg[d, zz, cc].astype(F32)
            for k in range(3):
                tot = tot + sgx[k, zz, cc].astype(F32)
            s2[zz, cc] = tot.astype(BF)
    g_pair(GAIN)
    g_rows_wait(IN)
    g_pair_wait(GAIN)
    g_line(GAIN)
    g_last(GAIN, gsmall_ref)
    drain()


def fast_body(n_dp, n_seq, tokens, segments, cotangent, in_weight, out_weight, gate_weight, up_weight, down_weight, norm_one, norm_two, kernel):
    tok, wid = tokens.shape[1], tokens.shape[2]
    nz = n_seq // 2
    rows = in_weight.shape[0]
    drows = down_weight.shape[0]
    ch = wid // n_dp
    fs = gate_weight.shape[1] // n_dp
    uw = 3 * ch
    cj = uw // 2
    lanes = kernel.shape[1]
    place = lax.axis_index("dp") * n_seq + lax.axis_index("seq")
    lane0 = lax.rem(place, 128 // lanes) * lanes
    gains = jnp.concatenate([norm_one[None], norm_two[None], kernel], axis=0).astype(BF)
    gain_tile = lax.dynamic_update_slice(jnp.zeros((16, 128), BF), gains, (0, lane0))
    offset = lax.axis_index("seq") * tok
    filler = jnp.full((2,), -1, jnp.int32)
    near = lax.dynamic_slice_in_dim(jnp.concatenate([filler, segments[0], filler]), offset, tok + 4)
    mid = near[2 : tok + 2]
    same = [mid == near[1 : tok + 1], mid == near[0:tok], mid == near[3 : tok + 3], mid == near[4 : tok + 4]]
    masks = jnp.pad(jnp.stack(same, axis=1).astype(BF), ((0, 0), (0, 124)))

    dims = (tok, wid, nz, rows, ch, fs, cj, uw, drows)
    top = nz - 1
    vm = pltpu.VMEM
    dma = lambda n: pltpu.SemaphoreType.DMA((n,))
    plane = lambda w, t=BF: vm((n_dp, tok, w), t)
    rs_set = [vm((tok, wid), BF)] * 2 + [vm((tok // 2, wid), BF)] * 2
    scratch = [
        vm((n_dp, rows, 4 * uw), BF),
        vm((n_dp, nz, 2, rows, 4 * uw), BF),
        vm((ch, wid), BF),
        vm((fs, wid), BF),
        vm((n_dp, nz, 2, 16, 128), BF),
        vm((16, wid), F32),
        plane(wid), plane(128), plane(wid), plane(wid), plane(wid),
        plane(3 * fs),
        plane(uw, F32), plane(ch), plane(ch),
        vm((n_dp, 16, ch), BF),
        vm((n_dp, 8, ch), F32),
        plane(wid),
        *rs_set, *rs_set,
        vm((tok, wid), F32), vm((tok, wid), F32), vm((tok, wid), F32),
        vm((n_dp, nz, 2, rows, 4 * uw), BF), vm((fs, wid), BF), vm((ch, wid), BF),
        vm((nz, n_dp, rows, 4 * uw), BF), vm((nz, drows, wid), BF), vm((nz, rows, wid), BF),
        vm((top, n_dp, rows, 4 * uw), BF), vm((top, drows, wid), BF), vm((top, rows, wid), BF),
        vm((top, n_dp, rows, 4 * uw), BF), vm((top, drows, wid), BF), vm((top, rows, wid), BF),
        vm((16, wid), F32),
        vm((n_dp, nz, 2, 16, 128), BF),
        vm((3, nz, 2, 16, 128), BF),
        vm((nz, 2, 16, 128), BF),
        vm((nz, 16, 128), BF), vm((top, 16, 128), BF), vm((top, 16, 128), BF),
        dma(7 * 13), dma(7 * 2 * nz), dma(12), dma(12), dma(3), dma(3), dma(3), dma(3), dma(2), dma(2),
        dma(24), dma(24), dma(24), dma(24), dma(7 * nz), dma(7 * nz),
        dma(7 * top * 2), dma(7 * top), dma(7 * top), dma(7 * top), dma(12), dma(12), dma(3), dma(3), dma(8 * fs // uw),
    ]
    f32 = lambda a: jax.ShapeDtypeStruct(a.shape, F32)
    vspec = pl.BlockSpec(memory_space=vm)
    res = pl.pallas_call(
        functools.partial(block_kernel, dims),
        out_shape=(
            jax.ShapeDtypeStruct((tok, wid), BF), jax.ShapeDtypeStruct((tok, wid), BF),
            jax.ShapeDtypeStruct((n_dp, rows, 4 * uw), BF), f32(out_weight), f32(down_weight),
            jax.ShapeDtypeStruct((16, 128), F32),
        ),
        in_specs=[vspec] * 6 + [pl.BlockSpec(memory_space=pl.ANY)] * 2 + [vspec],
        out_specs=(vspec,) * 6,
        scratch_shapes=scratch,
        compiler_params=pltpu.CompilerParams(collective_id=0, has_side_effects=True, vmem_limit_bytes=64 * 1024 * 1024),
    )(tokens[0], cotangent[0], masks, gain_tile, in_weight, out_weight, gate_weight, up_weight, down_weight)
    grad_tile = res[2].astype(F32)
    grad_in = grad_tile[:, :, :uw].reshape(n_dp, rows, 3, ch).transpose(1, 2, 0, 3).reshape(rows, 3 * wid)
    pairs = grad_tile[:, :, uw:].reshape(n_dp, rows, 3, 2, cj).transpose(3, 1, 0, 2, 4).reshape(2, rows, n_dp * fs)
    small = lax.dynamic_slice(res[5], (0, lane0), (16, lanes))
    return (res[0][None], res[1][None], grad_in, res[3], pairs[0], pairs[1], res[4], small[0], small[1], small[2:5])


def gather(value, axis=0):
    return lax.all_gather(value.astype(BF), ("dp", "seq"), axis=axis, tiled=True)


def norm_back(grad_unit, unit_rows, inverse):
    return inverse * (grad_unit - unit_rows * jnp.mean(grad_unit * unit_rows, axis=1, keepdims=True))


def from_behind(value, axis, steps):
    count = lax.axis_size(axis)
    leading, last = (max(0, -steps), min(count, count - steps))
    return lax.ppermute(value, axis, [(source, source + steps) for source in range(leading, last)])


def spread(value):
    n_dp, n_seq = lax.axis_size("dp"), lax.axis_size("seq")
    shaped = value.reshape((n_dp, n_seq, value.shape[0] // (n_dp * n_seq)) + value.shape[1:]).astype(BF)
    moved = lax.all_to_all(shaped, "seq", split_axis=1, concat_axis=1, tiled=True).astype(F32)
    summed = jnp.sum(moved, axis=1).astype(BF)
    owned = lax.psum_scatter(summed, "dp", scatter_dimension=0, tiled=True).astype(F32)
    return owned.reshape(owned.shape[1:])


def plain_body(tokens, segments, cotangent, in_weight, out_weight, gate_weight, up_weight, down_weight, norm_one, norm_two, kernel):
    width, count = tokens.shape[2], tokens.shape[1]
    in_mat, out_mat, gate_mat, up_mat, down_mat = map(gather, (in_weight, out_weight, gate_weight, up_weight, down_weight))
    gain_a, gain_b = gather(norm_one).astype(F32), gather(norm_two).astype(F32)
    taps = gather(kernel, 1).astype(F32)
    filler = jnp.full((2,), -1, jnp.int32)
    near = lax.dynamic_slice_in_dim(jnp.concatenate([filler, segments[0], filler]), lax.axis_index("seq") * count, count + 4)
    mid = near[2 : count + 2]
    same = lambda first: (mid == near[first : count + first]).astype(F32)[:, None]
    resident = tokens[0].astype(F32)
    inverse_a = lax.rsqrt(jnp.mean(resident * resident, axis=1, keepdims=True) + epsilon)
    unit_a = resident * inverse_a
    normed_a = (unit_a * gain_a).astype(BF)
    mixed = dot_nn(normed_a, in_mat)
    b_part, c_part, x_part = mixed[:, :width], mixed[:, width : 2 * width], mixed[:, 2 * width :]
    conv_in = (b_part * x_part).astype(BF)
    extended = jnp.concatenate([from_behind(conv_in[count - 2 :], "seq", 1), conv_in], axis=0).astype(F32)
    current, prev_one, prev_two = extended[2:], extended[1 : count + 1] * same(1), extended[0:count] * same(0)
    convolved = taps[0] * current + taps[1] * prev_one + taps[2] * prev_two
    gated = (c_part * convolved).astype(BF)
    hidden = resident + dot_nn(gated, out_mat)
    inverse_b = lax.rsqrt(jnp.mean(hidden * hidden, axis=1, keepdims=True) + epsilon)
    unit_b = hidden * inverse_b
    normed_b = (unit_b * gain_b).astype(BF)
    gate_pre, up_pre = dot_nn(normed_b, gate_mat), dot_nn(normed_b, up_mat)
    sig = jax.nn.sigmoid(gate_pre)
    swish = gate_pre * sig
    active = (swish * up_pre).astype(BF)
    output = hidden + dot_nn(active, down_mat)
    grad_low = cotangent[0]
    grad_active = dot_nt(grad_low, down_mat)
    grad_gate_pre = (grad_active * up_pre * sig * (1.0 + gate_pre * (1.0 - sig))).astype(BF)
    grad_up_pre = (grad_active * swish).astype(BF)
    grad_normed_b = dot_nt(grad_gate_pre, gate_mat) + dot_nt(grad_up_pre, up_mat)
    grad_hidden = grad_low.astype(F32) + norm_back(grad_normed_b * gain_b, unit_b, inverse_b)
    grad_branch = grad_hidden.astype(BF)
    grad_gated = dot_nt(grad_branch, out_mat)
    grad_conv = grad_gated * c_part
    ahead = jnp.concatenate([grad_conv, from_behind(grad_conv[:2], "seq", -1)], axis=0)
    grad_conv_in = taps[0] * grad_conv + taps[1] * (ahead[1 : count + 1] * same(3)) + taps[2] * (ahead[2 : count + 2] * same(4))
    grad_taps = jnp.stack([jnp.sum(grad_conv * part, axis=0) for part in (current, prev_one, prev_two)])
    grad_mixed = jnp.concatenate([grad_conv_in * x_part, grad_gated * convolved, grad_conv_in * b_part], axis=1).astype(BF)
    grad_normed_a = dot_nt(grad_mixed, in_mat)
    grad_resident = grad_hidden + norm_back(grad_normed_a * gain_a, unit_a, inverse_a)
    return (
        output.astype(BF)[None],
        grad_resident.astype(BF)[None],
        spread(dot_tn(normed_a, grad_mixed)),
        spread(dot_tn(gated, grad_branch)),
        spread(dot_tn(normed_b, grad_gate_pre)),
        spread(dot_tn(normed_b, grad_up_pre)),
        spread(dot_tn(active, grad_low)),
        spread(jnp.sum(grad_normed_a * unit_a, axis=0)),
        spread(jnp.sum(grad_normed_b * unit_b, axis=0)),
        jnp.transpose(spread(jnp.transpose(grad_taps))),
    )


def solution(mesh):
    n_dp, n_seq = mesh.shape["dp"], mesh.shape["seq"]

    def body(*args):
        tokens, in_weight, gate_weight, down_weight = args[0], args[3], args[5], args[7]
        width = tokens.shape[2]
        unit = 3 * width // max(n_dp, 1)
        fits = (
            n_dp == 4
            and n_seq % 2 == 0
            and tokens.shape[0] == 1
            and in_weight.shape[0] % 16 == 0
            and down_weight.shape[0] % 16 == 0
            and 128 % in_weight.shape[0] == 0
            and unit % 256 == 0
            and 2 * gate_weight.shape[1] == 3 * unit * n_dp
        )
        if fits:
            return fast_body(n_dp, n_seq, *args)
        return plain_body(*args)

    return jax.shard_map(
        body,
        mesh=mesh,
        in_specs=(
            P("dp", "seq", None),
            P("dp", None),
            P("dp", "seq", None),
            P(("dp", "seq"), None),
            P(("dp", "seq"), None),
            P(("dp", "seq"), None),
            P(("dp", "seq"), None),
            P(("dp", "seq"), None),
            P(("dp", "seq")),
            P(("dp", "seq")),
            P(None, ("dp", "seq")),
        ),
        out_specs=(
            P("dp", "seq", None),
            P("dp", "seq", None),
            P(("dp", "seq"), None),
            P(("dp", "seq"), None),
            P(("dp", "seq"), None),
            P(("dp", "seq"), None),
            P(("dp", "seq"), None),
            P(("dp", "seq")),
            P(("dp", "seq")),
            P(None, ("dp", "seq")),
        ),
        check_vma=False,
    )
```

```python
import functools

import jax
import jax.numpy as jnp
from jax import lax
from jax.experimental import pallas as pl
from jax.experimental.pallas import tpu as pltpu
from jax.sharding import PartitionSpec as P

epsilon = 1e-05
MESH = pl.DeviceIdType.MESH
BF = jnp.bfloat16
F32 = jnp.float32


def dot_nn(a, b):
    return jnp.dot(a, b, preferred_element_type=F32)


def dot_nt(a, b):
    return lax.dot_general(a, b, (((1,), (1,)), ((), ())), preferred_element_type=F32)


def dot_tn(a, b):
    return lax.dot_general(a, b, (((0,), (0,)), ((), ())), preferred_element_type=F32)


def when(pred, body):
    if pred is True:
        body()
    else:
        pl.when(pred)(body)


GAIN, IN, OUT, GU0, DOWN, GU1, GU2 = range(7)
SLOT = {IN: 0, GU0: 1, GU1: 2, GU2: 3}
AX, AZ, AO, AR = range(4)


def block_kernel(
    dims,
    x_ref, do_ref, mask_ref, gain_ref, win_ref, wout_ref, wg_ref, wu_ref, wdn_ref,
    out_ref, gtok_ref, gin_ref, gout_ref, ggate_ref, gup_ref, gdown_ref, gsmall_ref, gains_ref,
    stage, wall, wo, wd, gb, gv, xa, ma, za, oa, ra, big, mbuf, pbuf, ybuf, halo_p, halo_q,
    sb_a, sb_b, rx_a, ry_a, fx_a, fy_a, rx_b, ry_b, fx_b, fy_b, hid, dh,
    gw, gd, go, dd_g, dd_d, dd_o, up_g, up_d, up_o, dn_g, dn_d, dn_o,
    rbuf, gsum, s2, dd_s, up_s, dn_s,
    zs, zr, ws, wr, gs, gr, ms, mr, hs, hr, ags, agr, rss, rsr, ds_, dr_, us, ur, vs, vr, qs, qr, ins,
):
    tok, wid, nz, rows, ch, fs, cj, uw, drows = dims
    half = tok // 2
    d = lax.axis_index("dp")
    s = lax.axis_index("seq")
    x = lax.rem(d, 2)
    y = lax.div(d, 2)
    z = lax.div(s, 2)
    c = lax.rem(s, 2)
    xn = 2 * y + (1 - x)
    yn = 2 * (1 - y) + x
    dg = 2 * (1 - y) + (1 - x)
    oc = 1 - c
    top = nz - 1
    to_x, to_y, to_g = (xn, s), (yn, s), (dg, s)
    to_sib = (d, 2 * z + oc)
    to_up, to_dn = (d, s + 2), (d, s - 2)
    to_next, to_prev = (d, s + 1), (d, s - 1)
    pending = []

    def copy(src, dst, ssem, rsem, tgt):
        return pltpu.make_async_remote_copy(
            src_ref=src(), dst_ref=dst(), send_sem=ssem(), recv_sem=rsem(), device_id=tgt, device_id_type=MESH
        )

    def send(tag, pred, src, dst, ssem, rsem, tgt):
        when(pred, lambda: copy(src, dst, ssem, rsem, tgt).start())
        pending.append((tag, pred, src, dst, ssem, rsem, tgt))

    def recv(pred, dst, rsem):
        when(pred, lambda: copy(dst, dst, rsem, rsem, to_sib).wait_recv())

    def drain(tag=None):
        keep = []
        for item in pending:
            if tag is None or item[0] == tag:
                when(item[1], lambda item=item: copy(*item[2:]).wait_send())
            else:
                keep.append(item)
        pending[:] = keep

    barrier = pltpu.get_barrier_semaphore()

    def greet(tgt):
        pl.semaphore_signal(barrier, inc=1, device_id=tgt, device_id_type=MESH)

    for tgt in (to_x, to_y, to_g, to_sib):
        greet(tgt)
    has_up, has_dn = z < top, z > 0
    pl.when(has_up)(lambda: greet(to_up))
    pl.when(has_dn)(lambda: greet(to_dn))
    cross_next = jnp.logical_and(c == 1, z < top)
    cross_prev = jnp.logical_and(c == 0, z > 0)
    pl.when(cross_next)(lambda: greet(to_next))
    pl.when(cross_prev)(lambda: greet(to_prev))
    ones = [jnp.where(p, 1, 0) for p in (has_up, has_dn, cross_next, cross_prev)]
    pl.semaphore_wait(barrier, 4 + ones[0] + ones[1] + ones[2] + ones[3])

    def cols(unit):
        return pl.ds(SLOT[unit] * uw, uw)

    def w_block(unit, zz, cc):
        if unit == GAIN:
            return gb.at[d, zz, cc]
        if unit == OUT:
            return wo.at[pl.ds(pl.multiple_of((2 * zz + cc) * rows, rows), rows), :]
        if unit == DOWN:
            return wd.at[pl.ds(pl.multiple_of((2 * zz + cc) * drows, drows), drows), :]
        return wall.at[:, zz, cc, :, cols(unit)]

    def z_send(unit, pred, zz, ssem, tgt):
        blk = lambda: w_block(unit, zz, c)
        send("w", pred, blk, blk, lambda: zs.at[unit * 13 + ssem], lambda: zr.at[unit * 2 * nz + 2 * zz + c], tgt)

    def z_own(unit):
        z_send(unit, has_up, z, 0, to_up)
        z_send(unit, has_dn, z, 3, to_dn)
        z_send(unit, True, z, 6, to_sib)

    def z_fwd(unit, k):
        low, high = z - k, z + k
        has_low, has_high = z >= k, z + k <= top
        recv(has_low, lambda: w_block(unit, low, c), lambda: zr.at[unit * 2 * nz + 2 * low + c])
        if k < top:
            z_send(unit, jnp.logical_and(has_low, has_up), low, k, to_up)
        z_send(unit, has_low, low, 6 + k, to_sib)
        recv(has_high, lambda: w_block(unit, high, c), lambda: zr.at[unit * 2 * nz + 2 * high + c])
        if k < top:
            z_send(unit, jnp.logical_and(has_high, has_dn), high, 3 + k, to_dn)
        z_send(unit, has_high, high, 9 + k, to_sib)

    def z_finish(unit):
        for zz in range(nz):
            recv(True, lambda zz=zz: w_block(unit, zz, oc), lambda zz=zz: zr.at[unit * 2 * nz + 2 * zz + oc])

    peers = ((xn, to_x), (yn, to_y), (dg, to_g))

    def w_slice(unit):
        u = SLOT[unit]
        wall[d, z, c, :, cols(unit)] = stage[d, :, cols(unit)]
        for k, (idx, tgt) in enumerate(peers):
            send(
                "stage", True,
                lambda idx=idx: stage.at[idx, :, cols(unit)],
                lambda: wall.at[d, z, c, :, cols(unit)],
                lambda k=k: ws.at[u * 3 + k], lambda k=k: wr.at[u * 3 + k], tgt,
            )

    def w_slice_wait(unit):
        u = SLOT[unit]
        for k, (idx, _) in enumerate(peers):
            recv(True, lambda idx=idx: wall.at[idx, z, c, :, cols(unit)], lambda k=k: wr.at[u * 3 + k])

    lo, hi = pl.ds(0, half), pl.ds(half, half)

    def ag_send(a, buf, idx, part, k, rk, tgt):
        blk = lambda: buf.at[idx, part, :]
        send("ag", True, blk, blk, lambda: ags.at[a * 6 + k], lambda: agr.at[a * 6 + rk], tgt)

    def ag_start(a, buf):
        ag_send(a, buf, d, hi, 0, 1, to_x)
        ag_send(a, buf, d, lo, 1, 2, to_y)
        ag_send(a, buf, d, lo, 2, 0, to_x)
        ag_send(a, buf, d, hi, 3, 3, to_y)

    def ag_recv(a, buf, idx, part, rk):
        recv(True, lambda: buf.at[idx, part, :], lambda: agr.at[a * 6 + rk])

    def ag_fwd(a, buf):
        ag_recv(a, buf, yn, lo, 2)
        ag_send(a, buf, yn, lo, 4, 4, to_x)
        ag_recv(a, buf, xn, hi, 1)
        ag_send(a, buf, xn, hi, 5, 5, to_y)

    def ag_near(a, buf):
        ag_recv(a, buf, xn, lo, 0)
        ag_recv(a, buf, yn, hi, 3)

    def ag_far(a, buf):
        ag_recv(a, buf, dg, lo, 4)
        ag_recv(a, buf, dg, hi, 5)

    def rs_send(r, tag, src, dst, k, tgt):
        send(tag, True, src, dst, lambda: rss.at[r * 6 + k], lambda: rsr.at[r * 6 + k], tgt)

    def rs_run(r, sb, bufs, tile, tag, first=0):
        wide = pl.ds(first, wid)
        rx, ry, fx, fy = bufs
        sb[dg, :, wide] = tile(dg).astype(BF)
        rs_send(r, tag, lambda: sb.at[dg, lo, wide], lambda: fx, 0, to_x)
        rs_send(r, tag, lambda: sb.at[dg, hi, wide], lambda: fy, 1, to_y)
        sb[xn, :, wide] = tile(xn).astype(BF)
        rs_send(r, tag, lambda: sb.at[xn, lo, wide], lambda: rx.at[lo, :], 2, to_x)
        sb[yn, :, wide] = tile(yn).astype(BF)
        rs_send(r, tag, lambda: sb.at[yn, hi, wide], lambda: ry.at[hi, :], 3, to_y)

    def rs_pass(r, sb, bufs, tag, first=0):
        wide = pl.ds(first, wid)
        rx, ry, fx, fy = bufs
        recv(True, lambda: fx, lambda: rsr.at[r * 6 + 0])
        sb[yn, lo, wide] = (sb[yn, lo, wide].astype(F32) + fx[...].astype(F32)).astype(BF)
        rs_send(r, tag, lambda: sb.at[yn, lo, wide], lambda: ry.at[lo, :], 4, to_y)
        recv(True, lambda: fy, lambda: rsr.at[r * 6 + 1])
        sb[xn, hi, wide] = (sb[xn, hi, wide].astype(F32) + fy[...].astype(F32)).astype(BF)
        rs_send(r, tag, lambda: sb.at[xn, hi, wide], lambda: rx.at[hi, :], 5, to_x)

    def rs_wait(r, bufs):
        rx, ry, fx, fy = bufs
        recv(True, lambda: rx.at[lo, :], lambda: rsr.at[r * 6 + 2])
        recv(True, lambda: ry.at[hi, :], lambda: rsr.at[r * 6 + 3])
        recv(True, lambda: ry.at[lo, :], lambda: rsr.at[r * 6 + 4])
        recv(True, lambda: rx.at[hi, :], lambda: rsr.at[r * 6 + 5])

    bufs_a = (rx_a, ry_a, fx_a, fy_a)
    bufs_b = (rx_b, ry_b, fx_b, fy_b)

    def g_own(unit, zz, cc):
        if unit == GAIN:
            return s2.at[zz, cc]
        if unit == OUT:
            return go.at[pl.ds(pl.multiple_of((2 * zz + cc) * rows, rows), rows), :]
        if unit == DOWN:
            return gd.at[pl.ds(pl.multiple_of((2 * zz + cc) * drows, drows), drows), :]
        return gw.at[:, zz, cc, :, cols(unit)]

    def g_in(unit, trio, zz):
        buf = trio[{GAIN: 3, OUT: 2, DOWN: 1}.get(unit, 0)]
        if unit in SLOT:
            return buf.at[zz, :, :, cols(unit)]
        return buf.at[zz]

    t_dd = (dd_g, dd_d, dd_o, dd_s)
    t_up = (up_g, up_d, up_o, up_s)
    t_dn = (dn_g, dn_d, dn_o, dn_s)

    def g_pair(unit):
        for zz in range(nz):
            send(
                "g", True, lambda zz=zz: g_own(unit, zz, oc), lambda zz=zz: g_in(unit, t_dd, zz),
                lambda zz=zz: ds_.at[unit * nz + zz], lambda zz=zz: dr_.at[unit * nz + zz], to_sib,
            )

    def g_pair_wait(unit):
        for zz in range(nz):
            recv(True, lambda zz=zz: g_in(unit, t_dd, zz), lambda zz=zz: dr_.at[unit * nz + zz])

    def g_add(unit, dst, parts):
        shape = dst.shape
        if len(shape) == 3:
            for k in range(shape[0]):
                dst[k] = sum(p[k].astype(F32) for p in parts).astype(dst.dtype)
        else:
            dst[...] = sum(p[...].astype(F32) for p in parts).astype(dst.dtype)

    def g_step(unit, pred, zt, come, came, csem, ssem, rsem, there, tgt):
        mine, pair = (lambda: g_own(unit, zt, c)), (lambda: g_in(unit, t_dd, zt))
        if come:
            recv(pred, came, csem)
            pl.when(pred)(lambda: g_add(unit, mine(), (mine(), pair(), came())))
        else:
            pl.when(pred)(lambda: g_add(unit, mine(), (mine(), pair())))
        send("g", pred, mine, there, ssem, rsem, tgt)

    def g_hop(unit, h):
        for zt in range(top, h, -1):
            came = lambda zt=zt: g_in(unit, t_up, zt - 1)
            sem = lambda zt=zt: ur.at[unit * top + zt - 1]
            g_step(unit, z == h, zt, h > 0, came, sem, lambda zt=zt: us.at[unit * top + zt - 1], sem, came, to_up)
        for zt in range(top - h):
            came = lambda zt=zt: g_in(unit, t_dn, zt)
            sem = lambda zt=zt: vr.at[unit * top + zt]
            g_step(unit, z == top - h, zt, h > 0, came, sem, lambda zt=zt: vs.at[unit * top + zt], sem, came, to_dn)

    def g_last(unit, acc):
        up_ref = lambda: g_in(unit, t_up, z - 1)
        dn_ref = lambda: g_in(unit, t_dn, z)
        recv(has_dn, up_ref, lambda: ur.at[unit * top + z - 1])
        recv(has_up, dn_ref, lambda: vr.at[unit * top + z])
        g_add(unit, acc, (g_own(unit, z, c), g_in(unit, t_dd, z)))
        pl.when(has_dn)(lambda: g_add(unit, acc, (acc, up_ref())))
        pl.when(has_up)(lambda: g_add(unit, acc, (acc, dn_ref())))

    def row_send(unit, idx):
        return big.at[idx, pl.ds(SLOT[unit] * rows, rows), pl.ds(2 * fs, uw)]

    def g_rows(unit):
        facc = mbuf.at[:, pl.ds(0, rows), :]
        g_last(unit, facc)
        u = SLOT[unit]
        for k in range(4):
            big[k, pl.ds(u * rows, rows), pl.ds(2 * fs, uw)] = facc[k].astype(BF)
        rbuf[d, :, cols(unit)] = facc[d].astype(BF)
        for k, (idx, tgt) in enumerate(peers):
            send(
                "rows", True,
                lambda idx=idx: row_send(unit, idx),
                lambda: rbuf.at[d, :, cols(unit)],
                lambda k=k: qs.at[u * 3 + k], lambda k=k: qr.at[u * 3 + k], tgt,
            )

    def g_rows_wait(unit):
        u = SLOT[unit]
        for k, (idx, _) in enumerate(peers):
            recv(True, lambda idx=idx: rbuf.at[idx, :, cols(unit)], lambda k=k: qr.at[u * 3 + k])
        for k in range(4):
            if unit == IN:
                for p in range(3):
                    gin_ref[:, pl.ds(p * wid + k * ch, ch)] = rbuf[k, :, pl.ds(p * ch, ch)].astype(F32)
            else:
                j = u - 1
                ggate_ref[:, pl.ds(k * fs + j * cj, cj)] = rbuf[k, :, pl.ds(u * uw, cj)].astype(F32)
                gup_ref[:, pl.ds(k * fs + j * cj, cj)] = rbuf[k, :, pl.ds(u * uw + cj, cj)].astype(F32)

    count = 4 * fs // uw

    def wide_in(i):
        ref = wg_ref if i < count else wu_ref
        return pltpu.make_async_copy(
            ref.at[:, pl.ds((i % count) * uw, uw)], mbuf.at[i // 8, pl.ds((i % 8) * rows, rows), :], ins.at[i]
        )

    def wide_read(i, first, n):
        b = i * count + first // uw
        return mbuf[b // 8, pl.ds((b % 8) * rows, rows), pl.ds(first % uw, n)]

    x_in = pltpu.make_async_copy(x_ref.at[0], xa.at[d], ins.at[2 * count])
    do_in = pltpu.make_async_copy(do_ref.at[0], oa.at[d], ins.at[2 * count + 1])
    def down_in(i):
        n = (uw, wid - uw)[i]
        return pltpu.make_async_copy(
            wdn_ref.at[:, pl.ds(i * uw, n)], mbuf.at[2, pl.ds(i * drows, drows), pl.ds(0, n)] if i == 0
            else mbuf.at[3, pl.ds(0, drows), pl.ds(0, n)], ins.at[2 * count + 2 + i]
        )

    def first_in(i):
        return pltpu.make_async_copy(
            win_ref.at[:, pl.ds(i * uw, uw)], mbuf.at[2 + i // 2, pl.ds(tok - rows * (1 + i % 2), rows), :], ins.at[2 * count + 4 + i]
        )

    for i in range(4):
        first_in(i).start()
    x_in.start()
    for i in range(2 * count):
        wide_in(i).start()
    for i in range(2):
        down_in(i).start()
    do_in.start()
    for i in range(4):
        first_in(i).wait()
    for k in range(4):
        for p in range(3):
            b, first = divmod(p * wid + k * ch, uw)
            stage[k, :, pl.ds(p * ch, ch)] = mbuf[2 + b // 2, pl.ds(tok - rows * (1 + b % 2), rows), pl.ds(first, ch)].astype(BF)
    w_slice(IN)
    gb[d, z, c] = gain_ref[...]
    z_own(GAIN)
    x_in.wait()
    ag_start(AX, xa)
    wo[pl.ds(pl.multiple_of(s * rows, rows), rows), :] = wout_ref[...].astype(BF)
    z_own(OUT)
    ma[d] = mask_ref[...]
    for i in range(2 * count):
        wide_in(i).wait()
    for k in range(4):
        for j in range(3):
            stage[k, :, pl.ds((1 + j) * uw, cj)] = wide_read(0, k * fs + j * cj, cj).astype(BF)
            stage[k, :, pl.ds((1 + j) * uw + cj, cj)] = wide_read(1, k * fs + j * cj, cj).astype(BF)
    w_slice_wait(IN)
    z_own(IN)
    for i in range(2):
        down_in(i).wait()
    wd[pl.ds(pl.multiple_of(s * drows, drows), drows), pl.ds(0, uw)] = mbuf[2, pl.ds(0, drows), :].astype(BF)
    wd[pl.ds(pl.multiple_of(s * drows, drows), drows), pl.ds(uw, wid - uw)] = mbuf[3, pl.ds(0, drows), pl.ds(0, wid - uw)].astype(BF)
    z_fwd(GAIN, 1)
    z_fwd(OUT, 1)
    ag_fwd(AX, xa)
    for k, (idx, tgt) in enumerate(peers):
        send("ag", True, lambda: ma.at[d], lambda: ma.at[d], lambda k=k: ms.at[k], lambda k=k: mr.at[k], tgt)
    w_slice(GU0)
    z_fwd(GAIN, 2)
    z_fwd(IN, 1)
    z_fwd(OUT, 2)
    z_fwd(GAIN, 3)
    z_finish(GAIN)
    for k, (idx, tgt) in enumerate(peers):
        send("w", True, lambda: gb.at[d], lambda: gb.at[d], lambda k=k: gs.at[k], lambda k=k: gr.at[k], tgt)
    w_slice(GU1)
    w_slice(GU2)
    ag_near(AX, xa)
    z_fwd(IN, 2)
    z_fwd(OUT, 3)
    for k, (idx, _) in enumerate(peers):
        recv(True, lambda idx=idx: gb.at[idx], lambda k=k: gr.at[k])
    per = 128 // rows
    for g in range(wid // 128):
        tot = None
        for i in range(g * per, (g + 1) * per):
            dd, q = i // (2 * nz), i % (2 * nz)
            piece = gb[dd, q // 2, q % 2].astype(F32)
            tot = piece if tot is None else tot + piece
        gv[:, pl.ds(g * 128, 128)] = tot

    step = 32

    def norm_rows(xv):
        return lax.rsqrt(jnp.mean(xv * xv, axis=1, keepdims=True) + epsilon)

    zcol = pl.ds(0, wid)
    zstep = 64

    def make_z1(dd):
        @pl.loop(0, tok // zstep)
        def _(i):
            rr = pl.ds(pl.multiple_of(i * zstep, zstep), zstep)
            xv = xa[dd, rr, :].astype(F32)
            big[dd, rr, zcol] = (xv * norm_rows(xv) * gv[0:1, :]).astype(BF)

    make_z1(d)
    make_z1(xn)
    make_z1(yn)
    z_fwd(IN, 3)
    w_slice_wait(GU0)
    z_own(GU0)
    ag_far(AX, xa)
    make_z1(dg)
    z_finish(IN)
    for k, (idx, _) in enumerate(peers):
        recv(True, lambda idx=idx: ma.at[idx], lambda k=k: mr.at[k])

    def unit_w(lo_col, n):
        return wall[:, :, :, :, pl.ds(lo_col, n)].reshape(wid, n)

    @pl.loop(0, 4)
    def _(dd):
        m = dot_nn(big[dd, :, zcol], unit_w(0, uw))
        mbuf[dd] = m
        pbuf[dd] = (m[:, :ch] * m[:, 2 * ch :]).astype(BF)

    tail = 16
    send("halo", s < 2 * nz - 1, lambda: pbuf.at[:, pl.ds(tok - tail, tail), :], lambda: halo_p,
         lambda: hs.at[0], lambda: hr.at[0], to_next)

    @pl.when(s == 0)
    def _():
        halo_p[...] = jnp.zeros_like(halo_p)

    z_finish(OUT)
    z_fwd(GU0, 1)
    w_slice_wait(GU1)
    z_own(GU1)
    recv(s > 0, lambda: halo_p, lambda: hr.at[0])
    tap_cols = pl.ds(pl.multiple_of(d * ch, ch), ch)
    row = lax.broadcasted_iota(jnp.int32, (tok, ch), 0)

    def past(dd):
        cur = pbuf[dd].astype(F32)
        old = halo_p[dd].astype(F32)
        masks = ma[dd].astype(F32)
        one = jnp.where(row == 0, old[tail - 1 : tail], pltpu.roll(cur, 1, 0)) * masks[:, 0:1]
        two = jnp.where(row == 0, old[tail - 2 : tail - 1], jnp.where(row == 1, old[tail - 1 : tail], pltpu.roll(cur, 2, 0)))
        return cur, one, two * masks[:, 1:2], masks

    def convolve(cur, one, two):
        return gv[2:3, tap_cols] * cur + gv[3:4, tap_cols] * one + gv[4:5, tap_cols] * two

    def conv_rows(dd):
        cur, one, two, _ = past(dd)
        ybuf[dd] = (mbuf[dd, :, pl.ds(ch, ch)] * convolve(cur, one, two)).astype(BF)

    def h_tile(dd):
        conv_rows(dd)
        return dot_nn(ybuf[dd], wo[...])

    rs_run(0, sb_a, bufs_a, h_tile, "rs0")
    hid[...] = h_tile(d)
    z_fwd(GU0, 2)
    w_slice_wait(GU2)
    z_own(GU2)
    z_fwd(GU1, 1)
    rs_pass(0, sb_a, bufs_a, "rs0")
    z_fwd(GU0, 3)
    z_own(DOWN)
    z_fwd(GU1, 2)
    z_fwd(GU2, 1)
    rs_wait(0, bufs_a)

    @pl.loop(0, tok // step)
    def _(i):
        rr = pl.ds(pl.multiple_of(i * step, step), step)
        h = xa[d, rr, :].astype(F32) + hid[rr, :] + rx_a[rr, :].astype(F32) + ry_a[rr, :].astype(F32)
        hid[rr, :] = h
        za[d, rr, :] = (h * norm_rows(h) * gv[1:2, :]).astype(BF)

    ag_start(AZ, za)
    do_in.wait()

    def acol(j):
        return pl.ds(j * cj, cj)

    def gcol(j):
        return pl.ds(fs + j * uw, cj)

    def ucol(j):
        return pl.ds(fs + j * uw + cj, cj)

    def gate_one(j, dd):
        gu = dot_nn(za[dd], unit_w((1 + j) * uw, uw))
        g, u = gu[:, :cj], gu[:, cj:]
        sig = jax.nn.sigmoid(g)
        sw = g * sig
        big[dd, :, acol(j)] = (sw * u).astype(BF)
        big[dd, :, gcol(j)] = (u * sig * (1.0 + g * (1.0 - sig))).astype(BF)
        big[dd, :, ucol(j)] = sw.astype(BF)

    def gate_all(j):
        @pl.loop(0, 4)
        def _(dd):
            gate_one(j, dd)

    def back_all(j):
        @pl.loop(0, 4)
        def _(dd):
            da = dot_nt(oa[dd], wd[pl.ds(j * cj, cj), :])
            big[dd, :, gcol(j)] = (da * big[dd, :, gcol(j)].astype(F32)).astype(BF)
            big[dd, :, ucol(j)] = (da * big[dd, :, ucol(j)].astype(F32)).astype(BF)

    def grad_gu(j):
        @pl.loop(0, 4)
        def _(dd):
            left = za[:, :, pl.ds(pl.multiple_of(dd * ch, ch), ch)].reshape(4 * tok, ch)
            right = big[:, :, pl.ds(fs + j * uw, uw)].reshape(4 * tok, uw)
            res = dot_tn(left, right).astype(BF)
            gw[dd, :, :, :, pl.ds((1 + j) * uw, uw)] = res.reshape(nz, 2, rows, uw)

    def grad_down(j):
        left = big[:, :, pl.ds(j * cj, cj)].reshape(4 * tok, cj)
        gd[pl.ds(j * cj, cj), :] = dot_tn(left, oa[...].reshape(4 * tok, wid)).astype(BF)

    def dz2_tile(dd):
        return dot_nt(big[dd, :, pl.ds(fs, 3 * uw)], unit_w(uw, 3 * uw))

    def out_tile(dd):
        return dot_nn(big[dd, :, pl.ds(0, fs)], wd[...])

    z_finish(GU0)
    gate_one(0, d)
    z_fwd(GU1, 3)
    z_fwd(GU2, 2)
    ag_fwd(AZ, za)
    ag_start(AO, oa)
    z_finish(GU1)
    gate_one(1, d)
    z_fwd(DOWN, 1)
    ag_near(AZ, za)
    z_fwd(GU2, 3)
    z_finish(GU2)
    gate_one(2, d)
    for j in range(3):
        gate_one(j, xn)
    ag_fwd(AO, oa)
    z_fwd(DOWN, 2)
    for j in range(3):
        gate_one(j, yn)
    ag_far(AZ, za)
    for j in range(3):
        gate_one(j, dg)
    z_fwd(DOWN, 3)
    z_finish(DOWN)
    rs_run(2, sb_b, bufs_b, out_tile, "rs2")
    ag_near(AO, oa)
    ag_far(AO, oa)
    for j in range(3):
        grad_down(j)
    g_pair(DOWN)
    for j in range(3):
        back_all(j)
    g_pair_wait(DOWN)
    g_hop(DOWN, 0)

    drain("rs0")
    rs_run(1, sb_a, bufs_a, dz2_tile, "rs1")
    rs_pass(2, sb_b, bufs_b, "rs2")
    dh[...] = dz2_tile(d)
    grad_gu(0)
    g_pair(GU0)
    rs_pass(1, sb_a, bufs_a, "rs1")
    g_hop(DOWN, 1)
    g_pair_wait(GU0)
    g_hop(GU0, 0)
    grad_gu(1)
    g_pair(GU1)
    rs_wait(1, bufs_a)

    @pl.loop(0, tok // step)
    def _(i):
        rr = pl.ds(pl.multiple_of(i * step, step), step)
        dz = dh[rr, :] + rx_a[rr, :].astype(F32) + ry_a[rr, :].astype(F32)
        h = hid[rr, :]
        inv = norm_rows(h)
        unit = h * inv
        e = dz * gv[1:2, :]
        g = oa[d, rr, :].astype(F32) + inv * (e - unit * jnp.mean(e * unit, axis=1, keepdims=True))
        dh[rr, :] = g
        ra[d, rr, :] = g.astype(BF)

    ag_start(AR, ra)
    g_hop(DOWN, 2)
    g_hop(GU0, 1)
    g_pair_wait(GU1)
    g_hop(GU1, 0)
    grad_gu(2)
    g_pair(GU2)
    ag_fwd(AR, ra)
    hid[...] = hid[...] + out_tile(d)
    rs_wait(2, bufs_b)

    @pl.loop(0, tok // step)
    def _(i):
        rr = pl.ds(pl.multiple_of(i * step, step), step)
        sb_b[d, rr, :] = (hid[rr, :] + rx_b[rr, :].astype(F32) + ry_b[rr, :].astype(F32)).astype(BF)

    result = pltpu.make_async_copy(sb_b.at[d], out_ref.at[0], ins.at[2 * count])
    result.start()
    for dd in (d, xn, yn, dg):
        make_z1(dd)
    g_hop(GU0, 2)
    g_pair_wait(GU2)
    g_hop(GU2, 0)
    ag_near(AR, ra)
    ag_far(AR, ra)

    mcol = fs
    zero_tap = jnp.zeros((8, ch), F32)

    def back_conv(dd, acc):
        dy = dot_nt(ra[dd], wo[...])
        cur, one, two, _ = past(dd)
        q = dy * mbuf[dd, :, pl.ds(ch, ch)]
        mbuf[dd, :, pl.ds(ch, ch)] = q
        big[dd, :, pl.ds(mcol + ch, ch)] = (dy * convolve(cur, one, two)).astype(BF)
        return tuple(a + (q * v).reshape(tok // 8, 8, ch).sum(axis=0) for a, v in zip(acc, (cur, one, two)))

    taps = lax.fori_loop(0, 4, back_conv, (zero_tap, zero_tap, zero_tap))
    head = 8
    send("halo", s > 0, lambda: mbuf.at[:, pl.ds(0, head), pl.ds(ch, ch)], lambda: halo_q, lambda: hs.at[1], lambda: hr.at[1], to_prev)

    @pl.when(s == 2 * nz - 1)
    def _():
        halo_q[...] = jnp.zeros_like(halo_q)

    lines = lax.broadcasted_iota(jnp.int32, (16, ch), 0)
    tap_rows = jnp.zeros((16, ch), F32)
    for k in range(3):
        tap_rows = jnp.where(lines == k, jnp.sum(taps[k], axis=0, keepdims=True), tap_rows)
    for q in range(2 * nz):
        first = (q * rows) // 128 * 128
        s2[q // 2, q % 2] = tap_rows[:, first : first + 128].astype(BF)
    g_hop(GU1, 1)
    recv(s < 2 * nz - 1, lambda: halo_q, lambda: hr.at[1])

    @pl.loop(0, 4)
    def _(dd):
        q = mbuf[dd, :, pl.ds(ch, ch)]
        new = halo_q[dd]
        masks = ma[dd].astype(F32)
        one = jnp.where(row == tok - 1, new[0:1], pltpu.roll(q, tok - 1, 0)) * masks[:, 2:3]
        two = jnp.where(row == tok - 2, new[0:1], jnp.where(row == tok - 1, new[1:2], pltpu.roll(q, tok - 2, 0)))
        dp = gv[2:3, tap_cols] * q + gv[3:4, tap_cols] * one + gv[4:5, tap_cols] * (two * masks[:, 3:4])
        big[dd, :, pl.ds(mcol, ch)] = (dp * mbuf[dd, :, pl.ds(2 * ch, ch)]).astype(BF)
        big[dd, :, pl.ds(mcol + 2 * ch, ch)] = (dp * mbuf[dd, :, pl.ds(0, ch)]).astype(BF)

    drain("rs1")

    def dz1_tile(dd):
        return dot_nt(big[dd, :, pl.ds(mcol, uw)], unit_w(0, uw))

    rs_run(3, sb_a, bufs_a, dz1_tile, "rs3")

    @pl.loop(0, 4)
    def _(dd):
        left = big[:, :, pl.ds(pl.multiple_of(dd * ch, ch), ch)].reshape(4 * tok, ch)
        right = big[:, :, pl.ds(mcol, uw)].reshape(4 * tok, uw)
        gw[dd, :, :, :, pl.ds(0, uw)] = dot_tn(left, right).astype(BF).reshape(nz, 2, rows, uw)

    g_pair(IN)
    g_hop(GU2, 1)
    g_hop(GU1, 2)
    go[...] = dot_tn(ybuf[...].reshape(4 * tok, ch), ra[...].reshape(4 * tok, wid)).astype(BF)
    g_pair(OUT)
    g_pair(GAIN)
    rs_pass(3, sb_a, bufs_a, "rs3")
    g_pair_wait(IN)
    g_hop(IN, 0)
    g_pair_wait(OUT)
    g_hop(OUT, 0)
    g_pair_wait(GAIN)
    g_hop(GAIN, 0)
    hid[...] = dz1_tile(d)
    drain("halo")
    drain("rs2")
    g_hop(GU2, 2)
    g_rows(GU0)
    g_hop(IN, 1)
    g_hop(OUT, 1)
    g_hop(GAIN, 1)
    g_last(DOWN, gdown_ref)
    g_rows(GU1)
    rs_wait(3, bufs_a)
    g_hop(IN, 2)
    g_hop(OUT, 2)
    g_hop(GAIN, 2)
    g_rows(GU2)
    g_rows_wait(GU0)

    @pl.loop(0, tok // step)
    def _(i):
        rr = pl.ds(pl.multiple_of(i * step, step), step)
        dz = hid[rr, :] + rx_a[rr, :].astype(F32) + ry_a[rr, :].astype(F32)
        xv = xa[d, rr, :].astype(F32)
        inv = norm_rows(xv)
        unit = xv * inv
        e = dz * gv[0:1, :]
        g = dh[rr, :] + inv * (e - unit * jnp.mean(e * unit, axis=1, keepdims=True))
        sb_a[d, rr, :] = g.astype(BF)

    grads = pltpu.make_async_copy(sb_a.at[d], gtok_ref.at[0], ins.at[2 * count + 1])
    grads.start()

    g_rows_wait(GU1)
    g_rows(IN)
    g_last(OUT, gout_ref)
    g_last(GAIN, gsum)
    g_rows_wait(GU2)
    lane0 = lax.rem(s * rows, 128)
    gsmall_ref[...] = pltpu.roll(gsum[...], lax.rem(128 - lane0, 128), 1)
    g_rows_wait(IN)

    def gain_sum(first, n):
        acc = jnp.zeros((rows, 128), F32)
        for k in range(4):
            for q in range(n // 128):
                cc = pl.ds(first + q * 128, 128)
                acc = acc + stage[k, :, cc].astype(F32) * rbuf[k, :, cc].astype(F32)
        return acc

    gains_ref[0] = gain_sum(0, uw)
    gains_ref[1] = gain_sum(uw, 3 * uw)
    result.wait()
    grads.wait()
    drain()


def fast_body(n_dp, n_seq, tokens, segments, cotangent, in_weight, out_weight, gate_weight, up_weight, down_weight, norm_one, norm_two, kernel):
    tok, wid = tokens.shape[1], tokens.shape[2]
    nz = n_seq // 2
    rows = in_weight.shape[0]
    drows = down_weight.shape[0]
    ch = wid // n_dp
    fs = gate_weight.shape[1] // n_dp
    uw = 3 * ch
    cj = uw // 2
    lanes = kernel.shape[1]
    place = lax.axis_index("dp") * n_seq + lax.axis_index("seq")
    lane0 = lax.rem(place, 128 // lanes) * lanes
    gains = jnp.concatenate([norm_one[None], norm_two[None], kernel], axis=0).astype(BF)
    gain_tile = lax.dynamic_update_slice(jnp.zeros((16, 128), BF), gains, (0, lane0))
    offset = lax.axis_index("seq") * tok
    filler = jnp.full((2,), -1, jnp.int32)
    near = lax.dynamic_slice_in_dim(jnp.concatenate([filler, segments[0], filler]), offset, tok + 4)
    mid = near[2 : tok + 2]
    same = [mid == near[1 : tok + 1], mid == near[0:tok], mid == near[3 : tok + 3], mid == near[4 : tok + 4]]
    masks = jnp.pad(jnp.stack(same, axis=1).astype(BF), ((0, 0), (0, 124)))

    dims = (tok, wid, nz, rows, ch, fs, cj, uw, drows)
    top = nz - 1
    vm = pltpu.VMEM
    dma = lambda n: pltpu.SemaphoreType.DMA((n,))
    plane = lambda w, t=BF: vm((n_dp, tok, w), t)
    rs_set = [vm((tok, wid), BF)] * 2 + [vm((tok // 2, wid), BF)] * 2
    scratch = [
        vm((n_dp, rows, 4 * uw), BF),
        vm((n_dp, nz, 2, rows, 4 * uw), BF),
        vm((ch, wid), BF),
        vm((fs, wid), BF),
        vm((n_dp, nz, 2, 16, 128), BF),
        vm((16, wid), F32),
        plane(wid), plane(128), plane(wid), plane(wid), plane(wid),
        plane(3 * fs),
        plane(uw, F32), plane(ch), plane(ch),
        vm((n_dp, 16, ch), BF),
        vm((n_dp, 8, ch), F32),
        plane(wid), plane(wid),
        *rs_set, *rs_set,
        vm((tok, wid), F32), vm((tok, wid), F32),
        vm((n_dp, nz, 2, rows, 4 * uw), BF), vm((fs, wid), BF), vm((ch, wid), BF),
        vm((nz, n_dp, rows, 4 * uw), BF), vm((nz, drows, wid), BF), vm((nz, rows, wid), BF),
        vm((top, n_dp, rows, 4 * uw), BF), vm((top, drows, wid), BF), vm((top, rows, wid), BF),
        vm((top, n_dp, rows, 4 * uw), BF), vm((top, drows, wid), BF), vm((top, rows, wid), BF),
        vm((n_dp, rows, 4 * uw), BF), vm((16, 128), F32),
        vm((nz, 2, 16, 128), BF),
        vm((nz, 16, 128), BF), vm((top, 16, 128), BF), vm((top, 16, 128), BF),
        dma(7 * 13), dma(7 * 2 * nz), dma(12), dma(12), dma(3), dma(3), dma(3), dma(3), dma(2), dma(2),
        dma(24), dma(24), dma(24), dma(24), dma(7 * nz), dma(7 * nz),
        dma(7 * top), dma(7 * top), dma(7 * top), dma(7 * top), dma(12), dma(12), dma(8 * fs // uw + 8),
    ]
    f32 = lambda a: jax.ShapeDtypeStruct(a.shape, F32)
    vspec, anywhere = pl.BlockSpec(memory_space=vm), pl.BlockSpec(memory_space=pl.ANY)
    res = pl.pallas_call(
        functools.partial(block_kernel, dims),
        out_shape=(
            jax.ShapeDtypeStruct(tokens.shape, BF), jax.ShapeDtypeStruct(tokens.shape, BF),
            f32(in_weight), f32(out_weight), f32(gate_weight), f32(up_weight), f32(down_weight),
            jax.ShapeDtypeStruct((16, 128), F32), jax.ShapeDtypeStruct((2, rows, 128), F32),
        ),
        in_specs=[anywhere] * 2 + [vspec] * 2 + [anywhere, vspec] + [anywhere] * 3,
        out_specs=(anywhere,) * 2 + (vspec,) * 7,
        scratch_shapes=scratch,
        compiler_params=pltpu.CompilerParams(collective_id=0, has_side_effects=True, vmem_limit_bytes=64 * 1024 * 1024),
    )(tokens, cotangent, masks, gain_tile, in_weight, out_weight, gate_weight, up_weight, down_weight)
    sums = jnp.sum(res[8], axis=2)
    low = lambda g: g.astype(BF).astype(F32)
    return (*res[:7], sums[0] / low(norm_one), sums[1] / low(norm_two), res[7][:3, :lanes])


def gather(value, axis=0):
    return lax.all_gather(value.astype(BF), ("dp", "seq"), axis=axis, tiled=True)


def norm_back(grad_unit, unit_rows, inverse):
    return inverse * (grad_unit - unit_rows * jnp.mean(grad_unit * unit_rows, axis=1, keepdims=True))


def from_behind(value, axis, steps):
    count = lax.axis_size(axis)
    leading, last = (max(0, -steps), min(count, count - steps))
    return lax.ppermute(value, axis, [(source, source + steps) for source in range(leading, last)])


def spread(value):
    n_dp, n_seq = lax.axis_size("dp"), lax.axis_size("seq")
    shaped = value.reshape((n_dp, n_seq, value.shape[0] // (n_dp * n_seq)) + value.shape[1:]).astype(BF)
    moved = lax.all_to_all(shaped, "seq", split_axis=1, concat_axis=1, tiled=True).astype(F32)
    summed = jnp.sum(moved, axis=1).astype(BF)
    owned = lax.psum_scatter(summed, "dp", scatter_dimension=0, tiled=True).astype(F32)
    return owned.reshape(owned.shape[1:])


def plain_body(tokens, segments, cotangent, in_weight, out_weight, gate_weight, up_weight, down_weight, norm_one, norm_two, kernel):
    width, count = tokens.shape[2], tokens.shape[1]
    in_mat, out_mat, gate_mat, up_mat, down_mat = map(gather, (in_weight, out_weight, gate_weight, up_weight, down_weight))
    gain_a, gain_b = gather(norm_one).astype(F32), gather(norm_two).astype(F32)
    taps = gather(kernel, 1).astype(F32)
    filler = jnp.full((2,), -1, jnp.int32)
    near = lax.dynamic_slice_in_dim(jnp.concatenate([filler, segments[0], filler]), lax.axis_index("seq") * count, count + 4)
    mid = near[2 : count + 2]
    same = lambda first: (mid == near[first : count + first]).astype(F32)[:, None]
    resident = tokens[0].astype(F32)
    inverse_a = lax.rsqrt(jnp.mean(resident * resident, axis=1, keepdims=True) + epsilon)
    unit_a = resident * inverse_a
    normed_a = (unit_a * gain_a).astype(BF)
    mixed = dot_nn(normed_a, in_mat)
    b_part, c_part, x_part = mixed[:, :width], mixed[:, width : 2 * width], mixed[:, 2 * width :]
    conv_in = (b_part * x_part).astype(BF)
    extended = jnp.concatenate([from_behind(conv_in[count - 2 :], "seq", 1), conv_in], axis=0).astype(F32)
    current, prev_one, prev_two = extended[2:], extended[1 : count + 1] * same(1), extended[0:count] * same(0)
    convolved = taps[0] * current + taps[1] * prev_one + taps[2] * prev_two
    gated = (c_part * convolved).astype(BF)
    hidden = resident + dot_nn(gated, out_mat)
    inverse_b = lax.rsqrt(jnp.mean(hidden * hidden, axis=1, keepdims=True) + epsilon)
    unit_b = hidden * inverse_b
    normed_b = (unit_b * gain_b).astype(BF)
    gate_pre, up_pre = dot_nn(normed_b, gate_mat), dot_nn(normed_b, up_mat)
    sig = jax.nn.sigmoid(gate_pre)
    swish = gate_pre * sig
    active = (swish * up_pre).astype(BF)
    output = hidden + dot_nn(active, down_mat)
    grad_low = cotangent[0]
    grad_active = dot_nt(grad_low, down_mat)
    grad_gate_pre = (grad_active * up_pre * sig * (1.0 + gate_pre * (1.0 - sig))).astype(BF)
    grad_up_pre = (grad_active * swish).astype(BF)
    grad_normed_b = dot_nt(grad_gate_pre, gate_mat) + dot_nt(grad_up_pre, up_mat)
    grad_hidden = grad_low.astype(F32) + norm_back(grad_normed_b * gain_b, unit_b, inverse_b)
    grad_branch = grad_hidden.astype(BF)
    grad_gated = dot_nt(grad_branch, out_mat)
    grad_conv = grad_gated * c_part
    ahead = jnp.concatenate([grad_conv, from_behind(grad_conv[:2], "seq", -1)], axis=0)
    grad_conv_in = taps[0] * grad_conv + taps[1] * (ahead[1 : count + 1] * same(3)) + taps[2] * (ahead[2 : count + 2] * same(4))
    grad_taps = jnp.stack([jnp.sum(grad_conv * part, axis=0) for part in (current, prev_one, prev_two)])
    grad_mixed = jnp.concatenate([grad_conv_in * x_part, grad_gated * convolved, grad_conv_in * b_part], axis=1).astype(BF)
    grad_normed_a = dot_nt(grad_mixed, in_mat)
    grad_resident = grad_hidden + norm_back(grad_normed_a * gain_a, unit_a, inverse_a)
    return (
        output.astype(BF)[None],
        grad_resident.astype(BF)[None],
        spread(dot_tn(normed_a, grad_mixed)),
        spread(dot_tn(gated, grad_branch)),
        spread(dot_tn(normed_b, grad_gate_pre)),
        spread(dot_tn(normed_b, grad_up_pre)),
        spread(dot_tn(active, grad_low)),
        spread(jnp.sum(grad_normed_a * unit_a, axis=0)),
        spread(jnp.sum(grad_normed_b * unit_b, axis=0)),
        jnp.transpose(spread(jnp.transpose(grad_taps))),
    )


def solution(mesh):
    n_dp, n_seq = mesh.shape["dp"], mesh.shape["seq"]

    def body(*args):
        tokens, in_weight, gate_weight, down_weight = args[0], args[3], args[5], args[7]
        width = tokens.shape[2]
        unit = 3 * width // max(n_dp, 1)
        fits = (
            n_dp == 4
            and n_seq % 2 == 0
            and tokens.shape[0] == 1
            and in_weight.shape[0] % 16 == 0
            and down_weight.shape[0] % 16 == 0
            and 128 % in_weight.shape[0] == 0
            and unit % 256 == 0
            and 2 * gate_weight.shape[1] == 3 * unit * n_dp
        )
        if fits:
            return fast_body(n_dp, n_seq, *args)
        return plain_body(*args)

    return jax.shard_map(
        body,
        mesh=mesh,
        in_specs=(
            P("dp", "seq", None),
            P("dp", None),
            P("dp", "seq", None),
            P(("dp", "seq"), None),
            P(("dp", "seq"), None),
            P(("dp", "seq"), None),
            P(("dp", "seq"), None),
            P(("dp", "seq"), None),
            P(("dp", "seq")),
            P(("dp", "seq")),
            P(None, ("dp", "seq")),
        ),
        out_specs=(
            P("dp", "seq", None),
            P("dp", "seq", None),
            P(("dp", "seq"), None),
            P(("dp", "seq"), None),
            P(("dp", "seq"), None),
            P(("dp", "seq"), None),
            P(("dp", "seq"), None),
            P(("dp", "seq")),
            P(("dp", "seq")),
            P(None, ("dp", "seq")),
        ),
        check_vma=False,
    )
```

```python
import functools

import jax
import jax.numpy as jnp
from jax import lax
from jax.experimental import pallas as pl
from jax.experimental.pallas import tpu as pltpu
from jax.sharding import PartitionSpec as P

epsilon = 1e-05
MESH = pl.DeviceIdType.MESH
BF = jnp.bfloat16
F32 = jnp.float32


def dot_nn(a, b):
    return jnp.dot(a, b, preferred_element_type=F32)


def dot_nt(a, b):
    return lax.dot_general(a, b, (((1,), (1,)), ((), ())), preferred_element_type=F32)


def dot_tn(a, b):
    return lax.dot_general(a, b, (((0,), (0,)), ((), ())), preferred_element_type=F32)


def when(pred, body):
    if pred is True:
        body()
    else:
        pl.when(pred)(body)


GAIN, IN, OUT, GU0, DOWN, GU1, GU2, IN_A, IN_B, IN_C = range(10)
SLOT = {IN: 0, GU0: 1, GU1: 2, GU2: 3, IN_A: 4, IN_B: 5, IN_C: 6}
PIECES = (IN_A, IN_B, IN_C)
AX, AZ, AO, AR = range(4)


def block_kernel(
    dims,
    x_ref, do_ref, seg_ref, n1_ref, n2_ref, taps_ref, win_ref, wout_ref, wg_ref, wu_ref, wdn_ref,
    out_ref, gtok_ref, gin_ref, gout_ref, ggate_ref, gup_ref, gdown_ref, gsmall_ref,
    stage, wall, wo, wd, gb, gv, xa, ma, za, oa, ra, big, mbuf, pbuf, ybuf, halo_p, halo_q,
    sb_a, sb_b, rx_a, ry_a, fx_a, fy_a, rx_b, ry_b, fx_b, fy_b, hid, dh,
    gw, gd, go, dd_g, dd_d, dd_o, up_g, up_d, up_o, dn_g, dn_d, dn_o,
    rbuf, gsum, near, fm, s2, dd_s, up_s, dn_s,
    zs, zr, ws, wr, gs, gr, ms, mr, hs, hr, ags, agr, rss, rsr, ds_, dr_, us, ur, vs, vr, qs, qr, ins,
):
    tok, wid, nz, rows, ch, fs, cj, uw, drows = dims
    half = tok // 2
    d = lax.axis_index("dp")
    s = lax.axis_index("seq")
    x = lax.rem(d, 2)
    y = lax.div(d, 2)
    z = lax.div(s, 2)
    c = lax.rem(s, 2)
    xn = 2 * y + (1 - x)
    yn = 2 * (1 - y) + x
    dg = 2 * (1 - y) + (1 - x)
    oc = 1 - c
    top = nz - 1
    to_x, to_y, to_g = (xn, s), (yn, s), (dg, s)
    to_sib = (d, 2 * z + oc)
    to_up, to_dn = (d, s + 2), (d, s - 2)
    to_next, to_prev = (d, s + 1), (d, s - 1)
    pending = []

    def copy(src, dst, ssem, rsem, tgt):
        return pltpu.make_async_remote_copy(
            src_ref=src(), dst_ref=dst(), send_sem=ssem(), recv_sem=rsem(), device_id=tgt, device_id_type=MESH
        )

    def send(tag, pred, src, dst, ssem, rsem, tgt):
        when(pred, lambda: copy(src, dst, ssem, rsem, tgt).start())
        pending.append((tag, pred, src, dst, ssem, rsem, tgt))

    def recv(pred, dst, rsem):
        when(pred, lambda: copy(dst, dst, rsem, rsem, to_sib).wait_recv())

    def drain(tag=None):
        keep = []
        for item in pending:
            if tag is None or item[0] == tag:
                when(item[1], lambda item=item: copy(*item[2:]).wait_send())
            else:
                keep.append(item)
        pending[:] = keep

    barrier = pltpu.get_barrier_semaphore()

    def greet(tgt):
        pl.semaphore_signal(barrier, inc=1, device_id=tgt, device_id_type=MESH)

    for tgt in (to_x, to_y, to_g, to_sib):
        greet(tgt)
    has_up, has_dn = z < top, z > 0
    pl.when(has_up)(lambda: greet(to_up))
    pl.when(has_dn)(lambda: greet(to_dn))
    cross_next = jnp.logical_and(c == 1, z < top)
    cross_prev = jnp.logical_and(c == 0, z > 0)
    pl.when(cross_next)(lambda: greet(to_next))
    pl.when(cross_prev)(lambda: greet(to_prev))
    ones = [jnp.where(p, 1, 0) for p in (has_up, has_dn, cross_next, cross_prev)]
    pl.semaphore_wait(barrier, 4 + ones[0] + ones[1] + ones[2] + ones[3])

    def span(unit):
        if unit in PIECES:
            return (SLOT[unit] - SLOT[IN_A]) * ch, ch
        return SLOT[unit] * uw, uw

    def cols(unit):
        return pl.ds(*span(unit))

    def w_block(unit, zz, cc):
        if unit == GAIN:
            return gb.at[:, zz, cc]
        if unit == OUT:
            return wo.at[pl.ds(pl.multiple_of((2 * zz + cc) * rows, rows), rows), :]
        if unit == DOWN:
            return wd.at[pl.ds(pl.multiple_of((2 * zz + cc) * drows, drows), drows), :]
        return wall.at[:, zz, cc, :, cols(unit)]

    def z_send(unit, pred, zz, ssem, tgt):
        blk = lambda: w_block(unit, zz, c)
        send("w", pred, blk, blk, lambda: zs.at[unit * 13 + ssem], lambda: zr.at[unit * 2 * nz + 2 * zz + c], tgt)

    def z_own(unit):
        z_send(unit, has_up, z, 0, to_up)
        z_send(unit, has_dn, z, 3, to_dn)
        z_send(unit, True, z, 6, to_sib)

    def z_fwd(unit, k):
        low, high = z - k, z + k
        has_low, has_high = z >= k, z + k <= top
        recv(has_low, lambda: w_block(unit, low, c), lambda: zr.at[unit * 2 * nz + 2 * low + c])
        if k < top:
            z_send(unit, jnp.logical_and(has_low, has_up), low, k, to_up)
        z_send(unit, has_low, low, 6 + k, to_sib)
        recv(has_high, lambda: w_block(unit, high, c), lambda: zr.at[unit * 2 * nz + 2 * high + c])
        if k < top:
            z_send(unit, jnp.logical_and(has_high, has_dn), high, 3 + k, to_dn)
        z_send(unit, has_high, high, 9 + k, to_sib)

    def z_finish(unit):
        for zz in range(nz):
            recv(True, lambda zz=zz: w_block(unit, zz, oc), lambda zz=zz: zr.at[unit * 2 * nz + 2 * zz + oc])

    peers = ((xn, to_x), (yn, to_y), (dg, to_g))

    def w_slice(unit):
        u = SLOT[unit]
        wall[d, z, c, :, cols(unit)] = stage[d, :, cols(unit)]
        for k, (idx, tgt) in enumerate(peers):
            send(
                "stage", True,
                lambda idx=idx: stage.at[idx, :, cols(unit)],
                lambda: wall.at[d, z, c, :, cols(unit)],
                lambda k=k: ws.at[u * 3 + k], lambda k=k: wr.at[u * 3 + k], tgt,
            )

    def w_slice_wait(unit):
        u = SLOT[unit]
        for k, (idx, _) in enumerate(peers):
            recv(True, lambda idx=idx: wall.at[idx, z, c, :, cols(unit)], lambda k=k: wr.at[u * 3 + k])

    lo, hi = pl.ds(0, half), pl.ds(half, half)

    def ag_send(a, buf, idx, part, k, rk, tgt):
        blk = lambda: buf.at[idx, part, :]
        send("ag", True, blk, blk, lambda: ags.at[a * 6 + k], lambda: agr.at[a * 6 + rk], tgt)

    def ag_first(a, buf):
        ag_send(a, buf, d, hi, 0, 1, to_x)
        ag_send(a, buf, d, lo, 1, 2, to_y)

    def ag_second(a, buf):
        ag_send(a, buf, d, lo, 2, 0, to_x)
        ag_send(a, buf, d, hi, 3, 3, to_y)

    def ag_start(a, buf):
        ag_first(a, buf)
        ag_second(a, buf)

    def ag_recv(a, buf, idx, part, rk):
        recv(True, lambda: buf.at[idx, part, :], lambda: agr.at[a * 6 + rk])

    def ag_fwd(a, buf):
        ag_recv(a, buf, yn, lo, 2)
        ag_send(a, buf, yn, lo, 4, 4, to_x)
        ag_recv(a, buf, xn, hi, 1)
        ag_send(a, buf, xn, hi, 5, 5, to_y)

    def ag_near(a, buf):
        ag_recv(a, buf, xn, lo, 0)
        ag_recv(a, buf, yn, hi, 3)

    def ag_far(a, buf):
        ag_recv(a, buf, dg, lo, 4)
        ag_recv(a, buf, dg, hi, 5)

    def rs_send(r, tag, src, dst, k, tgt):
        send(tag, True, src, dst, lambda: rss.at[r * 6 + k], lambda: rsr.at[r * 6 + k], tgt)

    def rs_run(r, sb, bufs, tile, tag, first=0, between=None):
        wide = pl.ds(first, wid)
        rx, ry, fx, fy = bufs
        sb[dg, :, wide] = tile(dg).astype(BF)
        rs_send(r, tag, lambda: sb.at[dg, lo, wide], lambda: fx, 0, to_x)
        rs_send(r, tag, lambda: sb.at[dg, hi, wide], lambda: fy, 1, to_y)
        if between is not None:
            between()
        sb[xn, :, wide] = tile(xn).astype(BF)
        rs_send(r, tag, lambda: sb.at[xn, lo, wide], lambda: rx.at[lo, :], 2, to_x)
        sb[yn, :, wide] = tile(yn).astype(BF)
        rs_send(r, tag, lambda: sb.at[yn, hi, wide], lambda: ry.at[hi, :], 3, to_y)

    def rs_pass(r, sb, bufs, tag, first=0):
        wide = pl.ds(first, wid)
        rx, ry, fx, fy = bufs
        recv(True, lambda: fx, lambda: rsr.at[r * 6 + 0])
        sb[yn, lo, wide] = (sb[yn, lo, wide].astype(F32) + fx[...].astype(F32)).astype(BF)
        rs_send(r, tag, lambda: sb.at[yn, lo, wide], lambda: ry.at[lo, :], 4, to_y)
        recv(True, lambda: fy, lambda: rsr.at[r * 6 + 1])
        sb[xn, hi, wide] = (sb[xn, hi, wide].astype(F32) + fy[...].astype(F32)).astype(BF)
        rs_send(r, tag, lambda: sb.at[xn, hi, wide], lambda: rx.at[hi, :], 5, to_x)

    def rs_wait(r, bufs):
        rx, ry, fx, fy = bufs
        recv(True, lambda: rx.at[lo, :], lambda: rsr.at[r * 6 + 2])
        recv(True, lambda: ry.at[hi, :], lambda: rsr.at[r * 6 + 3])
        recv(True, lambda: ry.at[lo, :], lambda: rsr.at[r * 6 + 4])
        recv(True, lambda: rx.at[hi, :], lambda: rsr.at[r * 6 + 5])

    bufs_a = (rx_a, ry_a, fx_a, fy_a)
    bufs_b = (rx_b, ry_b, fx_b, fy_b)

    def g_own(unit, zz, cc):
        if unit == GAIN:
            return s2.at[zz, cc]
        if unit == OUT:
            return go.at[pl.ds(pl.multiple_of((2 * zz + cc) * rows, rows), rows), :]
        if unit == DOWN:
            return gd.at[pl.ds(pl.multiple_of((2 * zz + cc) * drows, drows), drows), :]
        return gw.at[:, zz, cc, :, cols(unit)]

    def g_in(unit, trio, zz):
        buf = trio[{GAIN: 3, OUT: 2, DOWN: 1}.get(unit, 0)]
        if unit in SLOT:
            return buf.at[zz, :, :, cols(unit)]
        return buf.at[zz]

    t_dd = (dd_g, dd_d, dd_o, dd_s)
    t_up = (up_g, up_d, up_o, up_s)
    t_dn = (dn_g, dn_d, dn_o, dn_s)

    def g_pair(unit):
        for zz in range(nz):
            send(
                "g", True, lambda zz=zz: g_own(unit, zz, oc), lambda zz=zz: g_in(unit, t_dd, zz),
                lambda zz=zz: ds_.at[unit * nz + zz], lambda zz=zz: dr_.at[unit * nz + zz], to_sib,
            )

    def g_pair_wait(unit):
        for zz in range(nz):
            recv(True, lambda zz=zz: g_in(unit, t_dd, zz), lambda zz=zz: dr_.at[unit * nz + zz])

    def g_add(unit, dst, parts):
        shape = dst.shape
        if len(shape) == 3:
            for k in range(shape[0]):
                dst[k] = sum(p[k].astype(F32) for p in parts).astype(dst.dtype)
        else:
            dst[...] = sum(p[...].astype(F32) for p in parts).astype(dst.dtype)

    def g_step(unit, pred, zt, come, came, csem, ssem, rsem, there, tgt):
        mine, pair = (lambda: g_own(unit, zt, c)), (lambda: g_in(unit, t_dd, zt))
        if come:
            recv(pred, came, csem)
            pl.when(pred)(lambda: g_add(unit, mine(), (mine(), pair(), came())))
        else:
            pl.when(pred)(lambda: g_add(unit, mine(), (mine(), pair())))
        send("g", pred, mine, there, ssem, rsem, tgt)

    def g_hop(unit, h):
        for zt in range(top, h, -1):
            came = lambda zt=zt: g_in(unit, t_up, zt - 1)
            sem = lambda zt=zt: ur.at[unit * top + zt - 1]
            g_step(unit, z == h, zt, h > 0, came, sem, lambda zt=zt: us.at[unit * top + zt - 1], sem, came, to_up)
        for zt in range(top - h):
            came = lambda zt=zt: g_in(unit, t_dn, zt)
            sem = lambda zt=zt: vr.at[unit * top + zt]
            g_step(unit, z == top - h, zt, h > 0, came, sem, lambda zt=zt: vs.at[unit * top + zt], sem, came, to_dn)

    def g_last(unit, acc):
        up_ref = lambda: g_in(unit, t_up, z - 1)
        dn_ref = lambda: g_in(unit, t_dn, z)
        recv(has_dn, up_ref, lambda: ur.at[unit * top + z - 1])
        recv(has_up, dn_ref, lambda: vr.at[unit * top + z])
        g_add(unit, acc, (g_own(unit, z, c), g_in(unit, t_dd, z)))
        pl.when(has_dn)(lambda: g_add(unit, acc, (acc, up_ref())))
        pl.when(has_up)(lambda: g_add(unit, acc, (acc, dn_ref())))

    def row_send(unit, idx):
        first, n = span(unit)
        row = 0 if unit in PIECES else SLOT[unit]
        return big.at[idx, pl.ds(row * rows, rows), pl.ds(2 * fs + (first if unit in PIECES else 0), n)]

    def g_rows(unit):
        first, n = span(unit)
        facc = mbuf.at[:, pl.ds(0, rows), pl.ds(0, n)]
        g_last(unit, facc)
        u = SLOT[unit]
        for k in range(4):
            row_send(unit, k)[...] = facc[k].astype(BF)
        rbuf[d, :, cols(unit)] = facc[d].astype(BF)
        for k, (idx, tgt) in enumerate(peers):
            send(
                "rows", True,
                lambda idx=idx: row_send(unit, idx),
                lambda: rbuf.at[d, :, cols(unit)],
                lambda k=k: qs.at[u * 3 + k], lambda k=k: qr.at[u * 3 + k], tgt,
            )

    def g_rows_wait(unit):
        u = SLOT[unit]
        first, n = span(unit)
        for k, (idx, _) in enumerate(peers):
            recv(True, lambda idx=idx: rbuf.at[idx, :, cols(unit)], lambda k=k: qr.at[u * 3 + k])
        for k in range(4):
            if unit in PIECES:
                gin_ref[:, pl.ds(first // ch * wid + k * ch, ch)] = rbuf[k, :, cols(unit)].astype(F32)
            else:
                j = u - 1
                ggate_ref[:, pl.ds(k * fs + j * cj, cj)] = rbuf[k, :, pl.ds(first, cj)].astype(F32)
                gup_ref[:, pl.ds(k * fs + j * cj, cj)] = rbuf[k, :, pl.ds(first + cj, cj)].astype(F32)

    count = 4 * fs // uw

    def wide_in(i):
        ref = wg_ref if i < count else wu_ref
        return pltpu.make_async_copy(
            ref.at[:, pl.ds((i % count) * uw, uw)], mbuf.at[i // 8, pl.ds((i % 8) * rows, rows), :], ins.at[i]
        )

    def wide_read(i, first, n):
        b = i * count + first // uw
        return mbuf[b // 8, pl.ds((b % 8) * rows, rows), pl.ds(first % uw, n)]

    x_in = pltpu.make_async_copy(x_ref.at[0], xa.at[d], ins.at[2 * count])
    do_in = pltpu.make_async_copy(do_ref.at[0], oa.at[d], ins.at[2 * count + 1])
    def down_in(i):
        n = (uw, wid - uw)[i]
        return pltpu.make_async_copy(
            wdn_ref.at[:, pl.ds(i * uw, n)], mbuf.at[2, pl.ds(i * drows, drows), pl.ds(0, n)] if i == 0
            else mbuf.at[3, pl.ds(0, drows), pl.ds(0, n)], ins.at[2 * count + 2 + i]
        )

    def first_in(i):
        return pltpu.make_async_copy(
            win_ref.at[:, pl.ds(i * uw, uw)], mbuf.at[2 + i // 2, pl.ds(tok - rows * (1 + i % 2), rows), :], ins.at[2 * count + 4 + i]
        )

    for i in range(4):
        first_in(i).start()
    x_in.start()
    for i in range(2 * count):
        wide_in(i).start()
    for i in range(2):
        down_in(i).start()
    do_in.start()
    for i in range(4):
        first_in(i).wait()
    for k in range(4):
        for p in range(3):
            b, first = divmod(p * wid + k * ch, uw)
            stage[k, :, pl.ds(p * ch, ch)] = mbuf[2 + b // 2, pl.ds(tok - rows * (1 + b % 2), rows), pl.ds(first, ch)].astype(BF)
    lanes = taps_ref.shape[1]
    lane0 = lax.rem(s * rows, 128)
    gsum[...] = jnp.zeros_like(gsum)
    gsum[0:1, 0:lanes] = n1_ref[...]
    gsum[1:2, 0:lanes] = n2_ref[...]
    gsum[2:5, 0:lanes] = taps_ref[...]
    gb[d, z, c] = pltpu.roll(gsum[...], lane0, 1).astype(BF)
    for k, (idx, tgt) in enumerate(peers):
        send("w", True, lambda: gb.at[d, z, c], lambda: gb.at[d, z, c], lambda k=k: gs.at[k], lambda k=k: gr.at[k], tgt)
    w_slice(IN)
    x_in.wait()
    ag_start(AX, xa)
    wo[pl.ds(pl.multiple_of(s * rows, rows), rows), :] = wout_ref[...].astype(BF)
    z_own(OUT)
    mid = seg_ref[:, pl.ds(pl.multiple_of(s * tok, tok), tok)]
    near[:, pl.ds(128, tok)] = mid
    near[:, pl.ds(0, 128)] = jnp.full((1, 128), -1, jnp.int32)
    near[:, pl.ds(128 + tok, 128)] = jnp.full((1, 128), -1, jnp.int32)

    @pl.when(s > 0)
    def _():
        near[:, pl.ds(0, 128)] = seg_ref[:, pl.ds(pl.multiple_of(s * tok - 128, 128), 128)]

    @pl.when(s < 2 * nz - 1)
    def _():
        near[:, pl.ds(128 + tok, 128)] = seg_ref[:, pl.ds(pl.multiple_of(s * tok + tok, 128), 128)]

    around = near[...]
    lane = lax.broadcasted_iota(jnp.int32, (128, tok), 0)
    flags = jnp.zeros((128, tok), F32)
    for k, move in enumerate((1, 2, tok + 255, tok + 254)):
        moved = pltpu.roll(around, move, 1)[:, 128 : 128 + tok]
        flags = jnp.where(lane == k, jnp.where(moved == mid, 1.0, 0.0), flags)
    fm[d] = flags[:16].astype(BF)
    for k, (idx, _) in enumerate(peers):
        recv(True, lambda idx=idx: gb.at[idx, z, c], lambda k=k: gr.at[k])
    z_own(GAIN)
    w_slice_wait(IN)
    z_own(IN)
    for i in range(2 * count):
        wide_in(i).wait()
    for k in range(4):
        for j in range(3):
            stage[k, :, pl.ds((1 + j) * uw, cj)] = wide_read(0, k * fs + j * cj, cj).astype(BF)
            stage[k, :, pl.ds((1 + j) * uw + cj, cj)] = wide_read(1, k * fs + j * cj, cj).astype(BF)
    for i in range(2):
        down_in(i).wait()
    wd[pl.ds(pl.multiple_of(s * drows, drows), drows), pl.ds(0, uw)] = mbuf[2, pl.ds(0, drows), :].astype(BF)
    wd[pl.ds(pl.multiple_of(s * drows, drows), drows), pl.ds(uw, wid - uw)] = mbuf[3, pl.ds(0, drows), pl.ds(0, wid - uw)].astype(BF)
    z_fwd(OUT, 1)
    z_fwd(GAIN, 1)
    ag_fwd(AX, xa)
    for k, (idx, tgt) in enumerate(peers):
        send("ag", True, lambda: fm.at[d], lambda: fm.at[d], lambda k=k: ms.at[k], lambda k=k: mr.at[k], tgt)
    w_slice(GU0)
    z_fwd(IN, 1)
    z_fwd(GAIN, 2)
    z_fwd(OUT, 2)
    w_slice(GU1)
    w_slice(GU2)
    do_in.wait()
    ag_first(AO, oa)
    z_fwd(GAIN, 3)
    z_finish(GAIN)
    per = 128 // rows
    for g in range(wid // 128):
        tot = None
        for i in range(g * per, (g + 1) * per):
            dd, q = i // (2 * nz), i % (2 * nz)
            piece = gb[dd, q // 2, q % 2].astype(F32)
            tot = piece if tot is None else tot + piece
        gv[:, pl.ds(g * 128, 128)] = tot

    step = 32

    def norm_rows(xv):
        return lax.rsqrt(jnp.mean(xv * xv, axis=1, keepdims=True) + epsilon)

    zcol = pl.ds(0, wid)
    zstep = 64

    def make_z1(dd):
        @pl.loop(0, tok // zstep)
        def _(i):
            rr = pl.ds(pl.multiple_of(i * zstep, zstep), zstep)
            xv = xa[dd, rr, :].astype(F32)
            big[dd, rr, zcol] = (xv * norm_rows(xv) * gv[0:1, :]).astype(BF)

    make_z1(d)
    ag_near(AX, xa)
    make_z1(xn)
    make_z1(yn)
    z_fwd(IN, 2)
    z_fwd(OUT, 3)
    z_own(DOWN)
    ag_far(AX, xa)
    make_z1(dg)
    w_slice_wait(GU0)
    z_own(GU0)
    z_fwd(IN, 3)
    z_finish(IN)
    for k, (idx, _) in enumerate(peers):
        recv(True, lambda idx=idx: fm.at[idx], lambda k=k: mr.at[k])
    for dd in range(4):
        ma[dd] = jnp.concatenate([fm[dd].astype(F32), jnp.zeros((112, tok), F32)], axis=0).T.astype(BF)

    def unit_w(lo_col, n):
        return wall[:, :, :, :, pl.ds(lo_col, n)].reshape(wid, n)

    @pl.loop(0, 4)
    def _(dd):
        m = dot_nn(big[dd, :, zcol], unit_w(0, uw))
        mbuf[dd] = m
        pbuf[dd] = (m[:, :ch] * m[:, 2 * ch :]).astype(BF)

    tail = 16
    send("halo", s < 2 * nz - 1, lambda: pbuf.at[:, pl.ds(tok - tail, tail), :], lambda: halo_p,
         lambda: hs.at[0], lambda: hr.at[0], to_next)

    @pl.when(s == 0)
    def _():
        halo_p[...] = jnp.zeros_like(halo_p)

    z_finish(OUT)
    w_slice_wait(GU1)
    z_own(GU1)
    recv(s > 0, lambda: halo_p, lambda: hr.at[0])
    tap_cols = pl.ds(pl.multiple_of(d * ch, ch), ch)
    row = lax.broadcasted_iota(jnp.int32, (tok, ch), 0)

    def past(dd):
        cur = pbuf[dd].astype(F32)
        old = halo_p[dd].astype(F32)
        masks = ma[dd].astype(F32)
        one = jnp.where(row == 0, old[tail - 1 : tail], pltpu.roll(cur, 1, 0)) * masks[:, 0:1]
        two = jnp.where(row == 0, old[tail - 2 : tail - 1], jnp.where(row == 1, old[tail - 1 : tail], pltpu.roll(cur, 2, 0)))
        return cur, one, two * masks[:, 1:2], masks

    def convolve(cur, one, two):
        return gv[2:3, tap_cols] * cur + gv[3:4, tap_cols] * one + gv[4:5, tap_cols] * two

    def conv_rows(dd):
        cur, one, two, _ = past(dd)
        ybuf[dd] = (mbuf[dd, :, pl.ds(ch, ch)] * convolve(cur, one, two)).astype(BF)

    def h_tile(dd):
        conv_rows(dd)
        return dot_nn(ybuf[dd], wo[...])

    rs_run(0, sb_a, bufs_a, h_tile, "rs0")
    hid[...] = h_tile(d)
    z_fwd(DOWN, 1)
    w_slice_wait(GU2)
    z_own(GU2)
    z_fwd(GU0, 1)
    rs_pass(0, sb_a, bufs_a, "rs0")
    z_fwd(GU1, 1)
    z_fwd(GU2, 1)
    z_fwd(DOWN, 2)
    rs_wait(0, bufs_a)

    @pl.loop(0, tok // step)
    def _(i):
        rr = pl.ds(pl.multiple_of(i * step, step), step)
        h = xa[d, rr, :].astype(F32) + hid[rr, :] + rx_a[rr, :].astype(F32) + ry_a[rr, :].astype(F32)
        hid[rr, :] = h
        za[d, rr, :] = (h * norm_rows(h) * gv[1:2, :]).astype(BF)

    ag_start(AZ, za)

    def acol(j):
        return pl.ds(j * cj, cj)

    def gcol(j):
        return pl.ds(fs + j * uw, cj)

    def ucol(j):
        return pl.ds(fs + j * uw + cj, cj)

    def gate_one(j, dd):
        gu = dot_nn(za[dd], unit_w((1 + j) * uw, uw))
        g, u = gu[:, :cj], gu[:, cj:]
        sig = jax.nn.sigmoid(g)
        sw = g * sig
        big[dd, :, acol(j)] = (sw * u).astype(BF)
        big[dd, :, gcol(j)] = (u * sig * (1.0 + g * (1.0 - sig))).astype(BF)
        big[dd, :, ucol(j)] = sw.astype(BF)

    def gate_all(j):
        @pl.loop(0, 4)
        def _(dd):
            gate_one(j, dd)

    def back_all(j):
        @pl.loop(0, 4)
        def _(dd):
            da = dot_nt(oa[dd], wd[pl.ds(j * cj, cj), :])
            big[dd, :, gcol(j)] = (da * big[dd, :, gcol(j)].astype(F32)).astype(BF)
            big[dd, :, ucol(j)] = (da * big[dd, :, ucol(j)].astype(F32)).astype(BF)

    def grad_gu(j):
        @pl.loop(0, 4)
        def _(dd):
            left = za[:, :, pl.ds(pl.multiple_of(dd * ch, ch), ch)].reshape(4 * tok, ch)
            right = big[:, :, pl.ds(fs + j * uw, uw)].reshape(4 * tok, uw)
            res = dot_tn(left, right).astype(BF)
            gw[dd, :, :, :, pl.ds((1 + j) * uw, uw)] = res.reshape(nz, 2, rows, uw)

    def grad_down(j):
        left = big[:, :, pl.ds(j * cj, cj)].reshape(4 * tok, cj)
        gd[pl.ds(j * cj, cj), :] = dot_tn(left, oa[...].reshape(4 * tok, wid)).astype(BF)

    def dz2_tile(dd):
        return dot_nt(big[dd, :, pl.ds(fs, 3 * uw)], unit_w(uw, 3 * uw))

    def out_tile(dd):
        return dot_nn(big[dd, :, pl.ds(0, fs)], wd[...])

    z_fwd(GU0, 2)
    z_fwd(GU1, 2)
    ag_fwd(AZ, za)
    ag_fwd(AO, oa)
    ag_second(AO, oa)
    z_fwd(GU2, 2)
    z_fwd(DOWN, 3)
    z_finish(DOWN)
    ag_near(AZ, za)
    z_fwd(GU0, 3)
    z_finish(GU0)
    ag_far(AZ, za)
    gate_all(0)
    z_fwd(GU1, 3)
    z_finish(GU1)
    gate_all(1)
    z_fwd(GU2, 3)
    z_finish(GU2)
    gate_all(2)
    ag_near(AO, oa)
    ag_far(AO, oa)
    for j in range(3):
        grad_down(j)
    g_pair(DOWN)

    def down_off():
        g_pair_wait(DOWN)
        g_hop(DOWN, 0)

    rs_run(2, sb_b, bufs_b, out_tile, "rs2", between=down_off)
    for j in range(3):
        back_all(j)

    drain("rs0")
    rs_run(1, sb_a, bufs_a, dz2_tile, "rs1")
    grad_gu(0)
    g_pair(GU0)
    g_hop(DOWN, 1)
    dh[...] = dz2_tile(d)
    g_pair_wait(GU0)
    g_hop(GU0, 0)
    rs_pass(1, sb_a, bufs_a, "rs1")
    grad_gu(1)
    g_pair(GU1)
    g_hop(DOWN, 2)
    g_pair_wait(GU1)
    g_hop(GU1, 0)
    grad_gu(2)
    g_pair(GU2)
    g_hop(GU0, 1)
    rs_wait(1, bufs_a)

    @pl.loop(0, tok // step)
    def _(i):
        rr = pl.ds(pl.multiple_of(i * step, step), step)
        dz = dh[rr, :] + rx_a[rr, :].astype(F32) + ry_a[rr, :].astype(F32)
        h = hid[rr, :]
        inv = norm_rows(h)
        unit = h * inv
        e = dz * gv[1:2, :]
        g = oa[d, rr, :].astype(F32) + inv * (e - unit * jnp.mean(e * unit, axis=1, keepdims=True))
        dh[rr, :] = g
        ra[d, rr, :] = g.astype(BF)

    ag_start(AR, ra)
    g_pair_wait(GU2)
    g_hop(GU2, 0)
    hid[...] = hid[...] + out_tile(d)
    for dd in (d, xn, yn, dg):
        make_z1(dd)
    g_hop(GU0, 2)
    ag_fwd(AR, ra)
    g_hop(GU1, 1)
    rs_pass(2, sb_b, bufs_b, "rs2")
    ag_near(AR, ra)
    g_hop(GU1, 2)
    ag_far(AR, ra)

    mcol = fs
    zero_tap = jnp.zeros((8, ch), F32)

    def back_conv(dd, acc):
        dy = dot_nt(ra[dd], wo[...])
        cur, one, two, _ = past(dd)
        q = dy * mbuf[dd, :, pl.ds(ch, ch)]
        mbuf[dd, :, pl.ds(ch, ch)] = q
        big[dd, :, pl.ds(mcol + ch, ch)] = (dy * convolve(cur, one, two)).astype(BF)
        return tuple(a + (q * v).reshape(tok // 8, 8, ch).sum(axis=0) for a, v in zip(acc, (cur, one, two)))

    taps = lax.fori_loop(0, 4, back_conv, (zero_tap, zero_tap, zero_tap))
    head = 8
    send("halo", s > 0, lambda: mbuf.at[:, pl.ds(0, head), pl.ds(ch, ch)], lambda: halo_q, lambda: hs.at[1], lambda: hr.at[1], to_prev)

    @pl.when(s == 2 * nz - 1)
    def _():
        halo_q[...] = jnp.zeros_like(halo_q)

    lines = lax.broadcasted_iota(jnp.int32, (16, ch), 0)
    tap_rows = jnp.zeros((16, ch), F32)
    for k in range(3):
        tap_rows = jnp.where(lines == k, jnp.sum(taps[k], axis=0, keepdims=True), tap_rows)
    for q in range(2 * nz):
        first = (q * rows) // 128 * 128
        s2[q // 2, q % 2] = tap_rows[:, first : first + 128].astype(BF)
    go[...] = dot_tn(ybuf[...].reshape(4 * tok, ch), ra[...].reshape(4 * tok, wid)).astype(BF)
    g_pair(OUT)
    g_pair(GAIN)
    g_hop(GU2, 1)
    recv(s < 2 * nz - 1, lambda: halo_q, lambda: hr.at[1])

    @pl.loop(0, 4)
    def _(dd):
        q = mbuf[dd, :, pl.ds(ch, ch)]
        new = halo_q[dd]
        masks = ma[dd].astype(F32)
        one = jnp.where(row == tok - 1, new[0:1], pltpu.roll(q, tok - 1, 0)) * masks[:, 2:3]
        two = jnp.where(row == tok - 2, new[0:1], jnp.where(row == tok - 1, new[1:2], pltpu.roll(q, tok - 2, 0)))
        dp = gv[2:3, tap_cols] * q + gv[3:4, tap_cols] * one + gv[4:5, tap_cols] * (two * masks[:, 3:4])
        big[dd, :, pl.ds(mcol, ch)] = (dp * mbuf[dd, :, pl.ds(2 * ch, ch)]).astype(BF)
        big[dd, :, pl.ds(mcol + 2 * ch, ch)] = (dp * mbuf[dd, :, pl.ds(0, ch)]).astype(BF)

    drain("rs1")

    def dz1_tile(dd):
        return dot_nt(big[dd, :, pl.ds(mcol, uw)], unit_w(0, uw))

    rs_run(3, sb_a, bufs_a, dz1_tile, "rs3")

    def grad_in(p):
        left = big[:, :, zcol].reshape(4 * tok, wid)
        right = big[:, :, pl.ds(mcol + p * ch, ch)].reshape(4 * tok, ch)
        gw[:, :, :, :, pl.ds(p * ch, ch)] = dot_tn(left, right).astype(BF).reshape(4, nz, 2, rows, ch)

    g_pair_wait(OUT)
    g_hop(OUT, 0)
    g_pair_wait(GAIN)
    g_hop(GAIN, 0)
    grad_in(0)
    g_pair(IN_A)
    grad_in(1)
    g_pair(IN_B)
    g_pair_wait(IN_A)
    g_hop(IN_A, 0)
    grad_in(2)
    g_pair(IN_C)
    g_pair_wait(IN_B)
    g_hop(IN_B, 0)
    g_hop(GU2, 2)
    g_pair_wait(IN_C)
    g_hop(IN_C, 0)
    rs_pass(3, sb_a, bufs_a, "rs3")
    g_hop(OUT, 1)
    g_hop(GAIN, 1)
    rs_wait(2, bufs_b)

    @pl.loop(0, tok // step)
    def _(i):
        rr = pl.ds(pl.multiple_of(i * step, step), step)
        sb_b[d, rr, :] = (hid[rr, :] + rx_b[rr, :].astype(F32) + ry_b[rr, :].astype(F32)).astype(BF)

    result = pltpu.make_async_copy(sb_b.at[d], out_ref.at[0], ins.at[2 * count])
    result.start()
    hid[...] = dz1_tile(d)
    drain("halo")
    g_hop(IN_A, 1)
    g_hop(OUT, 2)
    g_hop(GAIN, 2)
    g_rows(GU0)
    g_hop(IN_B, 1)
    g_hop(IN_A, 2)
    g_rows(GU1)
    g_hop(IN_C, 1)
    g_hop(IN_B, 2)
    g_last(DOWN, gdown_ref)
    g_hop(IN_C, 2)
    g_rows(GU2)
    g_rows_wait(GU0)
    g_rows_wait(GU1)
    rs_wait(3, bufs_a)

    @pl.loop(0, tok // step)
    def _(i):
        rr = pl.ds(pl.multiple_of(i * step, step), step)
        dz = hid[rr, :] + rx_a[rr, :].astype(F32) + ry_a[rr, :].astype(F32)
        xv = xa[d, rr, :].astype(F32)
        inv = norm_rows(xv)
        unit = xv * inv
        e = dz * gv[0:1, :]
        g = dh[rr, :] + inv * (e - unit * jnp.mean(e * unit, axis=1, keepdims=True))
        sb_a[d, rr, :] = g.astype(BF)

    grads = pltpu.make_async_copy(sb_a.at[d], gtok_ref.at[0], ins.at[2 * count + 1])
    grads.start()

    g_rows(IN_A)
    g_last(OUT, gout_ref)
    g_last(GAIN, gsum)
    gsmall_ref[pl.ds(8, 8), :] = pltpu.roll(gsum[...], lax.rem(128 - lane0, 128), 1)[:8]
    g_rows_wait(GU2)
    g_rows(IN_B)

    def gain_sum(first, n):
        acc = jnp.zeros((rows, 128), F32)
        for k in range(4):
            for q in range(n // 128):
                cc = pl.ds(first + q * 128, 128)
                acc = acc + stage[k, :, cc].astype(F32) * rbuf[k, :, cc].astype(F32)
        return acc

    def gain_out(k, first, n, gain):
        total = lax.dot_general(
            jnp.ones((8, 128), F32), gain_sum(first, n), (((1,), (1,)), ((), ())),
            precision=lax.Precision.HIGHEST, preferred_element_type=F32,
        )
        gsmall_ref[k : k + 1, 0:lanes] = total[0:1] / gain[...].astype(BF).astype(F32)

    gain_out(1, uw, 3 * uw, n2_ref)
    g_rows(IN_C)
    for unit in PIECES:
        g_rows_wait(unit)
    gain_out(0, 0, uw, n1_ref)
    result.wait()
    grads.wait()
    drain()


def move_out(lanes, *refs):
    n = (len(refs) - 6) // 3
    small_ref, one_ref, two_ref, taps_ref = refs[n], *refs[2 * n + 1 : 2 * n + 4]
    outs, held, sems, done = refs[n + 1 : 2 * n + 1], refs[2 * n + 4 : 3 * n + 4], refs[-2], refs[-1]
    loads = [pltpu.make_async_copy(refs[k], held[k], sems.at[k]) for k in range(n)]
    stores = [pltpu.make_async_copy(held[k], outs[k], done.at[k]) for k in range(n)]
    for load in loads:
        load.start()
    one_ref[...] = small_ref[0:1, 0:lanes]
    two_ref[...] = small_ref[1:2, 0:lanes]
    taps_ref[...] = small_ref[8:11, 0:lanes]
    for load, store in zip(loads, stores):
        load.wait()
        store.start()
    for store in stores:
        store.wait()


def fast_body(n_dp, n_seq, tokens, segments, cotangent, in_weight, out_weight, gate_weight, up_weight, down_weight, norm_one, norm_two, kernel):
    tok, wid = tokens.shape[1], tokens.shape[2]
    nz = n_seq // 2
    rows = in_weight.shape[0]
    drows = down_weight.shape[0]
    ch = wid // n_dp
    fs = gate_weight.shape[1] // n_dp
    uw = 3 * ch
    cj = uw // 2
    lanes = kernel.shape[1]

    dims = (tok, wid, nz, rows, ch, fs, cj, uw, drows)
    top = nz - 1
    vm = pltpu.VMEM
    dma = lambda n: pltpu.SemaphoreType.DMA((n,))
    plane = lambda w, t=BF: vm((n_dp, tok, w), t)
    rs_set = [vm((tok, wid), BF)] * 2 + [vm((tok // 2, wid), BF)] * 2
    scratch = [
        vm((n_dp, rows, 4 * uw), BF),
        vm((n_dp, nz, 2, rows, 4 * uw), BF),
        vm((ch, wid), BF),
        vm((fs, wid), BF),
        vm((n_dp, nz, 2, 16, 128), BF),
        vm((16, wid), F32),
        plane(wid), plane(128), plane(wid), plane(wid), plane(wid),
        plane(3 * fs),
        plane(uw, F32), plane(ch), plane(ch),
        vm((n_dp, 16, ch), BF),
        vm((n_dp, 8, ch), F32),
        plane(wid), plane(wid),
        *rs_set, *rs_set,
        vm((tok, wid), F32), vm((tok, wid), F32),
        vm((n_dp, nz, 2, rows, 4 * uw), BF), vm((fs, wid), BF), vm((ch, wid), BF),
        vm((nz, n_dp, rows, 4 * uw), BF), vm((nz, drows, wid), BF), vm((nz, rows, wid), BF),
        vm((top, n_dp, rows, 4 * uw), BF), vm((top, drows, wid), BF), vm((top, rows, wid), BF),
        vm((top, n_dp, rows, 4 * uw), BF), vm((top, drows, wid), BF), vm((top, rows, wid), BF),
        vm((n_dp, rows, 4 * uw), BF), vm((16, 128), F32), vm((1, tok + 256), jnp.int32), vm((n_dp, 16, tok), BF),
        vm((nz, 2, 16, 128), BF),
        vm((nz, 16, 128), BF), vm((top, 16, 128), BF), vm((top, 16, 128), BF),
        dma(7 * 13), dma(7 * 2 * nz), dma(12), dma(12), dma(3), dma(3), dma(3), dma(3), dma(2), dma(2),
        dma(24), dma(24), dma(24), dma(24), dma(10 * nz), dma(10 * nz),
        dma(10 * top), dma(10 * top), dma(10 * top), dma(10 * top), dma(21), dma(21), dma(8 * fs // uw + 8),
    ]
    f32 = lambda a: jax.ShapeDtypeStruct(a.shape, F32)
    vspec, anywhere = pl.BlockSpec(memory_space=vm), pl.BlockSpec(memory_space=pl.ANY)
    res = pl.pallas_call(
        functools.partial(block_kernel, dims),
        out_shape=(
            jax.ShapeDtypeStruct(tokens.shape, BF), jax.ShapeDtypeStruct(tokens.shape, BF),
            f32(in_weight), f32(out_weight), f32(gate_weight), f32(up_weight), f32(down_weight),
            jax.ShapeDtypeStruct((16, 128), F32),
        ),
        in_specs=[anywhere] * 2 + [vspec] * 4 + [anywhere, vspec] + [anywhere] * 3,
        out_specs=(anywhere,) * 2 + (vspec,) * 6,
        scratch_shapes=scratch,
        compiler_params=pltpu.CompilerParams(collective_id=0, has_side_effects=True, vmem_limit_bytes=64 * 1024 * 1024),
    )(tokens, cotangent, segments, norm_one[None], norm_two[None], kernel, in_weight, out_weight, gate_weight, up_weight, down_weight)
    final = [jax.ShapeDtypeStruct(v.shape, v.dtype) for v in res[:7]]
    final += [jax.ShapeDtypeStruct((k, lanes), F32) for k in (1, 1, 3)]
    moved = pl.pallas_call(
        functools.partial(move_out, lanes),
        out_shape=tuple(final),
        in_specs=[anywhere] * 7 + [vspec],
        out_specs=(anywhere,) * 7 + (vspec,) * 3,
        scratch_shapes=[vm(v.shape, v.dtype) for v in res[:7]] + [dma(7), dma(7)],
    )(*res)
    return (*moved[:7], moved[7][0], moved[8][0], moved[9])


def gather(value, axis=0):
    return lax.all_gather(value.astype(BF), ("dp", "seq"), axis=axis, tiled=True)


def norm_back(grad_unit, unit_rows, inverse):
    return inverse * (grad_unit - unit_rows * jnp.mean(grad_unit * unit_rows, axis=1, keepdims=True))


def from_behind(value, axis, steps):
    count = lax.axis_size(axis)
    leading, last = (max(0, -steps), min(count, count - steps))
    return lax.ppermute(value, axis, [(source, source + steps) for source in range(leading, last)])


def spread(value):
    n_dp, n_seq = lax.axis_size("dp"), lax.axis_size("seq")
    shaped = value.reshape((n_dp, n_seq, value.shape[0] // (n_dp * n_seq)) + value.shape[1:]).astype(BF)
    moved = lax.all_to_all(shaped, "seq", split_axis=1, concat_axis=1, tiled=True).astype(F32)
    summed = jnp.sum(moved, axis=1).astype(BF)
    owned = lax.psum_scatter(summed, "dp", scatter_dimension=0, tiled=True).astype(F32)
    return owned.reshape(owned.shape[1:])


def plain_body(tokens, segments, cotangent, in_weight, out_weight, gate_weight, up_weight, down_weight, norm_one, norm_two, kernel):
    width, count = tokens.shape[2], tokens.shape[1]
    in_mat, out_mat, gate_mat, up_mat, down_mat = map(gather, (in_weight, out_weight, gate_weight, up_weight, down_weight))
    gain_a, gain_b = gather(norm_one).astype(F32), gather(norm_two).astype(F32)
    taps = gather(kernel, 1).astype(F32)
    filler = jnp.full((2,), -1, jnp.int32)
    near = lax.dynamic_slice_in_dim(jnp.concatenate([filler, segments[0], filler]), lax.axis_index("seq") * count, count + 4)
    mid = near[2 : count + 2]
    same = lambda first: (mid == near[first : count + first]).astype(F32)[:, None]
    resident = tokens[0].astype(F32)
    inverse_a = lax.rsqrt(jnp.mean(resident * resident, axis=1, keepdims=True) + epsilon)
    unit_a = resident * inverse_a
    normed_a = (unit_a * gain_a).astype(BF)
    mixed = dot_nn(normed_a, in_mat)
    b_part, c_part, x_part = mixed[:, :width], mixed[:, width : 2 * width], mixed[:, 2 * width :]
    conv_in = (b_part * x_part).astype(BF)
    extended = jnp.concatenate([from_behind(conv_in[count - 2 :], "seq", 1), conv_in], axis=0).astype(F32)
    current, prev_one, prev_two = extended[2:], extended[1 : count + 1] * same(1), extended[0:count] * same(0)
    convolved = taps[0] * current + taps[1] * prev_one + taps[2] * prev_two
    gated = (c_part * convolved).astype(BF)
    hidden = resident + dot_nn(gated, out_mat)
    inverse_b = lax.rsqrt(jnp.mean(hidden * hidden, axis=1, keepdims=True) + epsilon)
    unit_b = hidden * inverse_b
    normed_b = (unit_b * gain_b).astype(BF)
    gate_pre, up_pre = dot_nn(normed_b, gate_mat), dot_nn(normed_b, up_mat)
    sig = jax.nn.sigmoid(gate_pre)
    swish = gate_pre * sig
    active = (swish * up_pre).astype(BF)
    output = hidden + dot_nn(active, down_mat)
    grad_low = cotangent[0]
    grad_active = dot_nt(grad_low, down_mat)
    grad_gate_pre = (grad_active * up_pre * sig * (1.0 + gate_pre * (1.0 - sig))).astype(BF)
    grad_up_pre = (grad_active * swish).astype(BF)
    grad_normed_b = dot_nt(grad_gate_pre, gate_mat) + dot_nt(grad_up_pre, up_mat)
    grad_hidden = grad_low.astype(F32) + norm_back(grad_normed_b * gain_b, unit_b, inverse_b)
    grad_branch = grad_hidden.astype(BF)
    grad_gated = dot_nt(grad_branch, out_mat)
    grad_conv = grad_gated * c_part
    ahead = jnp.concatenate([grad_conv, from_behind(grad_conv[:2], "seq", -1)], axis=0)
    grad_conv_in = taps[0] * grad_conv + taps[1] * (ahead[1 : count + 1] * same(3)) + taps[2] * (ahead[2 : count + 2] * same(4))
    grad_taps = jnp.stack([jnp.sum(grad_conv * part, axis=0) for part in (current, prev_one, prev_two)])
    grad_mixed = jnp.concatenate([grad_conv_in * x_part, grad_gated * convolved, grad_conv_in * b_part], axis=1).astype(BF)
    grad_normed_a = dot_nt(grad_mixed, in_mat)
    grad_resident = grad_hidden + norm_back(grad_normed_a * gain_a, unit_a, inverse_a)
    return (
        output.astype(BF)[None],
        grad_resident.astype(BF)[None],
        spread(dot_tn(normed_a, grad_mixed)),
        spread(dot_tn(gated, grad_branch)),
        spread(dot_tn(normed_b, grad_gate_pre)),
        spread(dot_tn(normed_b, grad_up_pre)),
        spread(dot_tn(active, grad_low)),
        spread(jnp.sum(grad_normed_a * unit_a, axis=0)),
        spread(jnp.sum(grad_normed_b * unit_b, axis=0)),
        jnp.transpose(spread(jnp.transpose(grad_taps))),
    )


def solution(mesh):
    n_dp, n_seq = mesh.shape["dp"], mesh.shape["seq"]

    def body(*args):
        tokens, in_weight, gate_weight, down_weight = args[0], args[3], args[5], args[7]
        width = tokens.shape[2]
        unit = 3 * width // max(n_dp, 1)
        fits = (
            n_dp == 4
            and n_seq % 2 == 0
            and tokens.shape[0] == 1
            and in_weight.shape[0] % 16 == 0
            and down_weight.shape[0] % 16 == 0
            and 128 % in_weight.shape[0] == 0
            and unit % 256 == 0
            and 2 * gate_weight.shape[1] == 3 * unit * n_dp
        )
        if fits:
            return fast_body(n_dp, n_seq, *args)
        return plain_body(*args)

    return jax.shard_map(
        body,
        mesh=mesh,
        in_specs=(
            P("dp", "seq", None),
            P("dp", None),
            P("dp", "seq", None),
            P(("dp", "seq"), None),
            P(("dp", "seq"), None),
            P(("dp", "seq"), None),
            P(("dp", "seq"), None),
            P(("dp", "seq"), None),
            P(("dp", "seq")),
            P(("dp", "seq")),
            P(None, ("dp", "seq")),
        ),
        out_specs=(
            P("dp", "seq", None),
            P("dp", "seq", None),
            P(("dp", "seq"), None),
            P(("dp", "seq"), None),
            P(("dp", "seq"), None),
            P(("dp", "seq"), None),
            P(("dp", "seq"), None),
            P(("dp", "seq")),
            P(("dp", "seq")),
            P(None, ("dp", "seq")),
        ),
        check_vma=False,
    )
```

```python
import functools

import jax
import jax.numpy as jnp
from jax import lax
from jax.experimental import pallas as pl
from jax.experimental.pallas import tpu as pltpu
from jax.sharding import PartitionSpec as P

epsilon = 1e-05
MESH = pl.DeviceIdType.MESH
BF = jnp.bfloat16
F32 = jnp.float32


def dot_nn(a, b):
    return jnp.dot(a, b, preferred_element_type=F32)


def dot_nt(a, b):
    return lax.dot_general(a, b, (((1,), (1,)), ((), ())), preferred_element_type=F32)


def dot_tn(a, b):
    return lax.dot_general(a, b, (((0,), (0,)), ((), ())), preferred_element_type=F32)


def when(pred, body):
    if pred is True:
        body()
    else:
        pl.when(pred)(body)


GAIN, IN, OUT, GU0, DOWN, GU1, GU2, IN_A, IN_B, IN_C = range(10)
SLOT = {IN: 0, GU0: 1, GU1: 2, GU2: 3, IN_A: 4, IN_B: 5, IN_C: 6}
PIECES = (IN_A, IN_B, IN_C)
AX, AZ, AO, AR = range(4)


def block_kernel(
    dims,
    x_ref, do_ref, seg_ref, n1_ref, n2_ref, taps_ref, win_ref, wout_ref, wg_ref, wu_ref, wdn_ref,
    out_ref, gtok_ref, rbuf, gout_ref, gdown_ref, gsmall_ref,
    stage, wall, wo, wd, gb, gv, xa, ma, za, oa, ra, big, mbuf, pbuf, ybuf, halo_p, halo_q,
    sb_a, sb_b, rx_a, ry_a, fx_a, fy_a, rx_b, ry_b, fx_b, fy_b, hid, dh,
    gw, gd, go, dd_g, dd_d, dd_o, up_g, up_d, up_o, dn_g, dn_d, dn_o,
    gsum, near, fm, oacc,
    zs, zr, ws, wr, gs, gr, ms, mr, hs, hr, ags, agr, rss, rsr, ds_, dr_, us, ur, vs, vr, qs, qr, ins,
):
    tok, wid, nz, rows, ch, fs, cj, uw, drows = dims
    half = tok // 2
    d = lax.axis_index("dp")
    s = lax.axis_index("seq")
    x = lax.rem(d, 2)
    y = lax.div(d, 2)
    z = lax.div(s, 2)
    c = lax.rem(s, 2)
    xn = 2 * y + (1 - x)
    yn = 2 * (1 - y) + x
    dg = 2 * (1 - y) + (1 - x)
    oc = 1 - c
    top = nz - 1
    to_x, to_y, to_g = (xn, s), (yn, s), (dg, s)
    to_sib = (d, 2 * z + oc)
    to_up, to_dn = (d, s + 2), (d, s - 2)
    to_next, to_prev = (d, s + 1), (d, s - 1)
    pending = []

    def copy(src, dst, ssem, rsem, tgt):
        return pltpu.make_async_remote_copy(
            src_ref=src(), dst_ref=dst(), send_sem=ssem(), recv_sem=rsem(), device_id=tgt, device_id_type=MESH
        )

    def send(tag, pred, src, dst, ssem, rsem, tgt):
        when(pred, lambda: copy(src, dst, ssem, rsem, tgt).start())
        pending.append((tag, pred, src, dst, ssem, rsem, tgt))

    def recv(pred, dst, rsem):
        when(pred, lambda: copy(dst, dst, rsem, rsem, to_sib).wait_recv())

    def drain(tag=None):
        keep = []
        for item in pending:
            if tag is None or item[0] == tag:
                when(item[1], lambda item=item: copy(*item[2:]).wait_send())
            else:
                keep.append(item)
        pending[:] = keep

    barrier = pltpu.get_barrier_semaphore()

    def greet(tgt):
        pl.semaphore_signal(barrier, inc=1, device_id=tgt, device_id_type=MESH)

    for tgt in (to_x, to_y, to_g, to_sib):
        greet(tgt)
    has_up, has_dn = z < top, z > 0
    pl.when(has_up)(lambda: greet(to_up))
    pl.when(has_dn)(lambda: greet(to_dn))
    cross_next = jnp.logical_and(c == 1, z < top)
    cross_prev = jnp.logical_and(c == 0, z > 0)
    pl.when(cross_next)(lambda: greet(to_next))
    pl.when(cross_prev)(lambda: greet(to_prev))
    def enter():
        ones = [jnp.where(p, 1, 0) for p in (has_up, has_dn, cross_next, cross_prev)]
        pl.semaphore_wait(barrier, 4 + ones[0] + ones[1] + ones[2] + ones[3])

    def span(unit):
        if unit in PIECES:
            return (SLOT[unit] - SLOT[IN_A]) * ch, ch
        return SLOT[unit] * uw, uw

    def cols(unit):
        return pl.ds(*span(unit))

    def w_block(unit, zz, cc):
        if unit == GAIN:
            return gb.at[:, zz, cc]
        if unit == OUT:
            return wo.at[pl.ds(pl.multiple_of((2 * zz + cc) * rows, rows), rows), :]
        if unit == DOWN:
            return wd.at[pl.ds(pl.multiple_of((2 * zz + cc) * drows, drows), drows), :]
        return wall.at[:, zz, cc, :, cols(unit)]

    def z_send(unit, pred, zz, ssem, tgt):
        blk = lambda: w_block(unit, zz, c)
        send("w", pred, blk, blk, lambda: zs.at[unit * 13 + ssem], lambda: zr.at[unit * 2 * nz + 2 * zz + c], tgt)

    def z_own(unit):
        z_send(unit, has_up, z, 0, to_up)
        z_send(unit, has_dn, z, 3, to_dn)
        z_send(unit, True, z, 6, to_sib)

    def z_fwd(unit, k):
        low, high = z - k, z + k
        has_low, has_high = z >= k, z + k <= top
        recv(has_low, lambda: w_block(unit, low, c), lambda: zr.at[unit * 2 * nz + 2 * low + c])
        if k < top:
            z_send(unit, jnp.logical_and(has_low, has_up), low, k, to_up)
        z_send(unit, has_low, low, 6 + k, to_sib)
        recv(has_high, lambda: w_block(unit, high, c), lambda: zr.at[unit * 2 * nz + 2 * high + c])
        if k < top:
            z_send(unit, jnp.logical_and(has_high, has_dn), high, 3 + k, to_dn)
        z_send(unit, has_high, high, 9 + k, to_sib)

    def z_finish(unit):
        for zz in range(nz):
            recv(True, lambda zz=zz: w_block(unit, zz, oc), lambda zz=zz: zr.at[unit * 2 * nz + 2 * zz + oc])

    peers = ((xn, to_x), (yn, to_y), (dg, to_g))

    def w_slice(unit):
        u = SLOT[unit]
        wall[d, z, c, :, cols(unit)] = stage[d, :, cols(unit)]
        for k, (idx, tgt) in enumerate(peers):
            send(
                "stage", True,
                lambda idx=idx: stage.at[idx, :, cols(unit)],
                lambda: wall.at[d, z, c, :, cols(unit)],
                lambda k=k: ws.at[u * 3 + k], lambda k=k: wr.at[u * 3 + k], tgt,
            )

    def w_slice_wait(unit):
        u = SLOT[unit]
        for k, (idx, _) in enumerate(peers):
            recv(True, lambda idx=idx: wall.at[idx, z, c, :, cols(unit)], lambda k=k: wr.at[u * 3 + k])

    lo, hi = pl.ds(0, half), pl.ds(half, half)

    def ag_send(a, buf, idx, part, k, rk, tgt):
        blk = lambda: buf.at[idx, part, :]
        send("ag", True, blk, blk, lambda: ags.at[a * 6 + k], lambda: agr.at[a * 6 + rk], tgt)

    def ag_first(a, buf):
        ag_send(a, buf, d, hi, 0, 1, to_x)
        ag_send(a, buf, d, lo, 1, 2, to_y)

    def ag_second(a, buf):
        ag_send(a, buf, d, lo, 2, 0, to_x)
        ag_send(a, buf, d, hi, 3, 3, to_y)

    def ag_start(a, buf):
        ag_first(a, buf)
        ag_second(a, buf)

    def ag_recv(a, buf, idx, part, rk):
        recv(True, lambda: buf.at[idx, part, :], lambda: agr.at[a * 6 + rk])

    def ag_fwd(a, buf):
        ag_recv(a, buf, yn, lo, 2)
        ag_send(a, buf, yn, lo, 4, 4, to_x)
        ag_recv(a, buf, xn, hi, 1)
        ag_send(a, buf, xn, hi, 5, 5, to_y)

    def ag_near(a, buf):
        ag_recv(a, buf, xn, lo, 0)
        ag_recv(a, buf, yn, hi, 3)

    def ag_far(a, buf):
        ag_recv(a, buf, dg, lo, 4)
        ag_recv(a, buf, dg, hi, 5)

    def rs_send(r, tag, src, dst, k, tgt):
        send(tag, True, src, dst, lambda: rss.at[r * 6 + k], lambda: rsr.at[r * 6 + k], tgt)

    def rs_run(r, sb, bufs, tile, tag, first=0, between=None):
        wide = pl.ds(first, wid)
        rx, ry, fx, fy = bufs
        sb[dg, :, wide] = tile(dg).astype(BF)
        rs_send(r, tag, lambda: sb.at[dg, lo, wide], lambda: fx, 0, to_x)
        rs_send(r, tag, lambda: sb.at[dg, hi, wide], lambda: fy, 1, to_y)
        if between is not None:
            between()
        sb[xn, :, wide] = tile(xn).astype(BF)
        rs_send(r, tag, lambda: sb.at[xn, lo, wide], lambda: rx.at[lo, :], 2, to_x)
        sb[yn, :, wide] = tile(yn).astype(BF)
        rs_send(r, tag, lambda: sb.at[yn, hi, wide], lambda: ry.at[hi, :], 3, to_y)

    def rs_pass(r, sb, bufs, tag, first=0):
        wide = pl.ds(first, wid)
        rx, ry, fx, fy = bufs
        recv(True, lambda: fx, lambda: rsr.at[r * 6 + 0])
        sb[yn, lo, wide] = (sb[yn, lo, wide].astype(F32) + fx[...].astype(F32)).astype(BF)
        rs_send(r, tag, lambda: sb.at[yn, lo, wide], lambda: ry.at[lo, :], 4, to_y)
        recv(True, lambda: fy, lambda: rsr.at[r * 6 + 1])
        sb[xn, hi, wide] = (sb[xn, hi, wide].astype(F32) + fy[...].astype(F32)).astype(BF)
        rs_send(r, tag, lambda: sb.at[xn, hi, wide], lambda: rx.at[hi, :], 5, to_x)

    def rs_wait(r, bufs):
        rx, ry, fx, fy = bufs
        recv(True, lambda: rx.at[lo, :], lambda: rsr.at[r * 6 + 2])
        recv(True, lambda: ry.at[hi, :], lambda: rsr.at[r * 6 + 3])
        recv(True, lambda: ry.at[lo, :], lambda: rsr.at[r * 6 + 4])
        recv(True, lambda: rx.at[hi, :], lambda: rsr.at[r * 6 + 5])

    bufs_a = (rx_a, ry_a, fx_a, fy_a)
    bufs_b = (rx_b, ry_b, fx_b, fy_b)

    def g_own(unit, zz, cc):
        if unit == OUT:
            return go.at[pl.ds(pl.multiple_of((2 * zz + cc) * rows, rows), rows), :]
        if unit == DOWN:
            return gd.at[pl.ds(pl.multiple_of((2 * zz + cc) * drows, drows), drows), :]
        return gw.at[:, zz, cc, :, cols(unit)]

    def g_in(unit, trio, zz):
        buf = trio[{OUT: 2, DOWN: 1}.get(unit, 0)]
        if unit in SLOT:
            return buf.at[zz, :, :, cols(unit)]
        return buf.at[zz]

    t_dd = (dd_g, dd_d, dd_o)
    t_up = (up_g, up_d, up_o)
    t_dn = (dn_g, dn_d, dn_o)

    def g_pair(unit, which=range(nz)):
        for zz in which:
            send(
                "g", True, lambda zz=zz: g_own(unit, zz, oc), lambda zz=zz: g_in(unit, t_dd, zz),
                lambda zz=zz: ds_.at[unit * nz + zz], lambda zz=zz: dr_.at[unit * nz + zz], to_sib,
            )

    def g_add(dst, parts):
        if len(dst.shape) == 3:
            for k in range(dst.shape[0]):
                dst[k] = sum(p[k].astype(F32) for p in parts).astype(dst.dtype)
        else:
            dst[...] = sum(p[...].astype(F32) for p in parts).astype(dst.dtype)

    def g_step(unit, pred, zt, come, came, csem, ssem, rsem, there, tgt):
        mine, pair = (lambda: g_own(unit, zt, c)), (lambda: g_in(unit, t_dd, zt))
        recv(pred, pair, lambda: dr_.at[unit * nz + zt])
        if come:
            recv(pred, came, csem)
            pl.when(pred)(lambda: g_add(mine(), (mine(), pair(), came())))
        else:
            pl.when(pred)(lambda: g_add(mine(), (mine(), pair())))
        send("g", pred, mine, there, ssem, rsem, tgt)

    def g_hop(unit, h):
        for zt in range(top, h, -1):
            came = lambda zt=zt: g_in(unit, t_up, zt - 1)
            sem = lambda zt=zt: ur.at[unit * top + zt - 1]
            g_step(unit, z == h, zt, h > 0, came, sem, lambda zt=zt: us.at[unit * top + zt - 1], sem, came, to_up)
        for zt in range(top - h):
            came = lambda zt=zt: g_in(unit, t_dn, zt)
            sem = lambda zt=zt: vr.at[unit * top + zt]
            g_step(unit, z == top - h, zt, h > 0, came, sem, lambda zt=zt: vs.at[unit * top + zt], sem, came, to_dn)

    def g_last(unit, acc):
        up_ref = lambda: g_in(unit, t_up, z - 1)
        dn_ref = lambda: g_in(unit, t_dn, z)
        recv(True, lambda: g_in(unit, t_dd, z), lambda: dr_.at[unit * nz + z])
        recv(has_dn, up_ref, lambda: ur.at[unit * top + z - 1])
        recv(has_up, dn_ref, lambda: vr.at[unit * top + z])
        g_add(acc, (g_own(unit, z, c), g_in(unit, t_dd, z)))
        pl.when(has_dn)(lambda: g_add(acc, (acc, up_ref())))
        pl.when(has_up)(lambda: g_add(acc, (acc, dn_ref())))

    def row_send(unit, idx):
        first, n = span(unit)
        row = 0 if unit in PIECES else SLOT[unit]
        return big.at[idx, pl.ds(row * rows, rows), pl.ds(2 * fs + (first if unit in PIECES else 0), n)]

    def g_rows(unit):
        first, n = span(unit)
        facc = mbuf.at[:, pl.ds(0, rows), pl.ds(0, n)]
        g_last(unit, facc)
        u = SLOT[unit]
        for k in range(4):
            row_send(unit, k)[...] = facc[k].astype(BF)
        rbuf[d, :, cols(unit)] = facc[d].astype(BF)
        for k, (idx, tgt) in enumerate(peers):
            send(
                "rows", True,
                lambda idx=idx: row_send(unit, idx),
                lambda: rbuf.at[d, :, cols(unit)],
                lambda k=k: qs.at[u * 3 + k], lambda k=k: qr.at[u * 3 + k], tgt,
            )

    def g_rows_wait(unit):
        u = SLOT[unit]
        first, n = span(unit)
        for k, (idx, _) in enumerate(peers):
            recv(True, lambda idx=idx: rbuf.at[idx, :, cols(unit)], lambda k=k: qr.at[u * 3 + k])

    count = 4 * fs // uw

    def wide_in(i):
        ref = wg_ref if i < count else wu_ref
        return pltpu.make_async_copy(
            ref.at[:, pl.ds((i % count) * uw, uw)], mbuf.at[i // 8, pl.ds((i % 8) * rows, rows), :], ins.at[i]
        )

    def wide_read(i, first, n):
        b = i * count + first // uw
        return mbuf[b // 8, pl.ds((b % 8) * rows, rows), pl.ds(first % uw, n)]

    x_in = pltpu.make_async_copy(x_ref.at[0], xa.at[d], ins.at[2 * count])
    do_in = pltpu.make_async_copy(do_ref.at[0], oa.at[d], ins.at[2 * count + 1])
    def down_in(i):
        n = (uw, wid - uw)[i]
        return pltpu.make_async_copy(
            wdn_ref.at[:, pl.ds(i * uw, n)], mbuf.at[2, pl.ds(i * drows, drows), pl.ds(0, n)] if i == 0
            else mbuf.at[3, pl.ds(0, drows), pl.ds(0, n)], ins.at[2 * count + 2 + i]
        )

    def first_in(i):
        return pltpu.make_async_copy(
            win_ref.at[:, pl.ds(i * uw, uw)], mbuf.at[2 + i // 2, pl.ds(tok - rows * (1 + i % 2), rows), :], ins.at[2 * count + 4 + i]
        )

    for i in range(4):
        first_in(i).start()
    x_in.start()
    for i in range(2 * count):
        wide_in(i).start()
    for i in range(2):
        down_in(i).start()
    do_in.start()
    for i in range(4):
        first_in(i).wait()
    for k in range(4):
        for p in range(3):
            b, first = divmod(p * wid + k * ch, uw)
            stage[k, :, pl.ds(p * ch, ch)] = mbuf[2 + b // 2, pl.ds(tok - rows * (1 + b % 2), rows), pl.ds(first, ch)].astype(BF)
    lanes = taps_ref.shape[1]
    lane0 = lax.rem(s * rows, 128)
    gsum[...] = jnp.zeros_like(gsum)
    gsum[0:1, 0:lanes] = n1_ref[...]
    gsum[1:2, 0:lanes] = n2_ref[...]
    gsum[2:5, 0:lanes] = taps_ref[...]
    gb[d, z, c] = pltpu.roll(gsum[...], lane0, 1).astype(BF)
    wo[pl.ds(pl.multiple_of(s * rows, rows), rows), :] = wout_ref[...].astype(BF)
    enter()
    for k, (idx, tgt) in enumerate(peers):
        send("w", True, lambda: gb.at[d, z, c], lambda: gb.at[d, z, c], lambda k=k: gs.at[k], lambda k=k: gr.at[k], tgt)
    w_slice(IN)
    x_in.wait()
    ag_start(AX, xa)
    z_own(OUT)
    mid = seg_ref[:, pl.ds(pl.multiple_of(s * tok, tok), tok)]
    near[:, pl.ds(128, tok)] = mid
    near[:, pl.ds(0, 128)] = jnp.full((1, 128), -1, jnp.int32)
    near[:, pl.ds(128 + tok, 128)] = jnp.full((1, 128), -1, jnp.int32)

    @pl.when(s > 0)
    def _():
        near[:, pl.ds(0, 128)] = seg_ref[:, pl.ds(pl.multiple_of(s * tok - 128, 128), 128)]

    @pl.when(s < 2 * nz - 1)
    def _():
        near[:, pl.ds(128 + tok, 128)] = seg_ref[:, pl.ds(pl.multiple_of(s * tok + tok, 128), 128)]

    around = near[...]
    lane = lax.broadcasted_iota(jnp.int32, (128, tok), 0)
    flags = jnp.zeros((128, tok), F32)
    for k, move in enumerate((1, 2, tok + 255, tok + 254)):
        moved = pltpu.roll(around, move, 1)[:, 128 : 128 + tok]
        flags = jnp.where(lane == k, jnp.where(moved == mid, 1.0, 0.0), flags)
    fm[d] = flags[:16].astype(BF)
    for k, (idx, _) in enumerate(peers):
        recv(True, lambda idx=idx: gb.at[idx, z, c], lambda k=k: gr.at[k])
    z_own(GAIN)
    w_slice_wait(IN)
    z_own(IN)
    for i in range(2 * count):
        wide_in(i).wait()
    for k in range(4):
        for j in range(3):
            stage[k, :, pl.ds((1 + j) * uw, cj)] = wide_read(0, k * fs + j * cj, cj).astype(BF)
            stage[k, :, pl.ds((1 + j) * uw + cj, cj)] = wide_read(1, k * fs + j * cj, cj).astype(BF)
    for i in range(2):
        down_in(i).wait()
    wd[pl.ds(pl.multiple_of(s * drows, drows), drows), pl.ds(0, uw)] = mbuf[2, pl.ds(0, drows), :].astype(BF)
    wd[pl.ds(pl.multiple_of(s * drows, drows), drows), pl.ds(uw, wid - uw)] = mbuf[3, pl.ds(0, drows), pl.ds(0, wid - uw)].astype(BF)
    z_fwd(OUT, 1)
    z_fwd(GAIN, 1)
    ag_fwd(AX, xa)
    for k, (idx, tgt) in enumerate(peers):
        send("ag", True, lambda: fm.at[d], lambda: fm.at[d], lambda k=k: ms.at[k], lambda k=k: mr.at[k], tgt)
    w_slice(GU0)
    z_fwd(IN, 1)
    z_fwd(GAIN, 2)
    z_fwd(OUT, 2)
    w_slice(GU1)
    w_slice(GU2)
    do_in.wait()
    ag_first(AO, oa)
    z_fwd(GAIN, 3)
    z_finish(GAIN)
    per = 128 // rows
    for g in range(wid // 128):
        tot = None
        for i in range(g * per, (g + 1) * per):
            dd, q = i // (2 * nz), i % (2 * nz)
            piece = gb[dd, q // 2, q % 2].astype(F32)
            tot = piece if tot is None else tot + piece
        gv[:, pl.ds(g * 128, 128)] = tot

    step = 32

    def norm_rows(xv):
        return lax.rsqrt(jnp.mean(xv * xv, axis=1, keepdims=True) + epsilon)

    zcol = pl.ds(0, wid)
    zstep = 64

    def make_z1(dd):
        @pl.loop(0, tok // zstep)
        def _(i):
            rr = pl.ds(pl.multiple_of(i * zstep, zstep), zstep)
            xv = xa[dd, rr, :].astype(F32)
            big[dd, rr, zcol] = (xv * norm_rows(xv) * gv[0:1, :]).astype(BF)

    make_z1(d)
    ag_near(AX, xa)
    make_z1(xn)
    make_z1(yn)
    z_fwd(IN, 2)
    z_fwd(OUT, 3)
    z_own(DOWN)
    ag_far(AX, xa)
    make_z1(dg)
    w_slice_wait(GU0)
    z_own(GU0)
    z_fwd(IN, 3)
    z_finish(IN)
    for k, (idx, _) in enumerate(peers):
        recv(True, lambda idx=idx: fm.at[idx], lambda k=k: mr.at[k])
    for dd in range(4):
        ma[dd] = jnp.concatenate([fm[dd].astype(F32), jnp.zeros((112, tok), F32)], axis=0).T.astype(BF)

    def unit_w(lo_col, n):
        return wall[:, :, :, :, pl.ds(lo_col, n)].reshape(wid, n)

    @pl.loop(0, 4)
    def _(dd):
        m = dot_nn(big[dd, :, zcol], unit_w(0, uw))
        mbuf[dd] = m
        pbuf[dd] = (m[:, :ch] * m[:, 2 * ch :]).astype(BF)

    tail = 16
    send("halo", s < 2 * nz - 1, lambda: pbuf.at[:, pl.ds(tok - tail, tail), :], lambda: halo_p,
         lambda: hs.at[0], lambda: hr.at[0], to_next)

    @pl.when(s == 0)
    def _():
        halo_p[...] = jnp.zeros_like(halo_p)

    z_finish(OUT)
    w_slice_wait(GU1)
    z_own(GU1)
    recv(s > 0, lambda: halo_p, lambda: hr.at[0])
    tap_cols = pl.ds(pl.multiple_of(d * ch, ch), ch)
    row = lax.broadcasted_iota(jnp.int32, (tok, ch), 0)

    def past(dd):
        cur = pbuf[dd].astype(F32)
        old = halo_p[dd].astype(F32)
        masks = ma[dd].astype(F32)
        one = jnp.where(row == 0, old[tail - 1 : tail], pltpu.roll(cur, 1, 0)) * masks[:, 0:1]
        two = jnp.where(row == 0, old[tail - 2 : tail - 1], jnp.where(row == 1, old[tail - 1 : tail], pltpu.roll(cur, 2, 0)))
        return cur, one, two * masks[:, 1:2], masks

    def convolve(cur, one, two):
        return gv[2:3, tap_cols] * cur + gv[3:4, tap_cols] * one + gv[4:5, tap_cols] * two

    def conv_rows(dd):
        cur, one, two, _ = past(dd)
        ybuf[dd] = (mbuf[dd, :, pl.ds(ch, ch)] * convolve(cur, one, two)).astype(BF)

    def h_tile(dd):
        conv_rows(dd)
        return dot_nn(ybuf[dd], wo[...])

    rs_run(0, sb_a, bufs_a, h_tile, "rs0")
    hid[...] = h_tile(d)
    w_slice_wait(GU2)
    z_own(GU2)
    z_fwd(GU0, 1)
    rs_pass(0, sb_a, bufs_a, "rs0")
    ag_fwd(AO, oa)
    z_fwd(GU1, 1)
    z_fwd(GU2, 1)
    z_fwd(DOWN, 1)
    z_fwd(GU0, 2)
    rs_wait(0, bufs_a)

    @pl.loop(0, tok // step)
    def _(i):
        rr = pl.ds(pl.multiple_of(i * step, step), step)
        h = xa[d, rr, :].astype(F32) + hid[rr, :] + rx_a[rr, :].astype(F32) + ry_a[rr, :].astype(F32)
        hid[rr, :] = h
        za[d, rr, :] = (h * norm_rows(h) * gv[1:2, :]).astype(BF)

    ag_start(AZ, za)

    def acol(j):
        return pl.ds(j * cj, cj)

    def gcol(j):
        return pl.ds(fs + j * uw, cj)

    def ucol(j):
        return pl.ds(fs + j * uw + cj, cj)

    def gate_one(j, dd):
        gu = dot_nn(za[dd], unit_w((1 + j) * uw, uw))
        g, u = gu[:, :cj], gu[:, cj:]
        sig = jax.nn.sigmoid(g)
        sw = g * sig
        big[dd, :, acol(j)] = (sw * u).astype(BF)
        big[dd, :, gcol(j)] = (u * sig * (1.0 + g * (1.0 - sig))).astype(BF)
        big[dd, :, ucol(j)] = sw.astype(BF)

    def gate_all(j):
        @pl.loop(0, 4)
        def _(dd):
            gate_one(j, dd)

    def back_all(j):
        @pl.loop(0, 4)
        def _(dd):
            da = dot_nt(oa[dd], wd[pl.ds(j * cj, cj), :])
            big[dd, :, gcol(j)] = (da * big[dd, :, gcol(j)].astype(F32)).astype(BF)
            big[dd, :, ucol(j)] = (da * big[dd, :, ucol(j)].astype(F32)).astype(BF)

    def grad_gu(j):
        @pl.loop(0, 4)
        def _(dd):
            left = za[:, :, pl.ds(pl.multiple_of(dd * ch, ch), ch)].reshape(4 * tok, ch)
            right = big[:, :, pl.ds(fs + j * uw, uw)].reshape(4 * tok, uw)
            res = dot_tn(left, right).astype(BF)
            gw[dd, :, :, :, pl.ds((1 + j) * uw, uw)] = res.reshape(nz, 2, rows, uw)

    def grad_down(j):
        left = big[:, :, pl.ds(j * cj, cj)].reshape(4 * tok, cj)
        gd[pl.ds(j * cj, cj), :] = dot_tn(left, oa[...].reshape(4 * tok, wid)).astype(BF)

    def dz2_tile(dd):
        return dot_nt(big[dd, :, pl.ds(fs, 3 * uw)], unit_w(uw, 3 * uw))

    def out_tile(dd):
        return dot_nn(big[dd, :, pl.ds(0, fs)], wd[...])

    z_fwd(GU1, 2)
    ag_fwd(AZ, za)
    ag_second(AO, oa)
    z_fwd(GU0, 3)
    z_fwd(GU2, 2)
    ag_near(AZ, za)
    z_finish(GU0)
    for dd in (d, xn, yn):
        gate_one(0, dd)
    z_fwd(DOWN, 2)
    z_fwd(GU1, 3)
    z_finish(GU1)
    ag_far(AZ, za)
    gate_one(0, dg)
    gate_all(1)
    z_fwd(GU2, 3)
    z_finish(GU2)
    gate_all(2)
    ag_near(AO, oa)
    ag_far(AO, oa)
    grad_down(0)
    g_pair(DOWN, (0,))
    grad_down(2)
    g_pair(DOWN, (3,))
    grad_down(1)
    g_pair(DOWN, (1, 2))
    g_hop(DOWN, 0)
    z_fwd(DOWN, 3)
    z_finish(DOWN)
    rs_run(2, sb_b, bufs_b, out_tile, "rs2")
    for j in range(3):
        back_all(j)

    drain("rs0")
    rs_run(1, sb_a, bufs_a, dz2_tile, "rs1")
    grad_gu(0)
    g_pair(GU0)
    g_hop(DOWN, 1)
    dh[...] = dz2_tile(d)
    g_hop(GU0, 0)
    rs_pass(1, sb_a, bufs_a, "rs1")
    grad_gu(1)
    g_pair(GU1)
    g_hop(DOWN, 2)
    g_hop(GU1, 0)
    grad_gu(2)
    g_pair(GU2)
    g_hop(GU0, 1)
    rs_wait(1, bufs_a)

    @pl.loop(0, tok // step)
    def _(i):
        rr = pl.ds(pl.multiple_of(i * step, step), step)
        dz = dh[rr, :] + rx_a[rr, :].astype(F32) + ry_a[rr, :].astype(F32)
        h = hid[rr, :]
        inv = norm_rows(h)
        unit = h * inv
        e = dz * gv[1:2, :]
        g = oa[d, rr, :].astype(F32) + inv * (e - unit * jnp.mean(e * unit, axis=1, keepdims=True))
        dh[rr, :] = g
        ra[d, rr, :] = g.astype(BF)

    ag_start(AR, ra)
    g_hop(GU2, 0)
    hid[...] = hid[...] + out_tile(d)
    for dd in (d, xn, yn, dg):
        make_z1(dd)
    g_hop(GU0, 2)
    ag_fwd(AR, ra)
    g_hop(GU1, 1)
    rs_pass(2, sb_b, bufs_b, "rs2")
    ag_near(AR, ra)
    g_hop(GU1, 2)
    ag_far(AR, ra)

    mcol = fs
    zero_tap = jnp.zeros((8, ch), F32)

    def back_conv(dd, acc):
        dy = dot_nt(ra[dd], wo[...])
        cur, one, two, _ = past(dd)
        q = dy * mbuf[dd, :, pl.ds(ch, ch)]
        mbuf[dd, :, pl.ds(ch, ch)] = q
        big[dd, :, pl.ds(mcol + ch, ch)] = (dy * convolve(cur, one, two)).astype(BF)
        return tuple(a + (q * v).reshape(tok // 8, 8, ch).sum(axis=0) for a, v in zip(acc, (cur, one, two)))

    taps = lax.fori_loop(0, 4, back_conv, (zero_tap, zero_tap, zero_tap))
    head = 8
    send("halo", s > 0, lambda: mbuf.at[:, pl.ds(0, head), pl.ds(ch, ch)], lambda: halo_q, lambda: hs.at[1], lambda: hr.at[1], to_prev)

    @pl.when(s == 2 * nz - 1)
    def _():
        halo_q[...] = jnp.zeros_like(halo_q)

    lines = lax.broadcasted_iota(jnp.int32, (rows, ch), 0)
    tap_rows = jnp.zeros((rows, ch), F32)
    for k in range(3):
        tap_rows = jnp.where(lines == k, jnp.sum(taps[k], axis=0, keepdims=True), tap_rows)
    for q in range(2 * nz):
        first = (q * rows) // 128 * 128
        go[pl.ds(q * rows, rows), pl.ds(wid, 128)] = tap_rows[:, first : first + 128].astype(BF)
    go[:, pl.ds(0, wid)] = dot_tn(ybuf[...].reshape(4 * tok, ch), ra[...].reshape(4 * tok, wid)).astype(BF)
    g_pair(OUT)
    g_hop(GU2, 1)
    recv(s < 2 * nz - 1, lambda: halo_q, lambda: hr.at[1])

    @pl.loop(0, 4)
    def _(dd):
        q = mbuf[dd, :, pl.ds(ch, ch)]
        new = halo_q[dd]
        masks = ma[dd].astype(F32)
        one = jnp.where(row == tok - 1, new[0:1], pltpu.roll(q, tok - 1, 0)) * masks[:, 2:3]
        two = jnp.where(row == tok - 2, new[0:1], jnp.where(row == tok - 1, new[1:2], pltpu.roll(q, tok - 2, 0)))
        dp = gv[2:3, tap_cols] * q + gv[3:4, tap_cols] * one + gv[4:5, tap_cols] * (two * masks[:, 3:4])
        big[dd, :, pl.ds(mcol, ch)] = (dp * mbuf[dd, :, pl.ds(2 * ch, ch)]).astype(BF)
        big[dd, :, pl.ds(mcol + 2 * ch, ch)] = (dp * mbuf[dd, :, pl.ds(0, ch)]).astype(BF)

    drain("rs1")

    def dz1_tile(dd):
        return dot_nt(big[dd, :, pl.ds(mcol, uw)], unit_w(0, uw))

    rs_run(3, sb_a, bufs_a, dz1_tile, "rs3")

    def grad_in(p):
        left = big[:, :, zcol].reshape(4 * tok, wid)
        right = big[:, :, pl.ds(mcol + p * ch, ch)].reshape(4 * tok, ch)
        gw[:, :, :, :, pl.ds(p * ch, ch)] = dot_tn(left, right).astype(BF).reshape(4, nz, 2, rows, ch)

    g_hop(OUT, 0)
    grad_in(0)
    g_pair(IN_A)
    grad_in(1)
    g_pair(IN_B)
    g_hop(IN_A, 0)
    grad_in(2)
    g_pair(IN_C)
    g_hop(IN_B, 0)
    g_hop(GU2, 2)
    g_hop(IN_C, 0)
    rs_pass(3, sb_a, bufs_a, "rs3")
    g_hop(OUT, 1)
    rs_wait(2, bufs_b)

    @pl.loop(0, tok // step)
    def _(i):
        rr = pl.ds(pl.multiple_of(i * step, step), step)
        sb_b[d, rr, :] = (hid[rr, :] + rx_b[rr, :].astype(F32) + ry_b[rr, :].astype(F32)).astype(BF)

    result = pltpu.make_async_copy(sb_b.at[d], out_ref.at[0], ins.at[2 * count])
    result.start()
    hid[...] = dz1_tile(d)
    drain("halo")
    g_hop(IN_A, 1)
    g_hop(OUT, 2)
    g_hop(IN_B, 1)
    g_hop(IN_A, 2)
    g_rows(GU0)
    g_hop(IN_C, 1)
    g_hop(IN_B, 2)
    g_rows(GU1)
    g_last(DOWN, gdown_ref)
    g_hop(IN_C, 2)
    g_rows(GU2)
    rs_wait(3, bufs_a)

    @pl.loop(0, tok // step)
    def _(i):
        rr = pl.ds(pl.multiple_of(i * step, step), step)
        dz = hid[rr, :] + rx_a[rr, :].astype(F32) + ry_a[rr, :].astype(F32)
        xv = xa[d, rr, :].astype(F32)
        inv = norm_rows(xv)
        unit = xv * inv
        e = dz * gv[0:1, :]
        g = dh[rr, :] + inv * (e - unit * jnp.mean(e * unit, axis=1, keepdims=True))
        sb_a[d, rr, :] = g.astype(BF)

    grads = pltpu.make_async_copy(sb_a.at[d], gtok_ref.at[0], ins.at[2 * count + 1])
    grads.start()

    g_rows(IN_A)
    g_last(OUT, oacc)
    gout_ref[...] = oacc[:, pl.ds(0, wid)]
    gsmall_ref[pl.ds(8, 8), :] = pltpu.roll(oacc[0:16, pl.ds(wid, 128)], lax.rem(128 - lane0, 128), 1)[:8]
    for unit in (GU0, GU1, GU2):
        g_rows_wait(unit)
    g_rows(IN_B)

    def gain_sum(first, n):
        acc = jnp.zeros((rows, 128), F32)
        for k in range(4):
            for q in range(n // 128):
                cc = pl.ds(first + q * 128, 128)
                acc = acc + stage[k, :, cc].astype(F32) * rbuf[k, :, cc].astype(F32)
        return acc

    def gain_out(k, first, n, gain):
        total = lax.dot_general(
            jnp.ones((8, 128), F32), gain_sum(first, n), (((1,), (1,)), ((), ())),
            precision=lax.Precision.HIGHEST, preferred_element_type=F32,
        )
        gsmall_ref[k : k + 1, 0:lanes] = total[0:1] / gain[...].astype(BF).astype(F32)

    gain_out(1, uw, 3 * uw, n2_ref)
    g_rows(IN_C)
    for unit in PIECES:
        g_rows_wait(unit)
    gain_out(0, 0, uw, n1_ref)
    result.wait()
    grads.wait()
    drain()


def move_out(shape, *refs):
    lanes, ch, fs, cj, uw = shape
    out_in, tok_in, tile_in, go_in, gd_in, small, out_ref, tok_ref, in_ref, go_ref, gate_ref, up_ref, gd_ref = refs[:13]
    one_ref, two_ref, taps_ref, a, b, tile, e, f, gin, gate, up, sems, done = refs[13:]
    wid = 4 * ch
    pairs = ((tile_in, tile, None), (out_in, a, out_ref), (tok_in, b, tok_ref), (gd_in, f, gd_ref), (go_in, e, go_ref))
    loads = [pltpu.make_async_copy(p[0], p[1], sems.at[k]) for k, p in enumerate(pairs)]
    for load in loads:
        load.start()
    one_ref[...] = small[0:1, 0:lanes]
    two_ref[...] = small[1:2, 0:lanes]
    taps_ref[...] = small[8:11, 0:lanes]
    stores = [pltpu.make_async_copy(p[1], p[2], done.at[k + 1]) for k, p in enumerate(pairs[1:])]
    loads[0].wait()
    for k in range(4):
        for p in range(3):
            gin[:, pl.ds(p * wid + k * ch, ch)] = tile[k, :, pl.ds(p * ch, ch)].astype(F32)
            first = (1 + p) * uw
            gate[:, pl.ds(k * fs + p * cj, cj)] = tile[k, :, pl.ds(first, cj)].astype(F32)
            up[:, pl.ds(k * fs + p * cj, cj)] = tile[k, :, pl.ds(first + cj, cj)].astype(F32)
    stores += [pltpu.make_async_copy(v, r, done.at[5 + k]) for k, (v, r) in enumerate(((gin, in_ref), (gate, gate_ref), (up, up_ref)))]
    for store in stores[4:]:
        store.start()
    for load, store in zip(loads[1:], stores):
        load.wait()
        store.start()
    for store in stores:
        store.wait()


def fast_body(n_dp, n_seq, tokens, segments, cotangent, in_weight, out_weight, gate_weight, up_weight, down_weight, norm_one, norm_two, kernel):
    tok, wid = tokens.shape[1], tokens.shape[2]
    nz = n_seq // 2
    rows = in_weight.shape[0]
    drows = down_weight.shape[0]
    ch = wid // n_dp
    fs = gate_weight.shape[1] // n_dp
    uw = 3 * ch
    cj = uw // 2
    lanes = kernel.shape[1]

    dims = (tok, wid, nz, rows, ch, fs, cj, uw, drows)
    top = nz - 1
    vm = pltpu.VMEM
    dma = lambda n: pltpu.SemaphoreType.DMA((n,))
    plane = lambda w, t=BF: vm((n_dp, tok, w), t)
    rs_set = [vm((tok, wid), BF)] * 2 + [vm((tok // 2, wid), BF)] * 2
    came = lambda n: (vm((n, n_dp, rows, 4 * uw), BF), vm((n, drows, wid), BF), vm((n, rows, wid + 128), BF))
    scratch = [
        vm((n_dp, rows, 4 * uw), BF),
        vm((n_dp, nz, 2, rows, 4 * uw), BF),
        vm((ch, wid), BF),
        vm((fs, wid), BF),
        vm((n_dp, nz, 2, 16, 128), BF),
        vm((16, wid), F32),
        plane(wid), plane(128), plane(wid), plane(wid), plane(wid),
        plane(3 * fs),
        plane(uw, F32), plane(ch), plane(ch),
        vm((n_dp, 16, ch), BF),
        vm((n_dp, 8, ch), F32),
        plane(wid), plane(wid),
        *rs_set, *rs_set,
        vm((tok, wid), F32), vm((tok, wid), F32),
        vm((n_dp, nz, 2, rows, 4 * uw), BF), vm((fs, wid), BF), vm((ch, wid + 128), BF),
        *came(nz), *came(top), *came(top),
        vm((16, 128), F32), vm((1, tok + 256), jnp.int32), vm((n_dp, 16, tok), BF), vm((rows, wid + 128), F32),
        dma(7 * 13), dma(7 * 2 * nz), dma(12), dma(12), dma(3), dma(3), dma(3), dma(3), dma(2), dma(2),
        dma(24), dma(24), dma(24), dma(24), dma(10 * nz), dma(10 * nz),
        dma(10 * top), dma(10 * top), dma(10 * top), dma(10 * top), dma(21), dma(21), dma(8 * fs // uw + 8),
    ]
    f32 = lambda a: jax.ShapeDtypeStruct(a.shape, F32)
    vspec, anywhere = pl.BlockSpec(memory_space=vm), pl.BlockSpec(memory_space=pl.ANY)
    res = pl.pallas_call(
        functools.partial(block_kernel, dims),
        out_shape=(
            jax.ShapeDtypeStruct(tokens.shape, BF), jax.ShapeDtypeStruct(tokens.shape, BF),
            jax.ShapeDtypeStruct((n_dp, rows, 4 * uw), BF), f32(out_weight), f32(down_weight),
            jax.ShapeDtypeStruct((16, 128), F32),
        ),
        in_specs=[anywhere] * 2 + [vspec] * 4 + [anywhere, vspec] + [anywhere] * 3,
        out_specs=(anywhere,) * 2 + (vspec,) * 4,
        scratch_shapes=scratch,
        compiler_params=pltpu.CompilerParams(collective_id=0, has_side_effects=True, vmem_limit_bytes=64 * 1024 * 1024),
    )(tokens, cotangent, segments, norm_one[None], norm_two[None], kernel, in_weight, out_weight, gate_weight, up_weight, down_weight)
    final = [jax.ShapeDtypeStruct(v.shape, v.dtype) for v in res[:2]]
    final += [f32(w) for w in (in_weight, out_weight, gate_weight, up_weight, down_weight)]
    final += [jax.ShapeDtypeStruct((k, lanes), F32) for k in (1, 1, 3)]
    moved = pl.pallas_call(
        functools.partial(move_out, (lanes, ch, fs, cj, uw)),
        out_shape=tuple(final),
        in_specs=[anywhere] * 5 + [vspec],
        out_specs=(anywhere,) * 7 + (vspec,) * 3,
        scratch_shapes=[vm(v.shape, v.dtype) for v in res[:5]]
        + [vm(w.shape, F32) for w in (in_weight, gate_weight, up_weight)] + [dma(5), dma(8)],
    )(*res)
    return (*moved[:7], moved[7][0], moved[8][0], moved[9])


def gather(value, axis=0):
    return lax.all_gather(value.astype(BF), ("dp", "seq"), axis=axis, tiled=True)


def norm_back(grad_unit, unit_rows, inverse):
    return inverse * (grad_unit - unit_rows * jnp.mean(grad_unit * unit_rows, axis=1, keepdims=True))


def from_behind(value, axis, steps):
    count = lax.axis_size(axis)
    leading, last = (max(0, -steps), min(count, count - steps))
    return lax.ppermute(value, axis, [(source, source + steps) for source in range(leading, last)])


def spread(value):
    n_dp, n_seq = lax.axis_size("dp"), lax.axis_size("seq")
    shaped = value.reshape((n_dp, n_seq, value.shape[0] // (n_dp * n_seq)) + value.shape[1:]).astype(BF)
    moved = lax.all_to_all(shaped, "seq", split_axis=1, concat_axis=1, tiled=True).astype(F32)
    summed = jnp.sum(moved, axis=1).astype(BF)
    owned = lax.psum_scatter(summed, "dp", scatter_dimension=0, tiled=True).astype(F32)
    return owned.reshape(owned.shape[1:])


def plain_body(tokens, segments, cotangent, in_weight, out_weight, gate_weight, up_weight, down_weight, norm_one, norm_two, kernel):
    width, count = tokens.shape[2], tokens.shape[1]
    in_mat, out_mat, gate_mat, up_mat, down_mat = map(gather, (in_weight, out_weight, gate_weight, up_weight, down_weight))
    gain_a, gain_b = gather(norm_one).astype(F32), gather(norm_two).astype(F32)
    taps = gather(kernel, 1).astype(F32)
    filler = jnp.full((2,), -1, jnp.int32)
    near = lax.dynamic_slice_in_dim(jnp.concatenate([filler, segments[0], filler]), lax.axis_index("seq") * count, count + 4)
    mid = near[2 : count + 2]
    same = lambda first: (mid == near[first : count + first]).astype(F32)[:, None]
    resident = tokens[0].astype(F32)
    inverse_a = lax.rsqrt(jnp.mean(resident * resident, axis=1, keepdims=True) + epsilon)
    unit_a = resident * inverse_a
    normed_a = (unit_a * gain_a).astype(BF)
    mixed = dot_nn(normed_a, in_mat)
    b_part, c_part, x_part = mixed[:, :width], mixed[:, width : 2 * width], mixed[:, 2 * width :]
    conv_in = (b_part * x_part).astype(BF)
    extended = jnp.concatenate([from_behind(conv_in[count - 2 :], "seq", 1), conv_in], axis=0).astype(F32)
    current, prev_one, prev_two = extended[2:], extended[1 : count + 1] * same(1), extended[0:count] * same(0)
    convolved = taps[0] * current + taps[1] * prev_one + taps[2] * prev_two
    gated = (c_part * convolved).astype(BF)
    hidden = resident + dot_nn(gated, out_mat)
    inverse_b = lax.rsqrt(jnp.mean(hidden * hidden, axis=1, keepdims=True) + epsilon)
    unit_b = hidden * inverse_b
    normed_b = (unit_b * gain_b).astype(BF)
    gate_pre, up_pre = dot_nn(normed_b, gate_mat), dot_nn(normed_b, up_mat)
    sig = jax.nn.sigmoid(gate_pre)
    swish = gate_pre * sig
    active = (swish * up_pre).astype(BF)
    output = hidden + dot_nn(active, down_mat)
    grad_low = cotangent[0]
    grad_active = dot_nt(grad_low, down_mat)
    grad_gate_pre = (grad_active * up_pre * sig * (1.0 + gate_pre * (1.0 - sig))).astype(BF)
    grad_up_pre = (grad_active * swish).astype(BF)
    grad_normed_b = dot_nt(grad_gate_pre, gate_mat) + dot_nt(grad_up_pre, up_mat)
    grad_hidden = grad_low.astype(F32) + norm_back(grad_normed_b * gain_b, unit_b, inverse_b)
    grad_branch = grad_hidden.astype(BF)
    grad_gated = dot_nt(grad_branch, out_mat)
    grad_conv = grad_gated * c_part
    ahead = jnp.concatenate([grad_conv, from_behind(grad_conv[:2], "seq", -1)], axis=0)
    grad_conv_in = taps[0] * grad_conv + taps[1] * (ahead[1 : count + 1] * same(3)) + taps[2] * (ahead[2 : count + 2] * same(4))
    grad_taps = jnp.stack([jnp.sum(grad_conv * part, axis=0) for part in (current, prev_one, prev_two)])
    grad_mixed = jnp.concatenate([grad_conv_in * x_part, grad_gated * convolved, grad_conv_in * b_part], axis=1).astype(BF)
    grad_normed_a = dot_nt(grad_mixed, in_mat)
    grad_resident = grad_hidden + norm_back(grad_normed_a * gain_a, unit_a, inverse_a)
    return (
        output.astype(BF)[None],
        grad_resident.astype(BF)[None],
        spread(dot_tn(normed_a, grad_mixed)),
        spread(dot_tn(gated, grad_branch)),
        spread(dot_tn(normed_b, grad_gate_pre)),
        spread(dot_tn(normed_b, grad_up_pre)),
        spread(dot_tn(active, grad_low)),
        spread(jnp.sum(grad_normed_a * unit_a, axis=0)),
        spread(jnp.sum(grad_normed_b * unit_b, axis=0)),
        jnp.transpose(spread(jnp.transpose(grad_taps))),
    )


def solution(mesh):
    n_dp, n_seq = mesh.shape["dp"], mesh.shape["seq"]

    def body(*args):
        tokens, in_weight, gate_weight, down_weight = args[0], args[3], args[5], args[7]
        width = tokens.shape[2]
        unit = 3 * width // max(n_dp, 1)
        fits = (
            n_dp == 4
            and n_seq % 2 == 0
            and tokens.shape[0] == 1
            and in_weight.shape[0] % 16 == 0
            and down_weight.shape[0] % 16 == 0
            and 128 % in_weight.shape[0] == 0
            and unit % 256 == 0
            and 2 * gate_weight.shape[1] == 3 * unit * n_dp
        )
        if fits:
            return fast_body(n_dp, n_seq, *args)
        return plain_body(*args)

    return jax.shard_map(
        body,
        mesh=mesh,
        in_specs=(
            P("dp", "seq", None),
            P("dp", None),
            P("dp", "seq", None),
            P(("dp", "seq"), None),
            P(("dp", "seq"), None),
            P(("dp", "seq"), None),
            P(("dp", "seq"), None),
            P(("dp", "seq"), None),
            P(("dp", "seq")),
            P(("dp", "seq")),
            P(None, ("dp", "seq")),
        ),
        out_specs=(
            P("dp", "seq", None),
            P("dp", "seq", None),
            P(("dp", "seq"), None),
            P(("dp", "seq"), None),
            P(("dp", "seq"), None),
            P(("dp", "seq"), None),
            P(("dp", "seq"), None),
            P(("dp", "seq")),
            P(("dp", "seq")),
            P(None, ("dp", "seq")),
        ),
        check_vma=False,
    )
```

```python
import functools

import jax
import jax.numpy as jnp
from jax import lax
from jax.experimental import pallas as pl
from jax.experimental.pallas import tpu as pltpu
from jax.sharding import PartitionSpec as P

epsilon = 1e-05
MESH = pl.DeviceIdType.MESH
BF = jnp.bfloat16
F32 = jnp.float32


def dot_nn(a, b):
    return jnp.dot(a, b, preferred_element_type=F32)


def dot_nt(a, b):
    return lax.dot_general(a, b, (((1,), (1,)), ((), ())), preferred_element_type=F32)


def dot_tn(a, b):
    return lax.dot_general(a, b, (((0,), (0,)), ((), ())), preferred_element_type=F32)


def when(pred, body):
    if pred is True:
        body()
    else:
        pl.when(pred)(body)


GAIN, IN, OUT, GU0, DOWN, GU1, GU2, IN_A, IN_B, IN_C = range(10)
SLOT = {IN: 0, GU0: 1, GU1: 2, GU2: 3, IN_A: 4, IN_B: 5, IN_C: 6}
PIECES = (IN_A, IN_B, IN_C)
AX, AZ, AO, AR = range(4)


def block_kernel(
    dims,
    x_ref, do_ref, seg_ref, n1_ref, n2_ref, taps_ref, win_ref, wout_ref, wg_ref, wu_ref, wdn_ref,
    out_ref, gtok_ref, rbuf, gout_ref, gdown_ref, gsmall_ref,
    stage, wall, wo, wd, gb, gv, xa, ma, za, oa, ra, big, mbuf, pbuf, ybuf, halo_p, halo_q,
    sb_a, sb_b, rx_a, ry_a, fx_a, fy_a, rx_b, ry_b, fx_b, fy_b, hid, dh,
    gw, gd, go, dd_g, dd_d, dd_o, up_g, up_d, up_o, dn_g, dn_d, dn_o,
    gsum, near, fm, oacc, fbuf,
    zs, zr, ws, wr, gs, gr, ms, mr, hs, hr, ags, agr, rss, rsr, ds_, dr_, us, ur, vs, vr, qs, qr, ins,
):
    tok, wid, nz, rows, ch, fs, cj, uw, drows = dims
    half = tok // 2
    d = lax.axis_index("dp")
    s = lax.axis_index("seq")
    x = lax.rem(d, 2)
    y = lax.div(d, 2)
    z = lax.div(s, 2)
    c = lax.rem(s, 2)
    xn = 2 * y + (1 - x)
    yn = 2 * (1 - y) + x
    dg = 2 * (1 - y) + (1 - x)
    oc = 1 - c
    top = nz - 1
    to_x, to_y, to_g = (xn, s), (yn, s), (dg, s)
    to_sib = (d, 2 * z + oc)
    to_up, to_dn = (d, s + 2), (d, s - 2)
    to_next, to_prev = (d, s + 1), (d, s - 1)
    pending = []

    def copy(src, dst, ssem, rsem, tgt):
        return pltpu.make_async_remote_copy(
            src_ref=src(), dst_ref=dst(), send_sem=ssem(), recv_sem=rsem(), device_id=tgt, device_id_type=MESH
        )

    def send(tag, pred, src, dst, ssem, rsem, tgt):
        when(pred, lambda: copy(src, dst, ssem, rsem, tgt).start())
        pending.append((tag, pred, src, dst, ssem, rsem, tgt))

    def recv(pred, dst, rsem):
        when(pred, lambda: copy(dst, dst, rsem, rsem, to_sib).wait_recv())

    def drain(tag=None):
        keep = []
        for item in pending:
            if tag is None or item[0] == tag:
                when(item[1], lambda item=item: copy(*item[2:]).wait_send())
            else:
                keep.append(item)
        pending[:] = keep

    barrier = pltpu.get_barrier_semaphore()

    def greet(tgt):
        pl.semaphore_signal(barrier, inc=1, device_id=tgt, device_id_type=MESH)

    for tgt in (to_x, to_y, to_g, to_sib):
        greet(tgt)
    has_up, has_dn = z < top, z > 0
    pl.when(has_up)(lambda: greet(to_up))
    pl.when(has_dn)(lambda: greet(to_dn))
    cross_next = jnp.logical_and(c == 1, z < top)
    cross_prev = jnp.logical_and(c == 0, z > 0)
    pl.when(cross_next)(lambda: greet(to_next))
    pl.when(cross_prev)(lambda: greet(to_prev))
    def enter():
        ones = [jnp.where(p, 1, 0) for p in (has_up, has_dn, cross_next, cross_prev)]
        pl.semaphore_wait(barrier, 4 + ones[0] + ones[1] + ones[2] + ones[3])

    def span(unit):
        if unit in PIECES:
            return (SLOT[unit] - SLOT[IN_A]) * ch, ch
        return SLOT[unit] * uw, uw

    def cols(unit):
        return pl.ds(*span(unit))

    def w_block(unit, zz, cc):
        if unit == GAIN:
            return gb.at[:, zz, cc]
        if unit == OUT:
            return wo.at[pl.ds(pl.multiple_of((2 * zz + cc) * rows, rows), rows), :]
        if unit == DOWN:
            return wd.at[pl.ds(pl.multiple_of((2 * zz + cc) * drows, drows), drows), :]
        return wall.at[:, zz, cc, :, cols(unit)]

    def z_send(unit, pred, zz, ssem, tgt):
        blk = lambda: w_block(unit, zz, c)
        send("w", pred, blk, blk, lambda: zs.at[unit * 13 + ssem], lambda: zr.at[unit * 2 * nz + 2 * zz + c], tgt)

    def z_own(unit):
        z_send(unit, has_up, z, 0, to_up)
        z_send(unit, has_dn, z, 3, to_dn)
        z_send(unit, True, z, 6, to_sib)

    def z_fwd(unit, k):
        low, high = z - k, z + k
        has_low, has_high = z >= k, z + k <= top
        recv(has_low, lambda: w_block(unit, low, c), lambda: zr.at[unit * 2 * nz + 2 * low + c])
        if k < top:
            z_send(unit, jnp.logical_and(has_low, has_up), low, k, to_up)
        z_send(unit, has_low, low, 6 + k, to_sib)
        recv(has_high, lambda: w_block(unit, high, c), lambda: zr.at[unit * 2 * nz + 2 * high + c])
        if k < top:
            z_send(unit, jnp.logical_and(has_high, has_dn), high, 3 + k, to_dn)
        z_send(unit, has_high, high, 9 + k, to_sib)

    def z_finish(unit):
        for zz in range(nz):
            recv(True, lambda zz=zz: w_block(unit, zz, oc), lambda zz=zz: zr.at[unit * 2 * nz + 2 * zz + oc])

    peers = ((xn, to_x), (yn, to_y), (dg, to_g))

    def w_slice(unit):
        u = SLOT[unit]
        wall[d, z, c, :, cols(unit)] = stage[d, :, cols(unit)]
        for k, (idx, tgt) in enumerate(peers):
            send(
                "stage", True,
                lambda idx=idx: stage.at[idx, :, cols(unit)],
                lambda: wall.at[d, z, c, :, cols(unit)],
                lambda k=k: ws.at[u * 3 + k], lambda k=k: wr.at[u * 3 + k], tgt,
            )

    def w_slice_wait(unit):
        u = SLOT[unit]
        for k, (idx, _) in enumerate(peers):
            recv(True, lambda idx=idx: wall.at[idx, z, c, :, cols(unit)], lambda k=k: wr.at[u * 3 + k])

    lo, hi = pl.ds(0, half), pl.ds(half, half)

    def ag_send(a, buf, idx, part, k, rk, tgt):
        blk = lambda: buf.at[idx, part, :]
        send("ag", True, blk, blk, lambda: ags.at[a * 6 + k], lambda: agr.at[a * 6 + rk], tgt)

    def ag_first(a, buf):
        ag_send(a, buf, d, hi, 0, 1, to_x)
        ag_send(a, buf, d, lo, 1, 2, to_y)

    def ag_second(a, buf):
        ag_send(a, buf, d, lo, 2, 0, to_x)
        ag_send(a, buf, d, hi, 3, 3, to_y)

    def ag_start(a, buf):
        ag_first(a, buf)
        ag_second(a, buf)

    def ag_recv(a, buf, idx, part, rk):
        recv(True, lambda: buf.at[idx, part, :], lambda: agr.at[a * 6 + rk])

    def ag_fwd(a, buf):
        ag_recv(a, buf, yn, lo, 2)
        ag_send(a, buf, yn, lo, 4, 4, to_x)
        ag_recv(a, buf, xn, hi, 1)
        ag_send(a, buf, xn, hi, 5, 5, to_y)

    def ag_near(a, buf):
        ag_recv(a, buf, xn, lo, 0)
        ag_recv(a, buf, yn, hi, 3)

    def ag_far(a, buf):
        ag_recv(a, buf, dg, lo, 4)
        ag_recv(a, buf, dg, hi, 5)

    def rs_send(r, tag, src, dst, k, tgt):
        send(tag, True, src, dst, lambda: rss.at[r * 6 + k], lambda: rsr.at[r * 6 + k], tgt)

    def rs_far(r, sb, bufs, tile, tag):
        sb[dg] = tile(dg).astype(BF)
        rs_send(r, tag, lambda: sb.at[dg, lo, :], lambda: bufs[2], 0, to_x)
        rs_send(r, tag, lambda: sb.at[dg, hi, :], lambda: bufs[3], 1, to_y)

    def rs_direct(r, sb, bufs, tile, tag):
        if tile is not None:
            sb[xn] = tile(xn).astype(BF)
        rs_send(r, tag, lambda: sb.at[xn, lo, :], lambda: bufs[0].at[lo, :], 2, to_x)
        if tile is not None:
            sb[yn] = tile(yn).astype(BF)
        rs_send(r, tag, lambda: sb.at[yn, hi, :], lambda: bufs[1].at[hi, :], 3, to_y)

    def rs_run(r, sb, bufs, tile, tag):
        rs_far(r, sb, bufs, tile, tag)
        rs_direct(r, sb, bufs, tile, tag)

    def rs_pass(r, sb, bufs, tag, first=0):
        wide = pl.ds(first, wid)
        rx, ry, fx, fy = bufs
        recv(True, lambda: fx, lambda: rsr.at[r * 6 + 0])
        sb[yn, lo, wide] = (sb[yn, lo, wide].astype(F32) + fx[...].astype(F32)).astype(BF)
        rs_send(r, tag, lambda: sb.at[yn, lo, wide], lambda: ry.at[lo, :], 4, to_y)
        recv(True, lambda: fy, lambda: rsr.at[r * 6 + 1])
        sb[xn, hi, wide] = (sb[xn, hi, wide].astype(F32) + fy[...].astype(F32)).astype(BF)
        rs_send(r, tag, lambda: sb.at[xn, hi, wide], lambda: rx.at[hi, :], 5, to_x)

    def rs_wait(r, bufs):
        rx, ry, fx, fy = bufs
        recv(True, lambda: rx.at[lo, :], lambda: rsr.at[r * 6 + 2])
        recv(True, lambda: ry.at[hi, :], lambda: rsr.at[r * 6 + 3])
        recv(True, lambda: ry.at[lo, :], lambda: rsr.at[r * 6 + 4])
        recv(True, lambda: rx.at[hi, :], lambda: rsr.at[r * 6 + 5])

    bufs_a = (rx_a, ry_a, fx_a, fy_a)
    bufs_b = (rx_b, ry_b, fx_b, fy_b)

    def g_own(unit, zz, cc):
        if unit == OUT:
            return go.at[pl.ds(pl.multiple_of((2 * zz + cc) * rows, rows), rows), :]
        if unit == DOWN:
            return gd.at[pl.ds(pl.multiple_of((2 * zz + cc) * drows, drows), drows), :]
        return gw.at[:, zz, cc, :, cols(unit)]

    def g_in(unit, trio, zz):
        buf = trio[{OUT: 2, DOWN: 1}.get(unit, 0)]
        if unit in SLOT:
            return buf.at[zz, :, :, cols(unit)]
        return buf.at[zz]

    t_dd = (dd_g, dd_d, dd_o)
    t_up = (up_g, up_d, up_o)
    t_dn = (dn_g, dn_d, dn_o)

    def g_pair(unit, which=range(nz)):
        for zz in which:
            send(
                "g", True, lambda zz=zz: g_own(unit, zz, oc), lambda zz=zz: g_in(unit, t_dd, zz),
                lambda zz=zz: ds_.at[unit * nz + zz], lambda zz=zz: dr_.at[unit * nz + zz], to_sib,
            )

    def g_add(dst, parts):
        if len(dst.shape) == 3:
            for k in range(dst.shape[0]):
                dst[k] = sum(p[k].astype(F32) for p in parts).astype(dst.dtype)
        else:
            dst[...] = sum(p[...].astype(F32) for p in parts).astype(dst.dtype)

    def g_step(unit, pred, zt, come, came, csem, ssem, rsem, there, tgt):
        mine, pair = (lambda: g_own(unit, zt, c)), (lambda: g_in(unit, t_dd, zt))
        recv(pred, pair, lambda: dr_.at[unit * nz + zt])
        if come:
            recv(pred, came, csem)
            pl.when(pred)(lambda: g_add(mine(), (mine(), pair(), came())))
        else:
            pl.when(pred)(lambda: g_add(mine(), (mine(), pair())))
        send("g", pred, mine, there, ssem, rsem, tgt)

    def g_hop(unit, h, up=True, down=(0, nz)):
        for zt in range(top, h if up else top, -1):
            came = lambda zt=zt: g_in(unit, t_up, zt - 1)
            sem = lambda zt=zt: ur.at[unit * top + zt - 1]
            g_step(unit, z == h, zt, h > 0, came, sem, lambda zt=zt: us.at[unit * top + zt - 1], sem, came, to_up)
        for zt in range(down[0], min(down[1], top - h)):
            came = lambda zt=zt: g_in(unit, t_dn, zt)
            sem = lambda zt=zt: vr.at[unit * top + zt]
            g_step(unit, z == top - h, zt, h > 0, came, sem, lambda zt=zt: vs.at[unit * top + zt], sem, came, to_dn)

    def g_last(unit, acc):
        up_ref = lambda: g_in(unit, t_up, z - 1)
        dn_ref = lambda: g_in(unit, t_dn, z)
        recv(True, lambda: g_in(unit, t_dd, z), lambda: dr_.at[unit * nz + z])
        recv(has_dn, up_ref, lambda: ur.at[unit * top + z - 1])
        recv(has_up, dn_ref, lambda: vr.at[unit * top + z])
        g_add(acc, (g_own(unit, z, c), g_in(unit, t_dd, z)))
        pl.when(has_dn)(lambda: g_add(acc, (acc, up_ref())))
        pl.when(has_up)(lambda: g_add(acc, (acc, dn_ref())))

    def row_send(unit, idx):
        first, n = span(unit)
        row = 0 if unit in PIECES else SLOT[unit]
        return big.at[idx, pl.ds(row * rows, rows), pl.ds(2 * fs + (first if unit in PIECES else 0), n)]

    def g_rows(unit):
        first, n = span(unit)
        facc = fbuf.at[:, :, pl.ds(0, n)]
        g_last(unit, facc)
        u = SLOT[unit]
        for k in range(4):
            row_send(unit, k)[...] = facc[k].astype(BF)
        rbuf[d, :, cols(unit)] = facc[d].astype(BF)
        for k, (idx, tgt) in enumerate(peers):
            send(
                "rows", True,
                lambda idx=idx: row_send(unit, idx),
                lambda: rbuf.at[d, :, cols(unit)],
                lambda k=k: qs.at[u * 3 + k], lambda k=k: qr.at[u * 3 + k], tgt,
            )

    def g_rows_wait(unit):
        u = SLOT[unit]
        first, n = span(unit)
        for k, (idx, _) in enumerate(peers):
            recv(True, lambda idx=idx: rbuf.at[idx, :, cols(unit)], lambda k=k: qr.at[u * 3 + k])

    count = 4 * fs // uw

    def wide_in(i):
        ref = wg_ref if i < count else wu_ref
        return pltpu.make_async_copy(
            ref.at[:, pl.ds((i % count) * uw, uw)], mbuf.at[i // 8, pl.ds((i % 8) * rows, rows), :], ins.at[i]
        )

    def wide_read(i, first, n):
        b = i * count + first // uw
        return mbuf[b // 8, pl.ds((b % 8) * rows, rows), pl.ds(first % uw, n)]

    x_in = pltpu.make_async_copy(x_ref.at[0], xa.at[d], ins.at[2 * count])
    do_in = pltpu.make_async_copy(do_ref.at[0], oa.at[d], ins.at[2 * count + 1])
    def down_in(i):
        n = (uw, wid - uw)[i]
        return pltpu.make_async_copy(
            wdn_ref.at[:, pl.ds(i * uw, n)], mbuf.at[2, pl.ds(i * drows, drows), pl.ds(0, n)] if i == 0
            else mbuf.at[3, pl.ds(0, drows), pl.ds(0, n)], ins.at[2 * count + 2 + i]
        )

    def first_in(i):
        return pltpu.make_async_copy(
            win_ref.at[:, pl.ds(i * uw, uw)], mbuf.at[2 + i // 2, pl.ds(tok - rows * (1 + i % 2), rows), :], ins.at[2 * count + 4 + i]
        )

    for i in range(4):
        first_in(i).start()
    x_in.start()
    for i in range(2):
        down_in(i).start()
    for i in range(2 * count):
        wide_in(i).start()
    do_in.start()
    for i in range(4):
        first_in(i).wait()
    for k in range(4):
        for p in range(3):
            b, first = divmod(p * wid + k * ch, uw)
            stage[k, :, pl.ds(p * ch, ch)] = mbuf[2 + b // 2, pl.ds(tok - rows * (1 + b % 2), rows), pl.ds(first, ch)].astype(BF)
    lanes = taps_ref.shape[1]
    lane0 = lax.rem(s * rows, 128)
    gsum[...] = jnp.zeros_like(gsum)
    gsum[0:1, 0:lanes] = n1_ref[...]
    gsum[1:2, 0:lanes] = n2_ref[...]
    gsum[2:5, 0:lanes] = taps_ref[...]
    gb[d, z, c] = pltpu.roll(gsum[...], lane0, 1).astype(BF)
    wo[pl.ds(pl.multiple_of(s * rows, rows), rows), :] = wout_ref[...].astype(BF)
    for i in range(2):
        down_in(i).wait()
    wd[pl.ds(pl.multiple_of(s * drows, drows), drows), pl.ds(0, uw)] = mbuf[2, pl.ds(0, drows), :].astype(BF)
    wd[pl.ds(pl.multiple_of(s * drows, drows), drows), pl.ds(uw, wid - uw)] = mbuf[3, pl.ds(0, drows), pl.ds(0, wid - uw)].astype(BF)
    enter()
    for k, (idx, tgt) in enumerate(peers):
        send("w", True, lambda: gb.at[d, z, c], lambda: gb.at[d, z, c], lambda k=k: gs.at[k], lambda k=k: gr.at[k], tgt)
    w_slice(IN)
    x_in.wait()
    ag_start(AX, xa)
    z_own(DOWN)
    z_own(OUT)
    mid = seg_ref[:, pl.ds(pl.multiple_of(s * tok, tok), tok)]
    near[:, pl.ds(128, tok)] = mid
    near[:, pl.ds(0, 128)] = jnp.full((1, 128), -1, jnp.int32)
    near[:, pl.ds(128 + tok, 128)] = jnp.full((1, 128), -1, jnp.int32)

    @pl.when(s > 0)
    def _():
        near[:, pl.ds(0, 128)] = seg_ref[:, pl.ds(pl.multiple_of(s * tok - 128, 128), 128)]

    @pl.when(s < 2 * nz - 1)
    def _():
        near[:, pl.ds(128 + tok, 128)] = seg_ref[:, pl.ds(pl.multiple_of(s * tok + tok, 128), 128)]

    around = near[...]
    lane = lax.broadcasted_iota(jnp.int32, (128, tok), 0)
    flags = jnp.zeros((128, tok), F32)
    for k, move in enumerate((1, 2, tok + 255, tok + 254)):
        moved = pltpu.roll(around, move, 1)[:, 128 : 128 + tok]
        flags = jnp.where(lane == k, jnp.where(moved == mid, 1.0, 0.0), flags)
    fm[d] = flags[:16].astype(BF)
    for k, (idx, _) in enumerate(peers):
        recv(True, lambda idx=idx: gb.at[idx, z, c], lambda k=k: gr.at[k])
    z_own(GAIN)
    w_slice_wait(IN)
    z_own(IN)
    for i in range(2 * count):
        wide_in(i).wait()
    for k in range(4):
        for j in range(3):
            stage[k, :, pl.ds((1 + j) * uw, cj)] = wide_read(0, k * fs + j * cj, cj).astype(BF)
            stage[k, :, pl.ds((1 + j) * uw + cj, cj)] = wide_read(1, k * fs + j * cj, cj).astype(BF)
    z_fwd(OUT, 1)
    z_fwd(GAIN, 1)
    ag_fwd(AX, xa)
    for k, (idx, tgt) in enumerate(peers):
        send("ag", True, lambda: fm.at[d], lambda: fm.at[d], lambda k=k: ms.at[k], lambda k=k: mr.at[k], tgt)
    w_slice(GU0)
    z_fwd(IN, 1)
    z_fwd(GAIN, 2)
    z_fwd(OUT, 2)
    w_slice(GU1)
    w_slice(GU2)
    do_in.wait()
    ag_first(AO, oa)
    z_fwd(GAIN, 3)
    z_finish(GAIN)
    per = 128 // rows
    for g in range(wid // 128):
        tot = None
        for i in range(g * per, (g + 1) * per):
            dd, q = i // (2 * nz), i % (2 * nz)
            piece = gb[dd, q // 2, q % 2].astype(F32)
            tot = piece if tot is None else tot + piece
        gv[:, pl.ds(g * 128, 128)] = tot

    step = 64

    def norm_rows(xv):
        return lax.rsqrt(jnp.mean(xv * xv, axis=1, keepdims=True) + epsilon)

    zcol = pl.ds(0, wid)
    zstep = 64

    def make_z1(dd):
        @pl.loop(0, tok // zstep)
        def _(i):
            rr = pl.ds(pl.multiple_of(i * zstep, zstep), zstep)
            xv = xa[dd, rr, :].astype(F32)
            big[dd, rr, zcol] = (xv * norm_rows(xv) * gv[0:1, :]).astype(BF)

    make_z1(d)
    ag_near(AX, xa)
    make_z1(xn)
    make_z1(yn)
    z_fwd(IN, 2)
    z_fwd(OUT, 3)
    ag_far(AX, xa)
    make_z1(dg)
    w_slice_wait(GU0)
    z_own(GU0)
    z_fwd(IN, 3)
    z_finish(IN)
    for k, (idx, _) in enumerate(peers):
        recv(True, lambda idx=idx: fm.at[idx], lambda k=k: mr.at[k])
    for dd in range(4):
        ma[dd] = jnp.concatenate([fm[dd].astype(F32), jnp.zeros((112, tok), F32)], axis=0).T.astype(BF)

    def unit_w(lo_col, n):
        return wall[:, :, :, :, pl.ds(lo_col, n)].reshape(wid, n)

    @pl.loop(0, 4)
    def _(dd):
        m = dot_nn(big[dd, :, zcol], unit_w(0, uw))
        mbuf[dd] = m
        pbuf[dd] = (m[:, :ch] * m[:, 2 * ch :]).astype(BF)

    tail = 16
    send("halo", s < 2 * nz - 1, lambda: pbuf.at[:, pl.ds(tok - tail, tail), :], lambda: halo_p,
         lambda: hs.at[0], lambda: hr.at[0], to_next)

    @pl.when(s == 0)
    def _():
        halo_p[...] = jnp.zeros_like(halo_p)

    z_finish(OUT)
    w_slice_wait(GU1)
    z_own(GU1)
    recv(s > 0, lambda: halo_p, lambda: hr.at[0])
    tap_cols = pl.ds(pl.multiple_of(d * ch, ch), ch)
    row = lax.broadcasted_iota(jnp.int32, (tok, ch), 0)

    def past(dd):
        cur = pbuf[dd].astype(F32)
        old = halo_p[dd].astype(F32)
        masks = ma[dd].astype(F32)
        one = jnp.where(row == 0, old[tail - 1 : tail], pltpu.roll(cur, 1, 0)) * masks[:, 0:1]
        two = jnp.where(row == 0, old[tail - 2 : tail - 1], jnp.where(row == 1, old[tail - 1 : tail], pltpu.roll(cur, 2, 0)))
        return cur, one, two * masks[:, 1:2], masks

    def convolve(cur, one, two):
        return gv[2:3, tap_cols] * cur + gv[3:4, tap_cols] * one + gv[4:5, tap_cols] * two

    def conv_rows(dd):
        cur, one, two, _ = past(dd)
        ybuf[dd] = (mbuf[dd, :, pl.ds(ch, ch)] * convolve(cur, one, two)).astype(BF)

    def h_tile(dd):
        conv_rows(dd)
        return dot_nn(ybuf[dd], wo[...])

    rs_run(0, sb_a, bufs_a, h_tile, "rs0")
    hid[...] = h_tile(d)
    w_slice_wait(GU2)
    z_own(GU2)
    z_fwd(GU0, 1)
    rs_pass(0, sb_a, bufs_a, "rs0")
    ag_fwd(AO, oa)
    z_fwd(GU1, 1)
    z_fwd(GU2, 1)
    z_fwd(DOWN, 1)
    z_fwd(GU0, 2)
    rs_wait(0, bufs_a)

    def hidden_rows(first):
        @pl.loop(0, half // step)
        def _(i):
            rr = pl.ds(pl.multiple_of(first + i * step, step), step)
            h = xa[d, rr, :].astype(F32) + hid[rr, :] + rx_a[rr, :].astype(F32) + ry_a[rr, :].astype(F32)
            hid[rr, :] = h
            za[d, rr, :] = (h * norm_rows(h) * gv[1:2, :]).astype(BF)

    hidden_rows(half)
    ag_send(AZ, za, d, hi, 0, 1, to_x)
    hidden_rows(0)
    ag_send(AZ, za, d, lo, 1, 2, to_y)
    ag_second(AZ, za)

    def acol(j):
        return pl.ds(j * cj, cj)

    def gcol(j):
        return pl.ds(fs + j * uw, cj)

    def ucol(j):
        return pl.ds(fs + j * uw + cj, cj)

    def gate_one(j, dd):
        gu = dot_nn(za[dd], unit_w((1 + j) * uw, uw))
        g, u = gu[:, :cj], gu[:, cj:]
        sig = jax.nn.sigmoid(g)
        sw = g * sig
        big[dd, :, acol(j)] = (sw * u).astype(BF)
        big[dd, :, gcol(j)] = (u * sig * (1.0 + g * (1.0 - sig))).astype(BF)
        big[dd, :, ucol(j)] = sw.astype(BF)

    def gate_all(j):
        @pl.loop(0, 4)
        def _(dd):
            gate_one(j, dd)

    def back_all(j):
        @pl.loop(0, 4)
        def _(dd):
            da = dot_nt(oa[dd], wd[pl.ds(j * cj, cj), :])
            big[dd, :, gcol(j)] = (da * big[dd, :, gcol(j)].astype(F32)).astype(BF)
            big[dd, :, ucol(j)] = (da * big[dd, :, ucol(j)].astype(F32)).astype(BF)

    def grad_gu(j):
        @pl.loop(0, 4)
        def _(dd):
            left = za[:, :, pl.ds(pl.multiple_of(dd * ch, ch), ch)].reshape(4 * tok, ch)
            right = big[:, :, pl.ds(fs + j * uw, uw)].reshape(4 * tok, uw)
            res = dot_tn(left, right).astype(BF)
            gw[dd, :, :, :, pl.ds((1 + j) * uw, uw)] = res.reshape(nz, 2, rows, uw)

    def grad_down(j):
        left = big[:, :, pl.ds(j * cj, cj)].reshape(4 * tok, cj)
        gd[pl.ds(j * cj, cj), :] = dot_tn(left, oa[...].reshape(4 * tok, wid)).astype(BF)

    def dz2_tile(dd):
        return dot_nt(big[dd, :, pl.ds(fs, 3 * uw)], unit_w(uw, 3 * uw))

    def out_tile(dd):
        return dot_nn(big[dd, :, pl.ds(0, fs)], wd[...])

    z_fwd(GU1, 2)
    ag_fwd(AZ, za)
    ag_second(AO, oa)
    z_fwd(GU0, 3)
    z_fwd(GU2, 2)
    ag_near(AZ, za)
    z_finish(GU0)
    for dd in (d, xn, yn):
        gate_one(0, dd)
    z_fwd(DOWN, 2)
    z_fwd(GU1, 3)
    z_finish(GU1)
    ag_far(AZ, za)
    gate_one(0, dg)
    gate_all(1)
    z_fwd(GU2, 3)
    z_finish(GU2)
    gate_all(2)
    z_fwd(DOWN, 3)
    z_finish(DOWN)

    rs_far(2, sb_b, bufs_b, out_tile, "rs2")
    ag_near(AO, oa)
    ag_far(AO, oa)
    grad_down(0)
    g_pair(DOWN, (0,))
    grad_down(2)
    g_pair(DOWN, (3,))
    grad_down(1)
    g_pair(DOWN, (1, 2))
    g_hop(DOWN, 0)
    rs_direct(2, sb_b, bufs_b, out_tile, "rs2")
    for j in range(3):
        back_all(j)

    drain("rs0")
    rs_run(1, sb_a, bufs_a, dz2_tile, "rs1")
    grad_gu(0)
    g_pair(GU0)
    g_hop(DOWN, 1)
    dh[...] = dz2_tile(d)
    g_hop(GU0, 0)
    rs_pass(1, sb_a, bufs_a, "rs1")
    grad_gu(1)
    g_pair(GU1)
    g_hop(DOWN, 2)
    g_hop(GU1, 0)
    grad_gu(2)
    g_pair(GU2)
    rs_wait(1, bufs_a)

    def back_two(first, i):
        rr = pl.ds(pl.multiple_of(first + i * step, step), step)
        dz = dh[rr, :] + rx_a[rr, :].astype(F32) + ry_a[rr, :].astype(F32)
        h = hid[rr, :]
        inv = norm_rows(h)
        unit = h * inv
        e = dz * gv[1:2, :]
        g = oa[d, rr, :].astype(F32) + inv * (e - unit * jnp.mean(e * unit, axis=1, keepdims=True))
        dh[rr, :] = g
        ra[d, rr, :] = g.astype(BF)

    pl.loop(0, half // step)(functools.partial(back_two, half))
    ag_send(AR, ra, d, hi, 0, 1, to_x)
    pl.loop(0, half // step)(functools.partial(back_two, 0))
    ag_send(AR, ra, d, lo, 1, 2, to_y)
    ag_second(AR, ra)
    g_hop(GU2, 0, down=(0, 1))
    g_hop(GU0, 1)
    hid[...] = hid[...] + out_tile(d)
    for dd in (d, xn, yn, dg):
        make_z1(dd)
    ag_fwd(AR, ra)
    rs_pass(2, sb_b, bufs_b, "rs2")
    g_hop(GU0, 2)
    g_last(DOWN, gdown_ref)
    ag_near(AR, ra)

    mcol = fs
    zero_tap = jnp.zeros((8, ch), F32)

    def back_conv(dd, acc):
        dy = dot_nt(ra[dd], wo[...])
        cur, one, two, _ = past(dd)
        q = dy * mbuf[dd, :, pl.ds(ch, ch)]
        mbuf[dd, :, pl.ds(ch, ch)] = q
        big[dd, :, pl.ds(mcol + ch, ch)] = (dy * convolve(cur, one, two)).astype(BF)
        return tuple(a + (q * v).reshape(tok // 8, 8, ch).sum(axis=0) for a, v in zip(acc, (cur, one, two)))

    taps = (zero_tap, zero_tap, zero_tap)
    for dd in (d, xn, yn):
        taps = back_conv(dd, taps)
    g_hop(GU1, 1)
    ag_far(AR, ra)
    taps = back_conv(dg, taps)
    head = 8
    send("halo", s > 0, lambda: mbuf.at[:, pl.ds(0, head), pl.ds(ch, ch)], lambda: halo_q, lambda: hs.at[1], lambda: hr.at[1], to_prev)

    g_hop(GU2, 0, up=False, down=(1, nz))

    @pl.when(s == 2 * nz - 1)
    def _():
        halo_q[...] = jnp.zeros_like(halo_q)

    lines = lax.broadcasted_iota(jnp.int32, (rows, ch), 0)
    tap_rows = jnp.zeros((rows, ch), F32)
    for k in range(3):
        tap_rows = jnp.where(lines == k, jnp.sum(taps[k], axis=0, keepdims=True), tap_rows)
    for q in range(2 * nz):
        first = (q * rows) // 128 * 128
        go[pl.ds(q * rows, rows), pl.ds(wid, 128)] = tap_rows[:, first : first + 128].astype(BF)
    go[:, pl.ds(0, wid)] = dot_tn(ybuf[...].reshape(4 * tok, ch), ra[...].reshape(4 * tok, wid)).astype(BF)
    g_pair(OUT)
    g_hop(GU1, 2)
    recv(s < 2 * nz - 1, lambda: halo_q, lambda: hr.at[1])

    @pl.loop(0, 4)
    def _(dd):
        q = mbuf[dd, :, pl.ds(ch, ch)]
        new = halo_q[dd]
        masks = ma[dd].astype(F32)
        one = jnp.where(row == tok - 1, new[0:1], pltpu.roll(q, tok - 1, 0)) * masks[:, 2:3]
        two = jnp.where(row == tok - 2, new[0:1], jnp.where(row == tok - 1, new[1:2], pltpu.roll(q, tok - 2, 0)))
        dp = gv[2:3, tap_cols] * q + gv[3:4, tap_cols] * one + gv[4:5, tap_cols] * (two * masks[:, 3:4])
        big[dd, :, pl.ds(mcol, ch)] = (dp * mbuf[dd, :, pl.ds(2 * ch, ch)]).astype(BF)
        big[dd, :, pl.ds(mcol + 2 * ch, ch)] = (dp * mbuf[dd, :, pl.ds(0, ch)]).astype(BF)

    drain("rs1")

    def dz1_tile(dd):
        return dot_nt(big[dd, :, pl.ds(mcol, uw)], unit_w(0, uw))

    def grad_in(p):
        left = big[:, :, zcol].reshape(4 * tok, wid)
        right = big[:, :, pl.ds(mcol + p * ch, ch)].reshape(4 * tok, ch)
        gw[:, :, :, :, pl.ds(p * ch, ch)] = dot_tn(left, right).astype(BF).reshape(4, nz, 2, rows, ch)

    grad_in(0)
    g_pair(IN_A)
    rs_run(3, sb_a, bufs_a, dz1_tile, "rs3")
    g_hop(IN_A, 0)
    grad_in(1)
    g_pair(IN_B)
    grad_in(2)
    g_pair(IN_C)
    g_hop(IN_B, 0)
    g_hop(IN_C, 0)
    g_hop(OUT, 0)
    g_hop(GU2, 1)
    rs_pass(3, sb_a, bufs_a, "rs3")
    g_rows(GU0)
    g_rows(GU1)
    g_hop(GU2, 2)
    g_hop(IN_A, 1)
    rs_wait(2, bufs_b)

    @pl.loop(0, tok // step)
    def _(i):
        rr = pl.ds(pl.multiple_of(i * step, step), step)
        sb_b[d, rr, :] = (hid[rr, :] + rx_b[rr, :].astype(F32) + ry_b[rr, :].astype(F32)).astype(BF)

    result = pltpu.make_async_copy(sb_b.at[d], out_ref.at[0], ins.at[2 * count])
    result.start()
    hid[...] = dz1_tile(d)
    g_hop(IN_A, 2)
    g_hop(IN_B, 1)
    g_hop(IN_B, 2)
    g_rows(GU2)
    g_rows(IN_A)
    g_hop(IN_C, 1)
    g_hop(OUT, 1)
    g_rows(IN_B)
    g_hop(IN_C, 2)
    rs_wait(3, bufs_a)

    @pl.loop(0, tok // step)
    def _(i):
        rr = pl.ds(pl.multiple_of(i * step, step), step)
        dz = hid[rr, :] + rx_a[rr, :].astype(F32) + ry_a[rr, :].astype(F32)
        xv = xa[d, rr, :].astype(F32)
        inv = norm_rows(xv)
        unit = xv * inv
        e = dz * gv[0:1, :]
        g = dh[rr, :] + inv * (e - unit * jnp.mean(e * unit, axis=1, keepdims=True))
        sb_a[d, rr, :] = g.astype(BF)

    grads = pltpu.make_async_copy(sb_a.at[d], gtok_ref.at[0], ins.at[2 * count + 1])
    grads.start()

    g_hop(OUT, 2)
    for unit in (GU0, GU1, GU2):
        g_rows_wait(unit)

    def gain_sum(first, n):
        acc = jnp.zeros((rows, 128), F32)
        for k in range(4):
            for q in range(n // 128):
                cc = pl.ds(first + q * 128, 128)
                acc = acc + stage[k, :, cc].astype(F32) * rbuf[k, :, cc].astype(F32)
        return acc

    def gain_out(k, first, n, gain):
        total = lax.dot_general(
            jnp.ones((8, 128), F32), gain_sum(first, n), (((1,), (1,)), ((), ())),
            precision=lax.Precision.HIGHEST, preferred_element_type=F32,
        )
        gsmall_ref[k : k + 1, 0:lanes] = total[0:1] / gain[...].astype(BF).astype(F32)

    g_rows(IN_C)
    gain_out(1, uw, 3 * uw, n2_ref)
    g_last(OUT, oacc)
    gout_ref[...] = oacc[:, pl.ds(0, wid)]
    gsmall_ref[pl.ds(8, 8), :] = pltpu.roll(oacc[0:16, pl.ds(wid, 128)], lax.rem(128 - lane0, 128), 1)[:8]
    for unit in PIECES:
        g_rows_wait(unit)
    gain_out(0, 0, uw, n1_ref)
    result.wait()
    grads.wait()
    drain()


def move_out(shape, *refs):
    lanes, ch, fs, cj, uw = shape
    out_in, tok_in, tile_in, go_in, gd_in, small, out_ref, tok_ref, in_ref, go_ref, gate_ref, up_ref, gd_ref = refs[:13]
    one_ref, two_ref, taps_ref, a, b, tile, e, f, gin, gate, up, sems, done = refs[13:]
    wid = 4 * ch
    pairs = ((tile_in, tile, None), (out_in, a, out_ref), (tok_in, b, tok_ref), (gd_in, f, gd_ref), (go_in, e, go_ref))
    loads = [pltpu.make_async_copy(p[0], p[1], sems.at[k]) for k, p in enumerate(pairs)]
    for load in loads:
        load.start()
    one_ref[...] = small[0:1, 0:lanes]
    two_ref[...] = small[1:2, 0:lanes]
    taps_ref[...] = small[8:11, 0:lanes]
    stores = [pltpu.make_async_copy(p[1], p[2], done.at[k + 1]) for k, p in enumerate(pairs[1:])]
    loads[0].wait()
    for k in range(4):
        for p in range(3):
            gin[:, pl.ds(p * wid + k * ch, ch)] = tile[k, :, pl.ds(p * ch, ch)].astype(F32)
            first = (1 + p) * uw
            gate[:, pl.ds(k * fs + p * cj, cj)] = tile[k, :, pl.ds(first, cj)].astype(F32)
            up[:, pl.ds(k * fs + p * cj, cj)] = tile[k, :, pl.ds(first + cj, cj)].astype(F32)
    stores += [pltpu.make_async_copy(v, r, done.at[5 + k]) for k, (v, r) in enumerate(((gin, in_ref), (gate, gate_ref), (up, up_ref)))]
    for store in stores[4:]:
        store.start()
    for load, store in zip(loads[1:], stores):
        load.wait()
        store.start()
    for store in stores:
        store.wait()


def fast_body(n_dp, n_seq, tokens, segments, cotangent, in_weight, out_weight, gate_weight, up_weight, down_weight, norm_one, norm_two, kernel):
    tok, wid = tokens.shape[1], tokens.shape[2]
    nz = n_seq // 2
    rows = in_weight.shape[0]
    drows = down_weight.shape[0]
    ch = wid // n_dp
    fs = gate_weight.shape[1] // n_dp
    uw = 3 * ch
    cj = uw // 2
    lanes = kernel.shape[1]

    dims = (tok, wid, nz, rows, ch, fs, cj, uw, drows)
    top = nz - 1
    vm = pltpu.VMEM
    dma = lambda n: pltpu.SemaphoreType.DMA((n,))
    plane = lambda w, t=BF: vm((n_dp, tok, w), t)
    rs_set = [vm((tok, wid), BF)] * 2 + [vm((tok // 2, wid), BF)] * 2
    came = lambda n: (vm((n, n_dp, rows, 4 * uw), BF), vm((n, drows, wid), BF), vm((n, rows, wid + 128), BF))
    scratch = [
        vm((n_dp, rows, 4 * uw), BF),
        vm((n_dp, nz, 2, rows, 4 * uw), BF),
        vm((ch, wid), BF),
        vm((fs, wid), BF),
        vm((n_dp, nz, 2, 16, 128), BF),
        vm((16, wid), F32),
        plane(wid), plane(128), plane(wid), plane(wid), plane(wid),
        plane(3 * fs),
        plane(uw, F32), plane(ch), plane(ch),
        vm((n_dp, 16, ch), BF),
        vm((n_dp, 8, ch), F32),
        plane(wid), plane(wid),
        *rs_set, *rs_set,
        vm((tok, wid), F32), vm((tok, wid), F32),
        vm((n_dp, nz, 2, rows, 4 * uw), BF), vm((fs, wid), BF), vm((ch, wid + 128), BF),
        *came(nz), *came(top), *came(top),
        vm((16, 128), F32), vm((1, tok + 256), jnp.int32), vm((n_dp, 16, tok), BF), vm((rows, wid + 128), F32), vm((n_dp, rows, uw), F32),
        dma(7 * 13), dma(7 * 2 * nz), dma(12), dma(12), dma(3), dma(3), dma(3), dma(3), dma(2), dma(2),
        dma(24), dma(24), dma(24), dma(24), dma(10 * nz), dma(10 * nz),
        dma(10 * top), dma(10 * top), dma(10 * top), dma(10 * top), dma(21), dma(21), dma(8 * fs // uw + 8),
    ]
    f32 = lambda a: jax.ShapeDtypeStruct(a.shape, F32)
    vspec, anywhere = pl.BlockSpec(memory_space=vm), pl.BlockSpec(memory_space=pl.ANY)
    res = pl.pallas_call(
        functools.partial(block_kernel, dims),
        out_shape=(
            jax.ShapeDtypeStruct(tokens.shape, BF), jax.ShapeDtypeStruct(tokens.shape, BF),
            jax.ShapeDtypeStruct((n_dp, rows, 4 * uw), BF), f32(out_weight), f32(down_weight),
            jax.ShapeDtypeStruct((16, 128), F32),
        ),
        in_specs=[anywhere] * 2 + [vspec] * 4 + [anywhere, vspec] + [anywhere] * 3,
        out_specs=(anywhere,) * 2 + (vspec,) * 4,
        scratch_shapes=scratch,
        compiler_params=pltpu.CompilerParams(collective_id=0, has_side_effects=True, vmem_limit_bytes=64 * 1024 * 1024),
    )(tokens, cotangent, segments, norm_one[None], norm_two[None], kernel, in_weight, out_weight, gate_weight, up_weight, down_weight)
    final = [jax.ShapeDtypeStruct(v.shape, v.dtype) for v in res[:2]]
    final += [f32(w) for w in (in_weight, out_weight, gate_weight, up_weight, down_weight)]
    final += [jax.ShapeDtypeStruct((k, lanes), F32) for k in (1, 1, 3)]
    moved = pl.pallas_call(
        functools.partial(move_out, (lanes, ch, fs, cj, uw)),
        out_shape=tuple(final),
        in_specs=[anywhere] * 5 + [vspec],
        out_specs=(anywhere,) * 7 + (vspec,) * 3,
        scratch_shapes=[vm(v.shape, v.dtype) for v in res[:5]]
        + [vm(w.shape, F32) for w in (in_weight, gate_weight, up_weight)] + [dma(5), dma(8)],
    )(*res)
    return (*moved[:7], moved[7][0], moved[8][0], moved[9])


def gather(value, axis=0):
    return lax.all_gather(value.astype(BF), ("dp", "seq"), axis=axis, tiled=True)


def norm_back(grad_unit, unit_rows, inverse):
    return inverse * (grad_unit - unit_rows * jnp.mean(grad_unit * unit_rows, axis=1, keepdims=True))


def from_behind(value, axis, steps):
    count = lax.axis_size(axis)
    leading, last = (max(0, -steps), min(count, count - steps))
    return lax.ppermute(value, axis, [(source, source + steps) for source in range(leading, last)])


def spread(value):
    n_dp, n_seq = lax.axis_size("dp"), lax.axis_size("seq")
    shaped = value.reshape((n_dp, n_seq, value.shape[0] // (n_dp * n_seq)) + value.shape[1:]).astype(BF)
    moved = lax.all_to_all(shaped, "seq", split_axis=1, concat_axis=1, tiled=True).astype(F32)
    summed = jnp.sum(moved, axis=1).astype(BF)
    owned = lax.psum_scatter(summed, "dp", scatter_dimension=0, tiled=True).astype(F32)
    return owned.reshape(owned.shape[1:])


def plain_body(tokens, segments, cotangent, in_weight, out_weight, gate_weight, up_weight, down_weight, norm_one, norm_two, kernel):
    width, count = tokens.shape[2], tokens.shape[1]
    in_mat, out_mat, gate_mat, up_mat, down_mat = map(gather, (in_weight, out_weight, gate_weight, up_weight, down_weight))
    gain_a, gain_b = gather(norm_one).astype(F32), gather(norm_two).astype(F32)
    taps = gather(kernel, 1).astype(F32)
    filler = jnp.full((2,), -1, jnp.int32)
    near = lax.dynamic_slice_in_dim(jnp.concatenate([filler, segments[0], filler]), lax.axis_index("seq") * count, count + 4)
    mid = near[2 : count + 2]
    same = lambda first: (mid == near[first : count + first]).astype(F32)[:, None]
    resident = tokens[0].astype(F32)
    inverse_a = lax.rsqrt(jnp.mean(resident * resident, axis=1, keepdims=True) + epsilon)
    unit_a = resident * inverse_a
    normed_a = (unit_a * gain_a).astype(BF)
    mixed = dot_nn(normed_a, in_mat)
    b_part, c_part, x_part = mixed[:, :width], mixed[:, width : 2 * width], mixed[:, 2 * width :]
    conv_in = (b_part * x_part).astype(BF)
    extended = jnp.concatenate([from_behind(conv_in[count - 2 :], "seq", 1), conv_in], axis=0).astype(F32)
    current, prev_one, prev_two = extended[2:], extended[1 : count + 1] * same(1), extended[0:count] * same(0)
    convolved = taps[0] * current + taps[1] * prev_one + taps[2] * prev_two
    gated = (c_part * convolved).astype(BF)
    hidden = resident + dot_nn(gated, out_mat)
    inverse_b = lax.rsqrt(jnp.mean(hidden * hidden, axis=1, keepdims=True) + epsilon)
    unit_b = hidden * inverse_b
    normed_b = (unit_b * gain_b).astype(BF)
    gate_pre, up_pre = dot_nn(normed_b, gate_mat), dot_nn(normed_b, up_mat)
    sig = jax.nn.sigmoid(gate_pre)
    swish = gate_pre * sig
    active = (swish * up_pre).astype(BF)
    output = hidden + dot_nn(active, down_mat)
    grad_low = cotangent[0]
    grad_active = dot_nt(grad_low, down_mat)
    grad_gate_pre = (grad_active * up_pre * sig * (1.0 + gate_pre * (1.0 - sig))).astype(BF)
    grad_up_pre = (grad_active * swish).astype(BF)
    grad_normed_b = dot_nt(grad_gate_pre, gate_mat) + dot_nt(grad_up_pre, up_mat)
    grad_hidden = grad_low.astype(F32) + norm_back(grad_normed_b * gain_b, unit_b, inverse_b)
    grad_branch = grad_hidden.astype(BF)
    grad_gated = dot_nt(grad_branch, out_mat)
    grad_conv = grad_gated * c_part
    ahead = jnp.concatenate([grad_conv, from_behind(grad_conv[:2], "seq", -1)], axis=0)
    grad_conv_in = taps[0] * grad_conv + taps[1] * (ahead[1 : count + 1] * same(3)) + taps[2] * (ahead[2 : count + 2] * same(4))
    grad_taps = jnp.stack([jnp.sum(grad_conv * part, axis=0) for part in (current, prev_one, prev_two)])
    grad_mixed = jnp.concatenate([grad_conv_in * x_part, grad_gated * convolved, grad_conv_in * b_part], axis=1).astype(BF)
    grad_normed_a = dot_nt(grad_mixed, in_mat)
    grad_resident = grad_hidden + norm_back(grad_normed_a * gain_a, unit_a, inverse_a)
    return (
        output.astype(BF)[None],
        grad_resident.astype(BF)[None],
        spread(dot_tn(normed_a, grad_mixed)),
        spread(dot_tn(gated, grad_branch)),
        spread(dot_tn(normed_b, grad_gate_pre)),
        spread(dot_tn(normed_b, grad_up_pre)),
        spread(dot_tn(active, grad_low)),
        spread(jnp.sum(grad_normed_a * unit_a, axis=0)),
        spread(jnp.sum(grad_normed_b * unit_b, axis=0)),
        jnp.transpose(spread(jnp.transpose(grad_taps))),
    )


def solution(mesh):
    n_dp, n_seq = mesh.shape["dp"], mesh.shape["seq"]

    def body(*args):
        tokens, in_weight, gate_weight, down_weight = args[0], args[3], args[5], args[7]
        width = tokens.shape[2]
        unit = 3 * width // max(n_dp, 1)
        fits = (
            n_dp == 4
            and n_seq % 2 == 0
            and tokens.shape[0] == 1
            and in_weight.shape[0] % 16 == 0
            and down_weight.shape[0] % 16 == 0
            and 128 % in_weight.shape[0] == 0
            and unit % 256 == 0
            and 2 * gate_weight.shape[1] == 3 * unit * n_dp
        )
        if fits:
            return fast_body(n_dp, n_seq, *args)
        return plain_body(*args)

    return jax.shard_map(
        body,
        mesh=mesh,
        in_specs=(
            P("dp", "seq", None),
            P("dp", None),
            P("dp", "seq", None),
            P(("dp", "seq"), None),
            P(("dp", "seq"), None),
            P(("dp", "seq"), None),
            P(("dp", "seq"), None),
            P(("dp", "seq"), None),
            P(("dp", "seq")),
            P(("dp", "seq")),
            P(None, ("dp", "seq")),
        ),
        out_specs=(
            P("dp", "seq", None),
            P("dp", "seq", None),
            P(("dp", "seq"), None),
            P(("dp", "seq"), None),
            P(("dp", "seq"), None),
            P(("dp", "seq"), None),
            P(("dp", "seq"), None),
            P(("dp", "seq")),
            P(("dp", "seq")),
            P(None, ("dp", "seq")),
        ),
        check_vma=False,
    )
```

```python
import functools

import jax
import jax.numpy as jnp
from jax import lax
from jax.experimental import pallas as pl
from jax.experimental.pallas import tpu as pltpu
from jax.sharding import PartitionSpec as P

epsilon = 1e-05
MESH = pl.DeviceIdType.MESH
BF = jnp.bfloat16
F32 = jnp.float32


def dot_nn(a, b):
    return jnp.dot(a, b, preferred_element_type=F32)


def dot_nt(a, b):
    return lax.dot_general(a, b, (((1,), (1,)), ((), ())), preferred_element_type=F32)


def dot_tn(a, b):
    return lax.dot_general(a, b, (((0,), (0,)), ((), ())), preferred_element_type=F32)


def when(pred, body):
    if pred is True:
        body()
    else:
        pl.when(pred)(body)


GAIN, IN, OUT, GU0, DOWN, GU1, GU2, IN_A, IN_B, IN_C = range(10)
SLOT = {IN: 0, GU0: 1, GU1: 2, GU2: 3, IN_A: 4, IN_B: 5, IN_C: 6}
PIECES = (IN_A, IN_B, IN_C)
AX, AZ, AO, AR = range(4)


def block_kernel(
    dims,
    x_ref, do_ref, seg_in, n1_in, n2_in, taps_in, win_ref, wout_in, wg_ref, wu_ref, wdn_ref,
    out_ref, gtok_ref, rbuf, gout_ref, gdown_ref, gsmall_ref,
    stage, wall, wo, wd, gb, gv, xa, ma, za, oa, ra, big, mbuf, pbuf, ybuf, halo_p, halo_q,
    sb_a, sb_b, rx_a, ry_a, fx_a, fy_a, rx_b, ry_b, fx_b, fy_b, hid, dh,
    gw, gd, go, dd_g, dd_d, dd_o, up_g, up_d, up_o, dn_g, dn_d, dn_o,
    gsum, near, fm, oacc, fbuf, seg_ref, n1_ref, n2_ref, taps_ref, wout_ref,
    zs, zr, ws, wr, gs, gr, ms, mr, hs, hr, ags, agr, rss, rsr, ds_, dr_, us, ur, vs, vr, qs, qr, ins, sms,
):
    tok, wid, nz, rows, ch, fs, cj, uw, drows = dims
    half = tok // 2
    d = lax.axis_index("dp")
    s = lax.axis_index("seq")
    x = lax.rem(d, 2)
    y = lax.div(d, 2)
    z = lax.div(s, 2)
    c = lax.rem(s, 2)
    xn = 2 * y + (1 - x)
    yn = 2 * (1 - y) + x
    dg = 2 * (1 - y) + (1 - x)
    oc = 1 - c
    top = nz - 1
    to_x, to_y, to_g = (xn, s), (yn, s), (dg, s)
    to_sib = (d, 2 * z + oc)
    to_up, to_dn = (d, s + 2), (d, s - 2)
    to_next, to_prev = (d, s + 1), (d, s - 1)
    pending = []

    def copy(src, dst, ssem, rsem, tgt):
        return pltpu.make_async_remote_copy(
            src_ref=src(), dst_ref=dst(), send_sem=ssem(), recv_sem=rsem(), device_id=tgt, device_id_type=MESH
        )

    def send(tag, pred, src, dst, ssem, rsem, tgt):
        when(pred, lambda: copy(src, dst, ssem, rsem, tgt).start())
        pending.append((tag, pred, src, dst, ssem, rsem, tgt))

    def recv(pred, dst, rsem):
        when(pred, lambda: copy(dst, dst, rsem, rsem, to_sib).wait_recv())

    def drain(tag=None):
        keep = []
        for item in pending:
            if tag is None or item[0] == tag:
                when(item[1], lambda item=item: copy(*item[2:]).wait_send())
            else:
                keep.append(item)
        pending[:] = keep

    small_in = [
        pltpu.make_async_copy(a, b, sms.at[k])
        for k, (a, b) in enumerate(((n1_in, n1_ref), (n2_in, n2_ref), (taps_in, taps_ref), (wout_in, wout_ref), (seg_in, seg_ref)))
    ]
    for move in small_in:
        move.start()

    barrier = pltpu.get_barrier_semaphore()

    def greet(tgt):
        pl.semaphore_signal(barrier, inc=1, device_id=tgt, device_id_type=MESH)

    for tgt in (to_x, to_y, to_g, to_sib):
        greet(tgt)
    has_up, has_dn = z < top, z > 0
    pl.when(has_up)(lambda: greet(to_up))
    pl.when(has_dn)(lambda: greet(to_dn))
    cross_next = jnp.logical_and(c == 1, z < top)
    cross_prev = jnp.logical_and(c == 0, z > 0)
    pl.when(cross_next)(lambda: greet(to_next))
    pl.when(cross_prev)(lambda: greet(to_prev))
    def enter():
        ones = [jnp.where(p, 1, 0) for p in (has_up, has_dn, cross_next, cross_prev)]
        pl.semaphore_wait(barrier, 4 + ones[0] + ones[1] + ones[2] + ones[3])

    def span(unit):
        if unit in PIECES:
            return (SLOT[unit] - SLOT[IN_A]) * ch, ch
        return SLOT[unit] * uw, uw

    def cols(unit):
        return pl.ds(*span(unit))

    def w_block(unit, zz, cc):
        if unit == GAIN:
            return gb.at[:, zz, cc]
        if unit == OUT:
            return wo.at[pl.ds(pl.multiple_of((2 * zz + cc) * rows, rows), rows), :]
        if unit == DOWN:
            return wd.at[pl.ds(pl.multiple_of((2 * zz + cc) * drows, drows), drows), :]
        return wall.at[:, zz, cc, :, cols(unit)]

    def z_send(unit, pred, zz, ssem, tgt):
        blk = lambda: w_block(unit, zz, c)
        send("w", pred, blk, blk, lambda: zs.at[unit * 13 + ssem], lambda: zr.at[unit * 2 * nz + 2 * zz + c], tgt)

    def z_own(unit):
        z_send(unit, has_up, z, 0, to_up)
        z_send(unit, has_dn, z, 3, to_dn)
        z_send(unit, True, z, 6, to_sib)

    def z_fwd(unit, k):
        low, high = z - k, z + k
        has_low, has_high = z >= k, z + k <= top
        recv(has_low, lambda: w_block(unit, low, c), lambda: zr.at[unit * 2 * nz + 2 * low + c])
        if k < top:
            z_send(unit, jnp.logical_and(has_low, has_up), low, k, to_up)
        z_send(unit, has_low, low, 6 + k, to_sib)
        recv(has_high, lambda: w_block(unit, high, c), lambda: zr.at[unit * 2 * nz + 2 * high + c])
        if k < top:
            z_send(unit, jnp.logical_and(has_high, has_dn), high, 3 + k, to_dn)
        z_send(unit, has_high, high, 9 + k, to_sib)

    def z_finish(unit):
        for zz in range(nz):
            recv(True, lambda zz=zz: w_block(unit, zz, oc), lambda zz=zz: zr.at[unit * 2 * nz + 2 * zz + oc])

    peers = ((xn, to_x), (yn, to_y), (dg, to_g))

    def w_slice(unit):
        u = SLOT[unit]
        wall[d, z, c, :, cols(unit)] = stage[d, :, cols(unit)]
        for k, (idx, tgt) in enumerate(peers):
            send(
                "stage", True,
                lambda idx=idx: stage.at[idx, :, cols(unit)],
                lambda: wall.at[d, z, c, :, cols(unit)],
                lambda k=k: ws.at[u * 3 + k], lambda k=k: wr.at[u * 3 + k], tgt,
            )

    def w_slice_wait(unit):
        u = SLOT[unit]
        for k, (idx, _) in enumerate(peers):
            recv(True, lambda idx=idx: wall.at[idx, z, c, :, cols(unit)], lambda k=k: wr.at[u * 3 + k])

    lo, hi = pl.ds(0, half), pl.ds(half, half)

    def ag_send(a, buf, idx, part, k, rk, tgt):
        blk = lambda: buf.at[idx, part, :]
        send("ag", True, blk, blk, lambda: ags.at[a * 6 + k], lambda: agr.at[a * 6 + rk], tgt)

    def ag_first(a, buf):
        ag_send(a, buf, d, hi, 0, 1, to_x)
        ag_send(a, buf, d, lo, 1, 2, to_y)

    def ag_second(a, buf):
        ag_send(a, buf, d, lo, 2, 0, to_x)
        ag_send(a, buf, d, hi, 3, 3, to_y)

    def ag_start(a, buf):
        ag_first(a, buf)
        ag_second(a, buf)

    def ag_recv(a, buf, idx, part, rk):
        recv(True, lambda: buf.at[idx, part, :], lambda: agr.at[a * 6 + rk])

    def ag_fwd(a, buf):
        ag_recv(a, buf, yn, lo, 2)
        ag_send(a, buf, yn, lo, 4, 4, to_x)
        ag_recv(a, buf, xn, hi, 1)
        ag_send(a, buf, xn, hi, 5, 5, to_y)

    def ag_near(a, buf):
        ag_recv(a, buf, xn, lo, 0)
        ag_recv(a, buf, yn, hi, 3)

    def ag_far(a, buf):
        ag_recv(a, buf, dg, lo, 4)
        ag_recv(a, buf, dg, hi, 5)

    def rs_send(r, tag, src, dst, k, tgt):
        send(tag, True, src, dst, lambda: rss.at[r * 6 + k], lambda: rsr.at[r * 6 + k], tgt)

    def rs_far(r, sb, bufs, tile, tag):
        sb[dg] = tile(dg).astype(BF)
        rs_send(r, tag, lambda: sb.at[dg, lo, :], lambda: bufs[2], 0, to_x)
        rs_send(r, tag, lambda: sb.at[dg, hi, :], lambda: bufs[3], 1, to_y)

    def rs_direct(r, sb, bufs, tile, tag):
        if tile is not None:
            sb[xn] = tile(xn).astype(BF)
        rs_send(r, tag, lambda: sb.at[xn, lo, :], lambda: bufs[0].at[lo, :], 2, to_x)
        if tile is not None:
            sb[yn] = tile(yn).astype(BF)
        rs_send(r, tag, lambda: sb.at[yn, hi, :], lambda: bufs[1].at[hi, :], 3, to_y)

    def rs_run(r, sb, bufs, tile, tag):
        rs_far(r, sb, bufs, tile, tag)
        rs_direct(r, sb, bufs, tile, tag)

    def rs_pass(r, sb, bufs, tag, first=0):
        wide = pl.ds(first, wid)
        rx, ry, fx, fy = bufs
        recv(True, lambda: fx, lambda: rsr.at[r * 6 + 0])
        sb[yn, lo, wide] = (sb[yn, lo, wide].astype(F32) + fx[...].astype(F32)).astype(BF)
        rs_send(r, tag, lambda: sb.at[yn, lo, wide], lambda: ry.at[lo, :], 4, to_y)
        recv(True, lambda: fy, lambda: rsr.at[r * 6 + 1])
        sb[xn, hi, wide] = (sb[xn, hi, wide].astype(F32) + fy[...].astype(F32)).astype(BF)
        rs_send(r, tag, lambda: sb.at[xn, hi, wide], lambda: rx.at[hi, :], 5, to_x)

    def rs_wait(r, bufs):
        rx, ry, fx, fy = bufs
        recv(True, lambda: rx.at[lo, :], lambda: rsr.at[r * 6 + 2])
        recv(True, lambda: ry.at[hi, :], lambda: rsr.at[r * 6 + 3])
        recv(True, lambda: ry.at[lo, :], lambda: rsr.at[r * 6 + 4])
        recv(True, lambda: rx.at[hi, :], lambda: rsr.at[r * 6 + 5])

    bufs_a = (rx_a, ry_a, fx_a, fy_a)
    bufs_b = (rx_b, ry_b, fx_b, fy_b)

    def g_own(unit, zz, cc):
        if unit == OUT:
            return go.at[pl.ds(pl.multiple_of((2 * zz + cc) * rows, rows), rows), :]
        if unit == DOWN:
            return gd.at[pl.ds(pl.multiple_of((2 * zz + cc) * drows, drows), drows), :]
        return gw.at[:, zz, cc, :, cols(unit)]

    def g_in(unit, trio, zz):
        buf = trio[{OUT: 2, DOWN: 1}.get(unit, 0)]
        if unit in SLOT:
            return buf.at[zz, :, :, cols(unit)]
        return buf.at[zz]

    t_dd = (dd_g, dd_d, dd_o)
    t_up = (up_g, up_d, up_o)
    t_dn = (dn_g, dn_d, dn_o)

    def g_pair(unit, which=range(nz)):
        for zz in which:
            send(
                ("g", unit), True, lambda zz=zz: g_own(unit, zz, oc), lambda zz=zz: g_in(unit, t_dd, zz),
                lambda zz=zz: ds_.at[unit * nz + zz], lambda zz=zz: dr_.at[unit * nz + zz], to_sib,
            )

    def g_add(dst, parts):
        if len(dst.shape) == 3:
            for k in range(dst.shape[0]):
                dst[k] = sum(p[k].astype(F32) for p in parts).astype(dst.dtype)
        else:
            dst[...] = sum(p[...].astype(F32) for p in parts).astype(dst.dtype)

    def g_step(unit, pred, zt, come, came, csem, ssem, rsem, there, tgt):
        mine, pair = (lambda: g_own(unit, zt, c)), (lambda: g_in(unit, t_dd, zt))
        recv(pred, pair, lambda: dr_.at[unit * nz + zt])
        if come:
            recv(pred, came, csem)
            pl.when(pred)(lambda: g_add(mine(), (mine(), pair(), came())))
        else:
            pl.when(pred)(lambda: g_add(mine(), (mine(), pair())))
        send(("g", unit), pred, mine, there, ssem, rsem, tgt)

    def g_hop(unit, h, up=True, down=(0, nz)):
        for zt in range(top, h if up else top, -1):
            came = lambda zt=zt: g_in(unit, t_up, zt - 1)
            sem = lambda zt=zt: ur.at[unit * top + zt - 1]
            g_step(unit, z == h, zt, h > 0, came, sem, lambda zt=zt: us.at[unit * top + zt - 1], sem, came, to_up)
        for zt in range(down[0], min(down[1], top - h)):
            came = lambda zt=zt: g_in(unit, t_dn, zt)
            sem = lambda zt=zt: vr.at[unit * top + zt]
            g_step(unit, z == top - h, zt, h > 0, came, sem, lambda zt=zt: vs.at[unit * top + zt], sem, came, to_dn)

    def g_last(unit, acc):
        up_ref = lambda: g_in(unit, t_up, z - 1)
        dn_ref = lambda: g_in(unit, t_dn, z)
        recv(True, lambda: g_in(unit, t_dd, z), lambda: dr_.at[unit * nz + z])
        recv(has_dn, up_ref, lambda: ur.at[unit * top + z - 1])
        recv(has_up, dn_ref, lambda: vr.at[unit * top + z])
        g_add(acc, (g_own(unit, z, c), g_in(unit, t_dd, z)))
        pl.when(has_dn)(lambda: g_add(acc, (acc, up_ref())))
        pl.when(has_up)(lambda: g_add(acc, (acc, dn_ref())))

    def row_send(unit, idx):
        first, n = span(unit)
        row = 0 if unit in PIECES else SLOT[unit]
        return big.at[idx, pl.ds(row * rows, rows), pl.ds(2 * fs + (first if unit in PIECES else 0), n)]

    def g_rows(unit):
        first, n = span(unit)
        facc = fbuf.at[:, :, pl.ds(0, n)]
        g_last(unit, facc)
        u = SLOT[unit]
        for k in range(4):
            row_send(unit, k)[...] = facc[k].astype(BF)
        rbuf[d, :, cols(unit)] = facc[d].astype(BF)
        for k, (idx, tgt) in enumerate(peers):
            send(
                "rows", True,
                lambda idx=idx: row_send(unit, idx),
                lambda: rbuf.at[d, :, cols(unit)],
                lambda k=k: qs.at[u * 3 + k], lambda k=k: qr.at[u * 3 + k], tgt,
            )

    def g_rows_wait(unit):
        u = SLOT[unit]
        first, n = span(unit)
        for k, (idx, _) in enumerate(peers):
            recv(True, lambda idx=idx: rbuf.at[idx, :, cols(unit)], lambda k=k: qr.at[u * 3 + k])

    count = 4 * fs // uw

    def wide_in(i):
        ref = wg_ref if i < count else wu_ref
        return pltpu.make_async_copy(
            ref.at[:, pl.ds((i % count) * uw, uw)], mbuf.at[i // 8, pl.ds((i % 8) * rows, rows), :], ins.at[i]
        )

    def wide_read(i, first, n):
        b = i * count + first // uw
        return mbuf[b // 8, pl.ds((b % 8) * rows, rows), pl.ds(first % uw, n)]

    x_in = pltpu.make_async_copy(x_ref.at[0], xa.at[d], ins.at[2 * count])
    do_in = pltpu.make_async_copy(do_ref.at[0], oa.at[d], ins.at[2 * count + 1])
    def down_in(i):
        n = (uw, wid - uw)[i]
        return pltpu.make_async_copy(
            wdn_ref.at[:, pl.ds(i * uw, n)], mbuf.at[2, pl.ds(i * drows, drows), pl.ds(0, n)] if i == 0
            else mbuf.at[3, pl.ds(0, drows), pl.ds(0, n)], ins.at[2 * count + 2 + i]
        )

    def first_in(i):
        return pltpu.make_async_copy(
            win_ref.at[:, pl.ds(i * uw, uw)], mbuf.at[2 + i // 2, pl.ds(tok - rows * (1 + i % 2), rows), :], ins.at[2 * count + 4 + i]
        )

    for i in range(4):
        first_in(i).start()
    x_in.start()
    for i in range(2):
        down_in(i).start()
    for i in range(2 * count):
        wide_in(i).start()
    do_in.start()
    for i in range(4):
        first_in(i).wait()
    for k in range(4):
        for p in range(3):
            b, first = divmod(p * wid + k * ch, uw)
            stage[k, :, pl.ds(p * ch, ch)] = mbuf[2 + b // 2, pl.ds(tok - rows * (1 + b % 2), rows), pl.ds(first, ch)].astype(BF)
    lanes = taps_ref.shape[1]
    lane0 = lax.rem(s * rows, 128)
    for move in small_in:
        move.wait()
    gsum[...] = jnp.zeros_like(gsum)
    gsum[0:1, 0:lanes] = n1_ref[...]
    gsum[1:2, 0:lanes] = n2_ref[...]
    gsum[2:5, 0:lanes] = taps_ref[...]
    gb[d, z, c] = pltpu.roll(gsum[...], lane0, 1).astype(BF)
    wo[pl.ds(pl.multiple_of(s * rows, rows), rows), :] = wout_ref[...].astype(BF)
    for i in range(2):
        down_in(i).wait()
    wd[pl.ds(pl.multiple_of(s * drows, drows), drows), pl.ds(0, uw)] = mbuf[2, pl.ds(0, drows), :].astype(BF)
    wd[pl.ds(pl.multiple_of(s * drows, drows), drows), pl.ds(uw, wid - uw)] = mbuf[3, pl.ds(0, drows), pl.ds(0, wid - uw)].astype(BF)
    enter()
    for k, (idx, tgt) in enumerate(peers):
        send("w", True, lambda: gb.at[d, z, c], lambda: gb.at[d, z, c], lambda k=k: gs.at[k], lambda k=k: gr.at[k], tgt)
    w_slice(IN)
    x_in.wait()
    ag_start(AX, xa)
    z_own(DOWN)
    z_own(OUT)
    mid = seg_ref[:, pl.ds(pl.multiple_of(s * tok, tok), tok)]
    near[:, pl.ds(128, tok)] = mid
    near[:, pl.ds(0, 128)] = jnp.full((1, 128), -1, jnp.int32)
    near[:, pl.ds(128 + tok, 128)] = jnp.full((1, 128), -1, jnp.int32)

    @pl.when(s > 0)
    def _():
        near[:, pl.ds(0, 128)] = seg_ref[:, pl.ds(pl.multiple_of(s * tok - 128, 128), 128)]

    @pl.when(s < 2 * nz - 1)
    def _():
        near[:, pl.ds(128 + tok, 128)] = seg_ref[:, pl.ds(pl.multiple_of(s * tok + tok, 128), 128)]

    around = near[...]
    lane = lax.broadcasted_iota(jnp.int32, (128, tok), 0)
    flags = jnp.zeros((128, tok), F32)
    for k, move in enumerate((1, 2, tok + 255, tok + 254)):
        moved = pltpu.roll(around, move, 1)[:, 128 : 128 + tok]
        flags = jnp.where(lane == k, jnp.where(moved == mid, 1.0, 0.0), flags)
    fm[d] = flags[:16].astype(BF)
    for k, (idx, _) in enumerate(peers):
        recv(True, lambda idx=idx: gb.at[idx, z, c], lambda k=k: gr.at[k])
    z_own(GAIN)
    w_slice_wait(IN)
    z_own(IN)
    for i in range(2 * count):
        wide_in(i).wait()
    for k in range(4):
        for j in range(3):
            stage[k, :, pl.ds((1 + j) * uw, cj)] = wide_read(0, k * fs + j * cj, cj).astype(BF)
            stage[k, :, pl.ds((1 + j) * uw + cj, cj)] = wide_read(1, k * fs + j * cj, cj).astype(BF)
    z_fwd(OUT, 1)
    z_fwd(GAIN, 1)
    ag_fwd(AX, xa)
    for k, (idx, tgt) in enumerate(peers):
        send("ag", True, lambda: fm.at[d], lambda: fm.at[d], lambda k=k: ms.at[k], lambda k=k: mr.at[k], tgt)
    w_slice(GU0)
    z_fwd(IN, 1)
    z_fwd(GAIN, 2)
    z_fwd(OUT, 2)
    w_slice(GU1)
    w_slice(GU2)
    do_in.wait()
    ag_first(AO, oa)
    z_fwd(GAIN, 3)
    z_finish(GAIN)
    per = 128 // rows
    for g in range(wid // 128):
        tot = None
        for i in range(g * per, (g + 1) * per):
            dd, q = i // (2 * nz), i % (2 * nz)
            piece = gb[dd, q // 2, q % 2].astype(F32)
            tot = piece if tot is None else tot + piece
        gv[:, pl.ds(g * 128, 128)] = tot

    step = 64

    def norm_rows(xv):
        return lax.rsqrt(jnp.mean(xv * xv, axis=1, keepdims=True) + epsilon)

    zcol = pl.ds(0, wid)
    zstep = 64

    def make_z1(dd):
        @pl.loop(0, tok // zstep)
        def _(i):
            rr = pl.ds(pl.multiple_of(i * zstep, zstep), zstep)
            xv = xa[dd, rr, :].astype(F32)
            big[dd, rr, zcol] = (xv * norm_rows(xv) * gv[0:1, :]).astype(BF)

    make_z1(d)
    ag_near(AX, xa)
    make_z1(xn)
    make_z1(yn)
    z_fwd(IN, 2)
    z_fwd(OUT, 3)
    ag_far(AX, xa)
    make_z1(dg)
    w_slice_wait(GU0)
    z_own(GU0)
    z_fwd(IN, 3)
    z_finish(IN)
    for k, (idx, _) in enumerate(peers):
        recv(True, lambda idx=idx: fm.at[idx], lambda k=k: mr.at[k])
    for dd in range(4):
        ma[dd] = jnp.concatenate([fm[dd].astype(F32), jnp.zeros((112, tok), F32)], axis=0).T.astype(BF)

    def unit_w(lo_col, n):
        return wall[:, :, :, :, pl.ds(lo_col, n)].reshape(wid, n)

    @pl.loop(0, 4)
    def _(dd):
        m = dot_nn(big[dd, :, zcol], unit_w(0, uw))
        mbuf[dd] = m
        pbuf[dd] = (m[:, :ch] * m[:, 2 * ch :]).astype(BF)

    tail = 16
    send("halo", s < 2 * nz - 1, lambda: pbuf.at[:, pl.ds(tok - tail, tail), :], lambda: halo_p,
         lambda: hs.at[0], lambda: hr.at[0], to_next)

    @pl.when(s == 0)
    def _():
        halo_p[...] = jnp.zeros_like(halo_p)

    z_finish(OUT)
    w_slice_wait(GU1)
    z_own(GU1)
    recv(s > 0, lambda: halo_p, lambda: hr.at[0])
    tap_cols = pl.ds(pl.multiple_of(d * ch, ch), ch)
    row = lax.broadcasted_iota(jnp.int32, (tok, ch), 0)

    def past(dd):
        cur = pbuf[dd].astype(F32)
        old = halo_p[dd].astype(F32)
        masks = ma[dd].astype(F32)
        one = jnp.where(row == 0, old[tail - 1 : tail], pltpu.roll(cur, 1, 0)) * masks[:, 0:1]
        two = jnp.where(row == 0, old[tail - 2 : tail - 1], jnp.where(row == 1, old[tail - 1 : tail], pltpu.roll(cur, 2, 0)))
        return cur, one, two * masks[:, 1:2], masks

    def convolve(cur, one, two):
        return gv[2:3, tap_cols] * cur + gv[3:4, tap_cols] * one + gv[4:5, tap_cols] * two

    def conv_rows(dd):
        cur, one, two, _ = past(dd)
        ybuf[dd] = (mbuf[dd, :, pl.ds(ch, ch)] * convolve(cur, one, two)).astype(BF)

    def h_tile(dd):
        conv_rows(dd)
        return dot_nn(ybuf[dd], wo[...])

    rs_run(0, sb_a, bufs_a, h_tile, "rs0")
    hid[...] = h_tile(d)
    w_slice_wait(GU2)
    z_own(GU2)
    z_fwd(GU0, 1)
    rs_pass(0, sb_a, bufs_a, "rs0")
    ag_fwd(AO, oa)
    z_fwd(GU1, 1)
    z_fwd(GU2, 1)
    z_fwd(DOWN, 1)
    z_fwd(GU0, 2)
    rs_wait(0, bufs_a)

    def hidden_rows(first):
        @pl.loop(0, half // step)
        def _(i):
            rr = pl.ds(pl.multiple_of(first + i * step, step), step)
            h = xa[d, rr, :].astype(F32) + hid[rr, :] + rx_a[rr, :].astype(F32) + ry_a[rr, :].astype(F32)
            hid[rr, :] = h
            za[d, rr, :] = (h * norm_rows(h) * gv[1:2, :]).astype(BF)

    hidden_rows(half)
    ag_send(AZ, za, d, hi, 0, 1, to_x)
    hidden_rows(0)
    ag_send(AZ, za, d, lo, 1, 2, to_y)
    ag_second(AZ, za)

    def acol(j):
        return pl.ds(j * cj, cj)

    def gcol(j):
        return pl.ds(fs + j * uw, cj)

    def ucol(j):
        return pl.ds(fs + j * uw + cj, cj)

    def gate_one(j, dd):
        gu = dot_nn(za[dd], unit_w((1 + j) * uw, uw))
        g, u = gu[:, :cj], gu[:, cj:]
        sig = jax.nn.sigmoid(g)
        sw = g * sig
        big[dd, :, acol(j)] = (sw * u).astype(BF)
        big[dd, :, gcol(j)] = (u * sig * (1.0 + g * (1.0 - sig))).astype(BF)
        big[dd, :, ucol(j)] = sw.astype(BF)

    def gate_all(j):
        @pl.loop(0, 4)
        def _(dd):
            gate_one(j, dd)

    def back_all(j):
        @pl.loop(0, 4)
        def _(dd):
            da = dot_nt(oa[dd], wd[pl.ds(j * cj, cj), :])
            big[dd, :, gcol(j)] = (da * big[dd, :, gcol(j)].astype(F32)).astype(BF)
            big[dd, :, ucol(j)] = (da * big[dd, :, ucol(j)].astype(F32)).astype(BF)

    def grad_gu(j):
        @pl.loop(0, 4)
        def _(dd):
            left = za[:, :, pl.ds(pl.multiple_of(dd * ch, ch), ch)].reshape(4 * tok, ch)
            right = big[:, :, pl.ds(fs + j * uw, uw)].reshape(4 * tok, uw)
            res = dot_tn(left, right).astype(BF)
            gw[dd, :, :, :, pl.ds((1 + j) * uw, uw)] = res.reshape(nz, 2, rows, uw)

    def grad_down(j):
        left = big[:, :, pl.ds(j * cj, cj)].reshape(4 * tok, cj)
        gd[pl.ds(j * cj, cj), :] = dot_tn(left, oa[...].reshape(4 * tok, wid)).astype(BF)

    def dz2_tile(dd):
        return dot_nt(big[dd, :, pl.ds(fs, 3 * uw)], unit_w(uw, 3 * uw))

    def out_tile(dd):
        return dot_nn(big[dd, :, pl.ds(0, fs)], wd[...])

    z_fwd(GU1, 2)
    ag_fwd(AZ, za)
    ag_second(AO, oa)
    z_fwd(GU0, 3)
    z_fwd(GU2, 2)
    ag_near(AZ, za)
    z_finish(GU0)
    for dd in (d, xn, yn):
        gate_one(0, dd)
    z_fwd(DOWN, 2)
    z_fwd(GU1, 3)
    z_finish(GU1)
    ag_far(AZ, za)
    gate_one(0, dg)
    gate_all(1)
    z_fwd(GU2, 3)
    z_finish(GU2)
    gate_all(2)
    z_fwd(DOWN, 3)
    z_finish(DOWN)

    rs_far(2, sb_b, bufs_b, out_tile, "rs2")
    ag_near(AO, oa)
    ag_far(AO, oa)
    grad_down(0)
    g_pair(DOWN, (0,))
    grad_down(2)
    g_pair(DOWN, (3,))
    grad_down(1)
    g_pair(DOWN, (1, 2))
    g_hop(DOWN, 0)
    rs_direct(2, sb_b, bufs_b, out_tile, "rs2")
    for j in range(3):
        back_all(j)

    drain("rs0")
    rs_run(1, sb_a, bufs_a, dz2_tile, "rs1")
    grad_gu(0)
    g_pair(GU0)
    g_hop(DOWN, 1)
    dh[...] = dz2_tile(d)
    g_hop(GU0, 0)
    rs_pass(1, sb_a, bufs_a, "rs1")
    grad_gu(1)
    g_pair(GU1)
    g_hop(DOWN, 2)
    g_hop(GU1, 0)
    grad_gu(2)
    g_pair(GU2)
    rs_wait(1, bufs_a)

    def back_two(first, i):
        rr = pl.ds(pl.multiple_of(first + i * step, step), step)
        dz = dh[rr, :] + rx_a[rr, :].astype(F32) + ry_a[rr, :].astype(F32)
        h = hid[rr, :]
        inv = norm_rows(h)
        unit = h * inv
        e = dz * gv[1:2, :]
        g = oa[d, rr, :].astype(F32) + inv * (e - unit * jnp.mean(e * unit, axis=1, keepdims=True))
        dh[rr, :] = g
        ra[d, rr, :] = g.astype(BF)

    pl.loop(0, half // step)(functools.partial(back_two, half))
    ag_send(AR, ra, d, hi, 0, 1, to_x)
    pl.loop(0, half // step)(functools.partial(back_two, 0))
    ag_send(AR, ra, d, lo, 1, 2, to_y)
    ag_second(AR, ra)
    g_hop(GU2, 0, down=(0, 1))
    g_hop(GU0, 1)
    hid[...] = hid[...] + out_tile(d)
    for dd in (d, xn, yn, dg):
        make_z1(dd)
    ag_fwd(AR, ra)
    rs_pass(2, sb_b, bufs_b, "rs2")
    g_hop(GU0, 2)
    g_last(DOWN, gdown_ref)
    drain("w")
    drain("stage")
    ag_near(AR, ra)

    mcol = fs
    zero_tap = jnp.zeros((8, ch), F32)

    def back_conv(dd, acc):
        dy = dot_nt(ra[dd], wo[...])
        cur, one, two, _ = past(dd)
        q = dy * mbuf[dd, :, pl.ds(ch, ch)]
        mbuf[dd, :, pl.ds(ch, ch)] = q
        big[dd, :, pl.ds(mcol + ch, ch)] = (dy * convolve(cur, one, two)).astype(BF)
        return tuple(a + (q * v).reshape(tok // 8, 8, ch).sum(axis=0) for a, v in zip(acc, (cur, one, two)))

    taps = (zero_tap, zero_tap, zero_tap)
    for dd in (d, xn, yn):
        taps = back_conv(dd, taps)
    g_hop(GU1, 1)
    ag_far(AR, ra)
    taps = back_conv(dg, taps)
    head = 8
    send("halo", s > 0, lambda: mbuf.at[:, pl.ds(0, head), pl.ds(ch, ch)], lambda: halo_q, lambda: hs.at[1], lambda: hr.at[1], to_prev)

    g_hop(GU2, 0, up=False, down=(1, nz))

    @pl.when(s == 2 * nz - 1)
    def _():
        halo_q[...] = jnp.zeros_like(halo_q)

    lines = lax.broadcasted_iota(jnp.int32, (rows, ch), 0)
    tap_rows = jnp.zeros((rows, ch), F32)
    for k in range(3):
        tap_rows = jnp.where(lines == k, jnp.sum(taps[k], axis=0, keepdims=True), tap_rows)
    for q in range(2 * nz):
        first = (q * rows) // 128 * 128
        go[pl.ds(q * rows, rows), pl.ds(wid, 128)] = tap_rows[:, first : first + 128].astype(BF)
    go[:, pl.ds(0, wid)] = dot_tn(ybuf[...].reshape(4 * tok, ch), ra[...].reshape(4 * tok, wid)).astype(BF)
    g_pair(OUT)
    g_hop(GU1, 2)
    recv(s < 2 * nz - 1, lambda: halo_q, lambda: hr.at[1])

    @pl.loop(0, 4)
    def _(dd):
        q = mbuf[dd, :, pl.ds(ch, ch)]
        new = halo_q[dd]
        masks = ma[dd].astype(F32)
        one = jnp.where(row == tok - 1, new[0:1], pltpu.roll(q, tok - 1, 0)) * masks[:, 2:3]
        two = jnp.where(row == tok - 2, new[0:1], jnp.where(row == tok - 1, new[1:2], pltpu.roll(q, tok - 2, 0)))
        dp = gv[2:3, tap_cols] * q + gv[3:4, tap_cols] * one + gv[4:5, tap_cols] * (two * masks[:, 3:4])
        big[dd, :, pl.ds(mcol, ch)] = (dp * mbuf[dd, :, pl.ds(2 * ch, ch)]).astype(BF)
        big[dd, :, pl.ds(mcol + 2 * ch, ch)] = (dp * mbuf[dd, :, pl.ds(0, ch)]).astype(BF)

    drain("rs1")

    def dz1_tile(dd):
        return dot_nt(big[dd, :, pl.ds(mcol, uw)], unit_w(0, uw))

    def grad_in(p):
        left = big[:, :, zcol].reshape(4 * tok, wid)
        right = big[:, :, pl.ds(mcol + p * ch, ch)].reshape(4 * tok, ch)
        gw[:, :, :, :, pl.ds(p * ch, ch)] = dot_tn(left, right).astype(BF).reshape(4, nz, 2, rows, ch)

    grad_in(0)
    g_pair(IN_A)
    rs_run(3, sb_a, bufs_a, dz1_tile, "rs3")
    g_hop(IN_A, 0)
    grad_in(1)
    g_pair(IN_B)
    grad_in(2)
    g_pair(IN_C)
    g_hop(IN_B, 0)
    g_hop(IN_C, 0)
    g_hop(OUT, 0)
    g_hop(GU2, 1)
    rs_pass(3, sb_a, bufs_a, "rs3")
    g_rows(GU0)
    g_rows(GU1)
    g_hop(GU2, 2)
    g_hop(IN_A, 1)
    drain("ag")
    for unit in (DOWN, GU0):
        drain(("g", unit))
    rs_wait(2, bufs_b)

    @pl.loop(0, tok // step)
    def _(i):
        rr = pl.ds(pl.multiple_of(i * step, step), step)
        sb_b[d, rr, :] = (hid[rr, :] + rx_b[rr, :].astype(F32) + ry_b[rr, :].astype(F32)).astype(BF)

    result = pltpu.make_async_copy(sb_b.at[d], out_ref.at[0], ins.at[2 * count])
    result.start()
    hid[...] = dz1_tile(d)
    g_hop(IN_A, 2)
    g_hop(IN_B, 1)
    g_hop(IN_B, 2)
    g_rows(GU2)
    g_rows(IN_A)
    g_hop(IN_C, 1)
    g_hop(OUT, 1)
    g_rows(IN_B)
    drain("halo")
    drain("rs2")
    for unit in (GU1, GU2):
        drain(("g", unit))
    g_hop(IN_C, 2)
    rs_wait(3, bufs_a)

    @pl.loop(0, tok // step)
    def _(i):
        rr = pl.ds(pl.multiple_of(i * step, step), step)
        dz = hid[rr, :] + rx_a[rr, :].astype(F32) + ry_a[rr, :].astype(F32)
        xv = xa[d, rr, :].astype(F32)
        inv = norm_rows(xv)
        unit = xv * inv
        e = dz * gv[0:1, :]
        g = dh[rr, :] + inv * (e - unit * jnp.mean(e * unit, axis=1, keepdims=True))
        sb_a[d, rr, :] = g.astype(BF)

    grads = pltpu.make_async_copy(sb_a.at[d], gtok_ref.at[0], ins.at[2 * count + 1])
    grads.start()

    g_hop(OUT, 2)
    for unit in (GU0, GU1, GU2):
        g_rows_wait(unit)

    def gain_sum(first, n):
        acc = jnp.zeros((rows, 128), F32)
        for k in range(4):
            for q in range(n // 128):
                cc = pl.ds(first + q * 128, 128)
                acc = acc + stage[k, :, cc].astype(F32) * rbuf[k, :, cc].astype(F32)
        return acc

    def gain_out(k, first, n, gain):
        total = lax.dot_general(
            jnp.ones((8, 128), F32), gain_sum(first, n), (((1,), (1,)), ((), ())),
            precision=lax.Precision.HIGHEST, preferred_element_type=F32,
        )
        gsmall_ref[k : k + 1, 0:lanes] = total[0:1] / gain[...].astype(BF).astype(F32)

    g_rows(IN_C)
    gain_out(1, uw, 3 * uw, n2_ref)
    g_last(OUT, oacc)
    gout_ref[...] = oacc[:, pl.ds(0, wid)]
    gsmall_ref[pl.ds(8, 8), :] = pltpu.roll(oacc[0:16, pl.ds(wid, 128)], lax.rem(128 - lane0, 128), 1)[:8]
    for unit in PIECES:
        g_rows_wait(unit)
    gain_out(0, 0, uw, n1_ref)
    result.wait()
    grads.wait()
    drain()


def move_out(shape, *refs):
    lanes, ch, fs, cj, uw = shape
    out_in, tok_in, tile_in, go_in, gd_in, small, out_ref, tok_ref, in_ref, go_ref, gate_ref, up_ref, gd_ref = refs[:13]
    one_ref, two_ref, taps_ref, a, b, tile, e, f, gin, gate, up, sems, done = refs[13:]
    wid = 4 * ch
    tile_load = pltpu.make_async_copy(tile_in, tile, sems.at[0])
    tile_load.start()
    pairs = ((gd_in, f, gd_ref), (out_in, a, out_ref), (tok_in, b, tok_ref), (go_in, e, go_ref))
    loads = [pltpu.make_async_copy(p[0], p[1], sems.at[k + 1]) for k, p in enumerate(pairs)]
    stores = [pltpu.make_async_copy(p[1], p[2], done.at[k]) for k, p in enumerate(pairs)]
    for load in loads:
        load.start()
    one_ref[...] = small[0:1, 0:lanes]
    two_ref[...] = small[1:2, 0:lanes]
    taps_ref[...] = small[8:11, 0:lanes]
    tile_load.wait()
    for k in range(4):
        for p in range(3):
            first = (1 + p) * uw
            gate[:, pl.ds(k * fs + p * cj, cj)] = tile[k, :, pl.ds(first, cj)].astype(F32)
    stores.append(pltpu.make_async_copy(gate, gate_ref, done.at[4]))
    stores[-1].start()
    for load, store in zip(loads, stores):
        load.wait()
        store.start()
    for k in range(4):
        for p in range(3):
            first = (1 + p) * uw
            up[:, pl.ds(k * fs + p * cj, cj)] = tile[k, :, pl.ds(first + cj, cj)].astype(F32)
    stores.append(pltpu.make_async_copy(up, up_ref, done.at[5]))
    stores[-1].start()
    for k in range(4):
        for p in range(3):
            gin[:, pl.ds(p * wid + k * ch, ch)] = tile[k, :, pl.ds(p * ch, ch)].astype(F32)
    stores.append(pltpu.make_async_copy(gin, in_ref, done.at[6]))
    stores[-1].start()
    for store in stores:
        store.wait()


def fast_body(n_dp, n_seq, tokens, segments, cotangent, in_weight, out_weight, gate_weight, up_weight, down_weight, norm_one, norm_two, kernel):
    tok, wid = tokens.shape[1], tokens.shape[2]
    nz = n_seq // 2
    rows = in_weight.shape[0]
    drows = down_weight.shape[0]
    ch = wid // n_dp
    fs = gate_weight.shape[1] // n_dp
    uw = 3 * ch
    cj = uw // 2
    lanes = kernel.shape[1]

    dims = (tok, wid, nz, rows, ch, fs, cj, uw, drows)
    top = nz - 1
    vm = pltpu.VMEM
    dma = lambda n: pltpu.SemaphoreType.DMA((n,))
    plane = lambda w, t=BF: vm((n_dp, tok, w), t)
    rs_set = [vm((tok, wid), BF)] * 2 + [vm((tok // 2, wid), BF)] * 2
    came = lambda n: (vm((n, n_dp, rows, 4 * uw), BF), vm((n, drows, wid), BF), vm((n, rows, wid + 128), BF))
    scratch = [
        vm((n_dp, rows, 4 * uw), BF),
        vm((n_dp, nz, 2, rows, 4 * uw), BF),
        vm((ch, wid), BF),
        vm((fs, wid), BF),
        vm((n_dp, nz, 2, 16, 128), BF),
        vm((16, wid), F32),
        plane(wid), plane(128), plane(wid), plane(wid), plane(wid),
        plane(3 * fs),
        plane(uw, F32), plane(ch), plane(ch),
        vm((n_dp, 16, ch), BF),
        vm((n_dp, 8, ch), F32),
        plane(wid), plane(wid),
        *rs_set, *rs_set,
        vm((tok, wid), F32), vm((tok, wid), F32),
        vm((n_dp, nz, 2, rows, 4 * uw), BF), vm((fs, wid), BF), vm((ch, wid + 128), BF),
        *came(nz), *came(top), *came(top),
        vm((16, 128), F32), vm((1, tok + 256), jnp.int32), vm((n_dp, 16, tok), BF), vm((rows, wid + 128), F32), vm((n_dp, rows, uw), F32),
        vm(segments.shape, jnp.int32), vm((1, lanes), F32), vm((1, lanes), F32), vm(kernel.shape, F32), vm(out_weight.shape, F32),
        dma(7 * 13), dma(7 * 2 * nz), dma(12), dma(12), dma(3), dma(3), dma(3), dma(3), dma(2), dma(2),
        dma(24), dma(24), dma(24), dma(24), dma(10 * nz), dma(10 * nz),
        dma(10 * top), dma(10 * top), dma(10 * top), dma(10 * top), dma(21), dma(21), dma(8 * fs // uw + 8), dma(5),
    ]
    f32 = lambda a: jax.ShapeDtypeStruct(a.shape, F32)
    vspec, anywhere = pl.BlockSpec(memory_space=vm), pl.BlockSpec(memory_space=pl.ANY)
    res = pl.pallas_call(
        functools.partial(block_kernel, dims),
        out_shape=(
            jax.ShapeDtypeStruct(tokens.shape, BF), jax.ShapeDtypeStruct(tokens.shape, BF),
            jax.ShapeDtypeStruct((n_dp, rows, 4 * uw), BF), f32(out_weight), f32(down_weight),
            jax.ShapeDtypeStruct((16, 128), F32),
        ),
        in_specs=[anywhere] * 11,
        out_specs=(anywhere,) * 2 + (vspec,) * 4,
        scratch_shapes=scratch,
        compiler_params=pltpu.CompilerParams(collective_id=0, has_side_effects=True, vmem_limit_bytes=64 * 1024 * 1024),
    )(tokens, cotangent, segments, norm_one[None], norm_two[None], kernel, in_weight, out_weight, gate_weight, up_weight, down_weight)
    final = [jax.ShapeDtypeStruct(v.shape, v.dtype) for v in res[:2]]
    final += [f32(w) for w in (in_weight, out_weight, gate_weight, up_weight, down_weight)]
    final += [jax.ShapeDtypeStruct((k, lanes), F32) for k in (1, 1, 3)]
    moved = pl.pallas_call(
        functools.partial(move_out, (lanes, ch, fs, cj, uw)),
        out_shape=tuple(final),
        in_specs=[anywhere] * 5 + [vspec],
        out_specs=(anywhere,) * 7 + (vspec,) * 3,
        scratch_shapes=[vm(v.shape, v.dtype) for v in res[:5]]
        + [vm(w.shape, F32) for w in (in_weight, gate_weight, up_weight)] + [dma(5), dma(7)],
    )(*res)
    return (*moved[:7], moved[7][0], moved[8][0], moved[9])


def gather(value, axis=0):
    return lax.all_gather(value.astype(BF), ("dp", "seq"), axis=axis, tiled=True)


def norm_back(grad_unit, unit_rows, inverse):
    return inverse * (grad_unit - unit_rows * jnp.mean(grad_unit * unit_rows, axis=1, keepdims=True))


def from_behind(value, axis, steps):
    count = lax.axis_size(axis)
    leading, last = (max(0, -steps), min(count, count - steps))
    return lax.ppermute(value, axis, [(source, source + steps) for source in range(leading, last)])


def spread(value):
    n_dp, n_seq = lax.axis_size("dp"), lax.axis_size("seq")
    shaped = value.reshape((n_dp, n_seq, value.shape[0] // (n_dp * n_seq)) + value.shape[1:]).astype(BF)
    moved = lax.all_to_all(shaped, "seq", split_axis=1, concat_axis=1, tiled=True).astype(F32)
    summed = jnp.sum(moved, axis=1).astype(BF)
    owned = lax.psum_scatter(summed, "dp", scatter_dimension=0, tiled=True).astype(F32)
    return owned.reshape(owned.shape[1:])


def plain_body(tokens, segments, cotangent, in_weight, out_weight, gate_weight, up_weight, down_weight, norm_one, norm_two, kernel):
    width, count = tokens.shape[2], tokens.shape[1]
    in_mat, out_mat, gate_mat, up_mat, down_mat = map(gather, (in_weight, out_weight, gate_weight, up_weight, down_weight))
    gain_a, gain_b = gather(norm_one).astype(F32), gather(norm_two).astype(F32)
    taps = gather(kernel, 1).astype(F32)
    filler = jnp.full((2,), -1, jnp.int32)
    near = lax.dynamic_slice_in_dim(jnp.concatenate([filler, segments[0], filler]), lax.axis_index("seq") * count, count + 4)
    mid = near[2 : count + 2]
    same = lambda first: (mid == near[first : count + first]).astype(F32)[:, None]
    resident = tokens[0].astype(F32)
    inverse_a = lax.rsqrt(jnp.mean(resident * resident, axis=1, keepdims=True) + epsilon)
    unit_a = resident * inverse_a
    normed_a = (unit_a * gain_a).astype(BF)
    mixed = dot_nn(normed_a, in_mat)
    b_part, c_part, x_part = mixed[:, :width], mixed[:, width : 2 * width], mixed[:, 2 * width :]
    conv_in = (b_part * x_part).astype(BF)
    extended = jnp.concatenate([from_behind(conv_in[count - 2 :], "seq", 1), conv_in], axis=0).astype(F32)
    current, prev_one, prev_two = extended[2:], extended[1 : count + 1] * same(1), extended[0:count] * same(0)
    convolved = taps[0] * current + taps[1] * prev_one + taps[2] * prev_two
    gated = (c_part * convolved).astype(BF)
    hidden = resident + dot_nn(gated, out_mat)
    inverse_b = lax.rsqrt(jnp.mean(hidden * hidden, axis=1, keepdims=True) + epsilon)
    unit_b = hidden * inverse_b
    normed_b = (unit_b * gain_b).astype(BF)
    gate_pre, up_pre = dot_nn(normed_b, gate_mat), dot_nn(normed_b, up_mat)
    sig = jax.nn.sigmoid(gate_pre)
    swish = gate_pre * sig
    active = (swish * up_pre).astype(BF)
    output = hidden + dot_nn(active, down_mat)
    grad_low = cotangent[0]
    grad_active = dot_nt(grad_low, down_mat)
    grad_gate_pre = (grad_active * up_pre * sig * (1.0 + gate_pre * (1.0 - sig))).astype(BF)
    grad_up_pre = (grad_active * swish).astype(BF)
    grad_normed_b = dot_nt(grad_gate_pre, gate_mat) + dot_nt(grad_up_pre, up_mat)
    grad_hidden = grad_low.astype(F32) + norm_back(grad_normed_b * gain_b, unit_b, inverse_b)
    grad_branch = grad_hidden.astype(BF)
    grad_gated = dot_nt(grad_branch, out_mat)
    grad_conv = grad_gated * c_part
    ahead = jnp.concatenate([grad_conv, from_behind(grad_conv[:2], "seq", -1)], axis=0)
    grad_conv_in = taps[0] * grad_conv + taps[1] * (ahead[1 : count + 1] * same(3)) + taps[2] * (ahead[2 : count + 2] * same(4))
    grad_taps = jnp.stack([jnp.sum(grad_conv * part, axis=0) for part in (current, prev_one, prev_two)])
    grad_mixed = jnp.concatenate([grad_conv_in * x_part, grad_gated * convolved, grad_conv_in * b_part], axis=1).astype(BF)
    grad_normed_a = dot_nt(grad_mixed, in_mat)
    grad_resident = grad_hidden + norm_back(grad_normed_a * gain_a, unit_a, inverse_a)
    return (
        output.astype(BF)[None],
        grad_resident.astype(BF)[None],
        spread(dot_tn(normed_a, grad_mixed)),
        spread(dot_tn(gated, grad_branch)),
        spread(dot_tn(normed_b, grad_gate_pre)),
        spread(dot_tn(normed_b, grad_up_pre)),
        spread(dot_tn(active, grad_low)),
        spread(jnp.sum(grad_normed_a * unit_a, axis=0)),
        spread(jnp.sum(grad_normed_b * unit_b, axis=0)),
        jnp.transpose(spread(jnp.transpose(grad_taps))),
    )


def solution(mesh):
    n_dp, n_seq = mesh.shape["dp"], mesh.shape["seq"]

    def body(*args):
        tokens, in_weight, gate_weight, down_weight = args[0], args[3], args[5], args[7]
        width = tokens.shape[2]
        unit = 3 * width // max(n_dp, 1)
        fits = (
            n_dp == 4
            and n_seq % 2 == 0
            and tokens.shape[0] == 1
            and in_weight.shape[0] % 16 == 0
            and down_weight.shape[0] % 16 == 0
            and 128 % in_weight.shape[0] == 0
            and unit % 256 == 0
            and 2 * gate_weight.shape[1] == 3 * unit * n_dp
        )
        if fits:
            return fast_body(n_dp, n_seq, *args)
        return plain_body(*args)

    return jax.shard_map(
        body,
        mesh=mesh,
        in_specs=(
            P("dp", "seq", None),
            P("dp", None),
            P("dp", "seq", None),
            P(("dp", "seq"), None),
            P(("dp", "seq"), None),
            P(("dp", "seq"), None),
            P(("dp", "seq"), None),
            P(("dp", "seq"), None),
            P(("dp", "seq")),
            P(("dp", "seq")),
            P(None, ("dp", "seq")),
        ),
        out_specs=(
            P("dp", "seq", None),
            P("dp", "seq", None),
            P(("dp", "seq"), None),
            P(("dp", "seq"), None),
            P(("dp", "seq"), None),
            P(("dp", "seq"), None),
            P(("dp", "seq"), None),
            P(("dp", "seq")),
            P(("dp", "seq")),
            P(None, ("dp", "seq")),
        ),
        check_vma=False,
    )
```

```python
import functools

import jax
import jax.numpy as jnp
from jax import lax
from jax.experimental import pallas as pl
from jax.experimental.pallas import tpu as pltpu
from jax.sharding import PartitionSpec as P

epsilon = 1e-05
MESH = pl.DeviceIdType.MESH
BF = jnp.bfloat16
F32 = jnp.float32


def dot_nn(a, b):
    return jnp.dot(a, b, preferred_element_type=F32)


def dot_nt(a, b):
    return lax.dot_general(a, b, (((1,), (1,)), ((), ())), preferred_element_type=F32)


def dot_tn(a, b):
    return lax.dot_general(a, b, (((0,), (0,)), ((), ())), preferred_element_type=F32)


def when(pred, body):
    if pred is True:
        body()
    else:
        pl.when(pred)(body)


GAIN, IN, OUT, GU0, DOWN, GU1, GU2, IN_A, IN_B, IN_C = range(10)
SLOT = {IN: 0, GU0: 1, GU1: 2, GU2: 3, IN_A: 4, IN_B: 5, IN_C: 6}
PIECES = (IN_A, IN_B, IN_C)
AX, AZ, AO, AR = range(4)


def block_kernel(
    dims,
    x_ref, do_ref, seg_in, n1_in, n2_in, taps_in, win_ref, wout_in, wg_ref, wu_ref, wdn_ref,
    out_ref, gtok_ref, rbuf, gout_ref, gdown_ref, gsmall_ref,
    stage, wall, wo, wd, gb, gv, xa, ma, za, oa, ra, big, mbuf, pbuf, ybuf, halo_p, halo_q,
    sb_a, sb_b, rx_a, ry_a, fx_a, fy_a, rx_b, ry_b, fx_b, fy_b, hid, dh,
    gw, gd, go, dd_g, dd_d, dd_o, up_g, up_d, up_o, dn_g, dn_d, dn_o,
    gsum, near, fm, oacc, fbuf, seg_ref, n1_ref, n2_ref, taps_ref, wout_ref,
    zs, zr, ws, wr, gs, gr, ms, mr, hs, hr, ags, agr, rss, rsr, ds_, dr_, us, ur, vs, vr, qs, qr, ins, sms,
):
    tok, wid, nz, rows, ch, fs, cj, uw, drows = dims
    half = tok // 2
    d = lax.axis_index("dp")
    s = lax.axis_index("seq")
    x = lax.rem(d, 2)
    y = lax.div(d, 2)
    z = lax.div(s, 2)
    c = lax.rem(s, 2)
    xn = 2 * y + (1 - x)
    yn = 2 * (1 - y) + x
    dg = 2 * (1 - y) + (1 - x)
    oc = 1 - c
    top = nz - 1
    to_x, to_y, to_g = (xn, s), (yn, s), (dg, s)
    to_sib = (d, 2 * z + oc)
    to_up, to_dn = (d, s + 2), (d, s - 2)
    to_next, to_prev = (d, s + 1), (d, s - 1)
    pending = []

    def copy(src, dst, ssem, rsem, tgt):
        return pltpu.make_async_remote_copy(
            src_ref=src(), dst_ref=dst(), send_sem=ssem(), recv_sem=rsem(), device_id=tgt, device_id_type=MESH
        )

    def send(tag, pred, src, dst, ssem, rsem, tgt):
        when(pred, lambda: copy(src, dst, ssem, rsem, tgt).start())
        pending.append((tag, pred, src, dst, ssem, rsem, tgt))

    def recv(pred, dst, rsem):
        when(pred, lambda: copy(dst, dst, rsem, rsem, to_sib).wait_recv())

    def drain(tag=None):
        keep = []
        for item in pending:
            if tag is None or item[0] == tag:
                when(item[1], lambda item=item: copy(*item[2:]).wait_send())
            else:
                keep.append(item)
        pending[:] = keep

    small_in = [
        pltpu.make_async_copy(a, b, sms.at[k])
        for k, (a, b) in enumerate(((n1_in, n1_ref), (n2_in, n2_ref), (taps_in, taps_ref), (wout_in, wout_ref), (seg_in, seg_ref)))
    ]
    for move in small_in:
        move.start()

    barrier = pltpu.get_barrier_semaphore()

    def greet(tgt):
        pl.semaphore_signal(barrier, inc=1, device_id=tgt, device_id_type=MESH)

    for tgt in (to_x, to_y, to_g, to_sib):
        greet(tgt)
    has_up, has_dn = z < top, z > 0
    pl.when(has_up)(lambda: greet(to_up))
    pl.when(has_dn)(lambda: greet(to_dn))
    cross_next = jnp.logical_and(c == 1, z < top)
    cross_prev = jnp.logical_and(c == 0, z > 0)
    pl.when(cross_next)(lambda: greet(to_next))
    pl.when(cross_prev)(lambda: greet(to_prev))
    def enter():
        ones = [jnp.where(p, 1, 0) for p in (has_up, has_dn, cross_next, cross_prev)]
        pl.semaphore_wait(barrier, 4 + ones[0] + ones[1] + ones[2] + ones[3])

    def span(unit):
        if unit in PIECES:
            return (SLOT[unit] - SLOT[IN_A]) * ch, ch
        return SLOT[unit] * uw, uw

    def cols(unit):
        return pl.ds(*span(unit))

    def w_block(unit, zz, cc):
        if unit == GAIN:
            return gb.at[:, zz, cc]
        if unit == OUT:
            return wo.at[pl.ds(pl.multiple_of((2 * zz + cc) * rows, rows), rows), :]
        if unit == DOWN:
            return wd.at[pl.ds(pl.multiple_of((2 * zz + cc) * drows, drows), drows), :]
        return wall.at[:, zz, cc, :, cols(unit)]

    def z_send(unit, pred, zz, ssem, tgt):
        blk = lambda: w_block(unit, zz, c)
        send("w", pred, blk, blk, lambda: zs.at[unit * 13 + ssem], lambda: zr.at[unit * 2 * nz + 2 * zz + c], tgt)

    def z_own(unit):
        z_send(unit, has_up, z, 0, to_up)
        z_send(unit, has_dn, z, 3, to_dn)
        z_send(unit, True, z, 6, to_sib)

    def z_fwd(unit, k):
        low, high = z - k, z + k
        has_low, has_high = z >= k, z + k <= top
        recv(has_low, lambda: w_block(unit, low, c), lambda: zr.at[unit * 2 * nz + 2 * low + c])
        if k < top:
            z_send(unit, jnp.logical_and(has_low, has_up), low, k, to_up)
        z_send(unit, has_low, low, 6 + k, to_sib)
        recv(has_high, lambda: w_block(unit, high, c), lambda: zr.at[unit * 2 * nz + 2 * high + c])
        if k < top:
            z_send(unit, jnp.logical_and(has_high, has_dn), high, 3 + k, to_dn)
        z_send(unit, has_high, high, 9 + k, to_sib)

    def z_finish(unit):
        for zz in range(nz):
            recv(True, lambda zz=zz: w_block(unit, zz, oc), lambda zz=zz: zr.at[unit * 2 * nz + 2 * zz + oc])

    peers = ((xn, to_x), (yn, to_y), (dg, to_g))

    def w_slice(unit):
        u = SLOT[unit]
        wall[d, z, c, :, cols(unit)] = stage[d, :, cols(unit)]
        for k, (idx, tgt) in enumerate(peers):
            send(
                "stage", True,
                lambda idx=idx: stage.at[idx, :, cols(unit)],
                lambda: wall.at[d, z, c, :, cols(unit)],
                lambda k=k: ws.at[u * 3 + k], lambda k=k: wr.at[u * 3 + k], tgt,
            )

    def w_slice_wait(unit):
        u = SLOT[unit]
        for k, (idx, _) in enumerate(peers):
            recv(True, lambda idx=idx: wall.at[idx, z, c, :, cols(unit)], lambda k=k: wr.at[u * 3 + k])

    lo, hi = pl.ds(0, half), pl.ds(half, half)

    def ag_send(a, buf, idx, part, k, rk, tgt):
        blk = lambda: buf.at[idx, part, :]
        send("ag", True, blk, blk, lambda: ags.at[a * 6 + k], lambda: agr.at[a * 6 + rk], tgt)

    def ag_first(a, buf):
        ag_send(a, buf, d, hi, 0, 1, to_x)
        ag_send(a, buf, d, lo, 1, 2, to_y)

    def ag_second(a, buf):
        ag_send(a, buf, d, lo, 2, 0, to_x)
        ag_send(a, buf, d, hi, 3, 3, to_y)

    def ag_start(a, buf):
        ag_first(a, buf)
        ag_second(a, buf)

    def ag_recv(a, buf, idx, part, rk):
        recv(True, lambda: buf.at[idx, part, :], lambda: agr.at[a * 6 + rk])

    def ag_fwd(a, buf):
        ag_recv(a, buf, yn, lo, 2)
        ag_send(a, buf, yn, lo, 4, 4, to_x)
        ag_recv(a, buf, xn, hi, 1)
        ag_send(a, buf, xn, hi, 5, 5, to_y)

    def ag_near(a, buf):
        ag_recv(a, buf, xn, lo, 0)
        ag_recv(a, buf, yn, hi, 3)

    def ag_far(a, buf):
        ag_recv(a, buf, dg, lo, 4)
        ag_recv(a, buf, dg, hi, 5)

    def rs_send(r, tag, src, dst, k, tgt):
        send(tag, True, src, dst, lambda: rss.at[r * 6 + k], lambda: rsr.at[r * 6 + k], tgt)

    def rs_far(r, sb, bufs, tile, tag):
        sb[dg] = tile(dg).astype(BF)
        rs_send(r, tag, lambda: sb.at[dg, lo, :], lambda: bufs[2], 0, to_x)
        rs_send(r, tag, lambda: sb.at[dg, hi, :], lambda: bufs[3], 1, to_y)

    def rs_direct(r, sb, bufs, tile, tag):
        if tile is not None:
            sb[xn] = tile(xn).astype(BF)
        rs_send(r, tag, lambda: sb.at[xn, lo, :], lambda: bufs[0].at[lo, :], 2, to_x)
        if tile is not None:
            sb[yn] = tile(yn).astype(BF)
        rs_send(r, tag, lambda: sb.at[yn, hi, :], lambda: bufs[1].at[hi, :], 3, to_y)

    def rs_run(r, sb, bufs, tile, tag):
        rs_far(r, sb, bufs, tile, tag)
        rs_direct(r, sb, bufs, tile, tag)

    def rs_pass(r, sb, bufs, tag, first=0):
        wide = pl.ds(first, wid)
        rx, ry, fx, fy = bufs
        recv(True, lambda: fx, lambda: rsr.at[r * 6 + 0])
        sb[yn, lo, wide] = (sb[yn, lo, wide].astype(F32) + fx[...].astype(F32)).astype(BF)
        rs_send(r, tag, lambda: sb.at[yn, lo, wide], lambda: ry.at[lo, :], 4, to_y)
        recv(True, lambda: fy, lambda: rsr.at[r * 6 + 1])
        sb[xn, hi, wide] = (sb[xn, hi, wide].astype(F32) + fy[...].astype(F32)).astype(BF)
        rs_send(r, tag, lambda: sb.at[xn, hi, wide], lambda: rx.at[hi, :], 5, to_x)

    def rs_wait(r, bufs):
        rx, ry, fx, fy = bufs
        recv(True, lambda: rx.at[lo, :], lambda: rsr.at[r * 6 + 2])
        recv(True, lambda: ry.at[hi, :], lambda: rsr.at[r * 6 + 3])
        recv(True, lambda: ry.at[lo, :], lambda: rsr.at[r * 6 + 4])
        recv(True, lambda: rx.at[hi, :], lambda: rsr.at[r * 6 + 5])

    bufs_a = (rx_a, ry_a, fx_a, fy_a)
    bufs_b = (rx_b, ry_b, fx_b, fy_b)

    def g_own(unit, zz, cc):
        if unit == OUT:
            return go.at[pl.ds(pl.multiple_of((2 * zz + cc) * rows, rows), rows), :]
        if unit == DOWN:
            return gd.at[pl.ds(pl.multiple_of((2 * zz + cc) * drows, drows), drows), :]
        return gw.at[:, zz, cc, :, cols(unit)]

    def g_in(unit, trio, zz):
        buf = trio[{OUT: 2, DOWN: 1}.get(unit, 0)]
        if unit in SLOT:
            return buf.at[zz, :, :, cols(unit)]
        return buf.at[zz]

    t_dd = (dd_g, dd_d, dd_o)
    t_up = (up_g, up_d, up_o)
    t_dn = (dn_g, dn_d, dn_o)

    def g_pair(unit, which=range(nz)):
        for zz in which:
            send(
                ("g", unit), True, lambda zz=zz: g_own(unit, zz, oc), lambda zz=zz: g_in(unit, t_dd, zz),
                lambda zz=zz: ds_.at[unit * nz + zz], lambda zz=zz: dr_.at[unit * nz + zz], to_sib,
            )

    def g_add(dst, parts):
        if len(dst.shape) == 3:
            for k in range(dst.shape[0]):
                dst[k] = sum(p[k].astype(F32) for p in parts).astype(dst.dtype)
        else:
            dst[...] = sum(p[...].astype(F32) for p in parts).astype(dst.dtype)

    def g_step(unit, pred, zt, come, came, csem, ssem, rsem, there, tgt):
        mine, pair = (lambda: g_own(unit, zt, c)), (lambda: g_in(unit, t_dd, zt))
        recv(pred, pair, lambda: dr_.at[unit * nz + zt])
        if come:
            recv(pred, came, csem)
            pl.when(pred)(lambda: g_add(mine(), (mine(), pair(), came())))
        else:
            pl.when(pred)(lambda: g_add(mine(), (mine(), pair())))
        send(("g", unit), pred, mine, there, ssem, rsem, tgt)

    def g_hop(unit, h, up=True, down=(0, nz)):
        for zt in range(top, h if up else top, -1):
            came = lambda zt=zt: g_in(unit, t_up, zt - 1)
            sem = lambda zt=zt: ur.at[unit * top + zt - 1]
            g_step(unit, z == h, zt, h > 0, came, sem, lambda zt=zt: us.at[unit * top + zt - 1], sem, came, to_up)
        for zt in range(down[0], min(down[1], top - h)):
            came = lambda zt=zt: g_in(unit, t_dn, zt)
            sem = lambda zt=zt: vr.at[unit * top + zt]
            g_step(unit, z == top - h, zt, h > 0, came, sem, lambda zt=zt: vs.at[unit * top + zt], sem, came, to_dn)

    def g_last(unit, acc):
        up_ref = lambda: g_in(unit, t_up, z - 1)
        dn_ref = lambda: g_in(unit, t_dn, z)
        recv(True, lambda: g_in(unit, t_dd, z), lambda: dr_.at[unit * nz + z])
        recv(has_dn, up_ref, lambda: ur.at[unit * top + z - 1])
        recv(has_up, dn_ref, lambda: vr.at[unit * top + z])
        g_add(acc, (g_own(unit, z, c), g_in(unit, t_dd, z)))
        pl.when(has_dn)(lambda: g_add(acc, (acc, up_ref())))
        pl.when(has_up)(lambda: g_add(acc, (acc, dn_ref())))

    def row_send(unit, idx):
        first, n = span(unit)
        row = 0 if unit in PIECES else SLOT[unit]
        return big.at[idx, pl.ds(row * rows, rows), pl.ds(2 * fs + (first if unit in PIECES else 0), n)]

    def g_rows(unit):
        first, n = span(unit)
        facc = fbuf.at[:, :, pl.ds(0, n)]
        g_last(unit, facc)
        u = SLOT[unit]
        for k in range(4):
            row_send(unit, k)[...] = facc[k].astype(BF)
        rbuf[d, :, cols(unit)] = facc[d].astype(BF)
        for k, (idx, tgt) in enumerate(peers):
            send(
                "rows", True,
                lambda idx=idx: row_send(unit, idx),
                lambda: rbuf.at[d, :, cols(unit)],
                lambda k=k: qs.at[u * 3 + k], lambda k=k: qr.at[u * 3 + k], tgt,
            )

    def g_rows_wait(unit):
        u = SLOT[unit]
        first, n = span(unit)
        for k, (idx, _) in enumerate(peers):
            recv(True, lambda idx=idx: rbuf.at[idx, :, cols(unit)], lambda k=k: qr.at[u * 3 + k])

    count = 4 * fs // uw

    def wide_in(i):
        ref = wg_ref if i < count else wu_ref
        return pltpu.make_async_copy(
            ref.at[:, pl.ds((i % count) * uw, uw)], mbuf.at[i // 8, pl.ds((i % 8) * rows, rows), :], ins.at[i]
        )

    def wide_read(i, first, n):
        b = i * count + first // uw
        return mbuf[b // 8, pl.ds((b % 8) * rows, rows), pl.ds(first % uw, n)]

    x_in = pltpu.make_async_copy(x_ref.at[0], xa.at[d], ins.at[2 * count])
    do_in = pltpu.make_async_copy(do_ref.at[0], oa.at[d], ins.at[2 * count + 1])
    def down_in(i):
        n = (uw, wid - uw)[i]
        return pltpu.make_async_copy(
            wdn_ref.at[:, pl.ds(i * uw, n)], mbuf.at[2, pl.ds(i * drows, drows), pl.ds(0, n)] if i == 0
            else mbuf.at[3, pl.ds(0, drows), pl.ds(0, n)], ins.at[2 * count + 2 + i]
        )

    def first_in(i):
        return pltpu.make_async_copy(
            win_ref.at[:, pl.ds(i * uw, uw)], mbuf.at[2 + i // 2, pl.ds(tok - rows * (1 + i % 2), rows), :], ins.at[2 * count + 4 + i]
        )

    for i in range(4):
        first_in(i).start()
    x_in.start()
    for i in range(2):
        down_in(i).start()
    for i in range(2 * count):
        wide_in(i).start()
    do_in.start()
    for i in range(4):
        first_in(i).wait()
    for k in range(4):
        for p in range(3):
            b, first = divmod(p * wid + k * ch, uw)
            stage[k, :, pl.ds(p * ch, ch)] = mbuf[2 + b // 2, pl.ds(tok - rows * (1 + b % 2), rows), pl.ds(first, ch)].astype(BF)
    lanes = taps_ref.shape[1]
    lane0 = lax.rem(s * rows, 128)
    for move in small_in:
        move.wait()
    gsum[...] = jnp.zeros_like(gsum)
    gsum[0:1, 0:lanes] = n1_ref[...]
    gsum[1:2, 0:lanes] = n2_ref[...]
    gsum[2:5, 0:lanes] = taps_ref[...]
    gb[d, z, c] = pltpu.roll(gsum[...], lane0, 1).astype(BF)
    wo[pl.ds(pl.multiple_of(s * rows, rows), rows), :] = wout_ref[...].astype(BF)
    for i in range(2):
        down_in(i).wait()
    wd[pl.ds(pl.multiple_of(s * drows, drows), drows), pl.ds(0, uw)] = mbuf[2, pl.ds(0, drows), :].astype(BF)
    wd[pl.ds(pl.multiple_of(s * drows, drows), drows), pl.ds(uw, wid - uw)] = mbuf[3, pl.ds(0, drows), pl.ds(0, wid - uw)].astype(BF)
    enter()
    for k, (idx, tgt) in enumerate(peers):
        send("w", True, lambda: gb.at[d, z, c], lambda: gb.at[d, z, c], lambda k=k: gs.at[k], lambda k=k: gr.at[k], tgt)
    w_slice(IN)
    x_in.wait()
    ag_start(AX, xa)
    z_own(DOWN)
    z_own(OUT)
    mid = seg_ref[:, pl.ds(pl.multiple_of(s * tok, tok), tok)]
    near[:, pl.ds(128, tok)] = mid
    near[:, pl.ds(0, 128)] = jnp.full((1, 128), -1, jnp.int32)
    near[:, pl.ds(128 + tok, 128)] = jnp.full((1, 128), -1, jnp.int32)

    @pl.when(s > 0)
    def _():
        near[:, pl.ds(0, 128)] = seg_ref[:, pl.ds(pl.multiple_of(s * tok - 128, 128), 128)]

    @pl.when(s < 2 * nz - 1)
    def _():
        near[:, pl.ds(128 + tok, 128)] = seg_ref[:, pl.ds(pl.multiple_of(s * tok + tok, 128), 128)]

    around = near[...]
    lane = lax.broadcasted_iota(jnp.int32, (128, tok), 0)
    flags = jnp.zeros((128, tok), F32)
    for k, move in enumerate((1, 2, tok + 255, tok + 254)):
        moved = pltpu.roll(around, move, 1)[:, 128 : 128 + tok]
        flags = jnp.where(lane == k, jnp.where(moved == mid, 1.0, 0.0), flags)
    fm[d] = flags[:16].astype(BF)
    for k, (idx, _) in enumerate(peers):
        recv(True, lambda idx=idx: gb.at[idx, z, c], lambda k=k: gr.at[k])
    z_own(GAIN)
    w_slice_wait(IN)
    z_own(IN)
    for i in range(2 * count):
        wide_in(i).wait()
    for k in range(4):
        for j in range(3):
            stage[k, :, pl.ds((1 + j) * uw, cj)] = wide_read(0, k * fs + j * cj, cj).astype(BF)
            stage[k, :, pl.ds((1 + j) * uw + cj, cj)] = wide_read(1, k * fs + j * cj, cj).astype(BF)
    z_fwd(OUT, 1)
    z_fwd(GAIN, 1)
    ag_fwd(AX, xa)
    for k, (idx, tgt) in enumerate(peers):
        send("ag", True, lambda: fm.at[d], lambda: fm.at[d], lambda k=k: ms.at[k], lambda k=k: mr.at[k], tgt)
    w_slice(GU0)
    z_fwd(IN, 1)
    z_fwd(GAIN, 2)
    z_fwd(OUT, 2)
    w_slice(GU1)
    w_slice(GU2)
    do_in.wait()
    ag_first(AO, oa)
    z_fwd(GAIN, 3)
    z_finish(GAIN)
    per = 128 // rows
    for g in range(wid // 128):
        tot = None
        for i in range(g * per, (g + 1) * per):
            dd, q = i // (2 * nz), i % (2 * nz)
            piece = gb[dd, q // 2, q % 2].astype(F32)
            tot = piece if tot is None else tot + piece
        gv[:, pl.ds(g * 128, 128)] = tot

    step = 128

    def norm_rows(xv):
        return lax.rsqrt(jnp.mean(xv * xv, axis=1, keepdims=True) + epsilon)

    zcol = pl.ds(0, wid)
    zstep = 128

    def make_z1(dd):
        @pl.loop(0, tok // zstep)
        def _(i):
            rr = pl.ds(pl.multiple_of(i * zstep, zstep), zstep)
            xv = xa[dd, rr, :].astype(F32)
            big[dd, rr, zcol] = (xv * norm_rows(xv) * gv[0:1, :]).astype(BF)

    make_z1(d)
    ag_near(AX, xa)
    make_z1(xn)
    make_z1(yn)
    z_fwd(IN, 2)
    z_fwd(OUT, 3)
    ag_far(AX, xa)
    make_z1(dg)
    w_slice_wait(GU0)
    z_own(GU0)
    z_fwd(IN, 3)
    z_finish(IN)
    for k, (idx, _) in enumerate(peers):
        recv(True, lambda idx=idx: fm.at[idx], lambda k=k: mr.at[k])
    for dd in range(4):
        ma[dd] = jnp.concatenate([fm[dd].astype(F32), jnp.zeros((112, tok), F32)], axis=0).T.astype(BF)

    def unit_w(lo_col, n):
        return wall[:, :, :, :, pl.ds(lo_col, n)].reshape(wid, n)

    @pl.loop(0, 4)
    def _(dd):
        m = dot_nn(big[dd, :, zcol], unit_w(0, uw))
        mbuf[dd] = m
        pbuf[dd] = (m[:, :ch] * m[:, 2 * ch :]).astype(BF)

    tail = 16
    send("halo", s < 2 * nz - 1, lambda: pbuf.at[:, pl.ds(tok - tail, tail), :], lambda: halo_p,
         lambda: hs.at[0], lambda: hr.at[0], to_next)

    @pl.when(s == 0)
    def _():
        halo_p[...] = jnp.zeros_like(halo_p)

    z_finish(OUT)
    w_slice_wait(GU1)
    z_own(GU1)
    recv(s > 0, lambda: halo_p, lambda: hr.at[0])
    tap_cols = pl.ds(pl.multiple_of(d * ch, ch), ch)
    row = lax.broadcasted_iota(jnp.int32, (tok, ch), 0)

    def past(dd):
        cur = pbuf[dd].astype(F32)
        old = halo_p[dd].astype(F32)
        masks = ma[dd].astype(F32)
        one = jnp.where(row == 0, old[tail - 1 : tail], pltpu.roll(cur, 1, 0)) * masks[:, 0:1]
        two = jnp.where(row == 0, old[tail - 2 : tail - 1], jnp.where(row == 1, old[tail - 1 : tail], pltpu.roll(cur, 2, 0)))
        return cur, one, two * masks[:, 1:2], masks

    def convolve(cur, one, two):
        return gv[2:3, tap_cols] * cur + gv[3:4, tap_cols] * one + gv[4:5, tap_cols] * two

    def conv_rows(dd):
        cur, one, two, _ = past(dd)
        ybuf[dd] = (mbuf[dd, :, pl.ds(ch, ch)] * convolve(cur, one, two)).astype(BF)

    def h_tile(dd):
        conv_rows(dd)
        return dot_nn(ybuf[dd], wo[...])

    rs_run(0, sb_a, bufs_a, h_tile, "rs0")
    hid[...] = h_tile(d)
    w_slice_wait(GU2)
    z_own(GU2)
    z_fwd(GU0, 1)
    rs_pass(0, sb_a, bufs_a, "rs0")
    ag_fwd(AO, oa)
    z_fwd(GU1, 1)
    z_fwd(GU2, 1)
    z_fwd(DOWN, 1)
    z_fwd(GU0, 2)
    rs_wait(0, bufs_a)

    def hidden_rows(first):
        @pl.loop(0, half // step)
        def _(i):
            rr = pl.ds(pl.multiple_of(first + i * step, step), step)
            h = xa[d, rr, :].astype(F32) + hid[rr, :] + rx_a[rr, :].astype(F32) + ry_a[rr, :].astype(F32)
            hid[rr, :] = h
            za[d, rr, :] = (h * norm_rows(h) * gv[1:2, :]).astype(BF)

    hidden_rows(half)
    ag_send(AZ, za, d, hi, 0, 1, to_x)
    hidden_rows(0)
    ag_send(AZ, za, d, lo, 1, 2, to_y)
    ag_second(AZ, za)

    def acol(j):
        return pl.ds(j * cj, cj)

    def gcol(j):
        return pl.ds(fs + j * uw, cj)

    def ucol(j):
        return pl.ds(fs + j * uw + cj, cj)

    def gate_one(j, dd):
        gu = dot_nn(za[dd], unit_w((1 + j) * uw, uw))
        g, u = gu[:, :cj], gu[:, cj:]
        sig = jax.nn.sigmoid(g)
        sw = g * sig
        big[dd, :, acol(j)] = (sw * u).astype(BF)
        big[dd, :, gcol(j)] = (u * sig * (1.0 + g * (1.0 - sig))).astype(BF)
        big[dd, :, ucol(j)] = sw.astype(BF)

    def gate_all(j):
        @pl.loop(0, 4)
        def _(dd):
            gate_one(j, dd)

    def back_all(j):
        @pl.loop(0, 4)
        def _(dd):
            da = dot_nt(oa[dd], wd[pl.ds(j * cj, cj), :])
            big[dd, :, gcol(j)] = (da * big[dd, :, gcol(j)].astype(F32)).astype(BF)
            big[dd, :, ucol(j)] = (da * big[dd, :, ucol(j)].astype(F32)).astype(BF)

    def grad_gu(j):
        @pl.loop(0, 4)
        def _(dd):
            left = za[:, :, pl.ds(pl.multiple_of(dd * ch, ch), ch)].reshape(4 * tok, ch)
            right = big[:, :, pl.ds(fs + j * uw, uw)].reshape(4 * tok, uw)
            res = dot_tn(left, right).astype(BF)
            gw[dd, :, :, :, pl.ds((1 + j) * uw, uw)] = res.reshape(nz, 2, rows, uw)

    def grad_down(j):
        left = big[:, :, pl.ds(j * cj, cj)].reshape(4 * tok, cj)
        gd[pl.ds(j * cj, cj), :] = dot_tn(left, oa[...].reshape(4 * tok, wid)).astype(BF)

    def dz2_tile(dd):
        return dot_nt(big[dd, :, pl.ds(fs, 3 * uw)], unit_w(uw, 3 * uw))

    def out_tile(dd):
        return dot_nn(big[dd, :, pl.ds(0, fs)], wd[...])

    z_fwd(GU1, 2)
    ag_fwd(AZ, za)
    ag_second(AO, oa)
    z_fwd(GU0, 3)
    z_fwd(GU2, 2)
    ag_near(AZ, za)
    z_finish(GU0)
    for dd in (d, xn, yn):
        gate_one(0, dd)
    z_fwd(DOWN, 2)
    z_fwd(GU1, 3)
    z_finish(GU1)
    ag_far(AZ, za)
    gate_one(0, dg)
    gate_all(1)
    z_fwd(GU2, 3)
    z_finish(GU2)
    gate_all(2)
    z_fwd(DOWN, 3)
    z_finish(DOWN)

    rs_far(2, sb_b, bufs_b, out_tile, "rs2")
    ag_near(AO, oa)
    ag_far(AO, oa)
    grad_down(0)
    g_pair(DOWN, (0,))
    grad_down(2)
    g_pair(DOWN, (3,))
    grad_down(1)
    g_pair(DOWN, (1, 2))
    g_hop(DOWN, 0)
    rs_direct(2, sb_b, bufs_b, out_tile, "rs2")
    for j in range(3):
        back_all(j)

    drain("rs0")
    rs_run(1, sb_a, bufs_a, dz2_tile, "rs1")
    grad_gu(0)
    g_pair(GU0)
    g_hop(DOWN, 1)
    dh[...] = dz2_tile(d)
    g_hop(GU0, 0)
    rs_pass(1, sb_a, bufs_a, "rs1")
    grad_gu(1)
    g_pair(GU1)
    g_hop(DOWN, 2)
    g_hop(GU1, 0)
    grad_gu(2)
    g_pair(GU2)
    rs_wait(1, bufs_a)

    def back_two(first, i):
        rr = pl.ds(pl.multiple_of(first + i * step, step), step)
        dz = dh[rr, :] + rx_a[rr, :].astype(F32) + ry_a[rr, :].astype(F32)
        h = hid[rr, :]
        inv = norm_rows(h)
        unit = h * inv
        e = dz * gv[1:2, :]
        g = oa[d, rr, :].astype(F32) + inv * (e - unit * jnp.mean(e * unit, axis=1, keepdims=True))
        dh[rr, :] = g
        ra[d, rr, :] = g.astype(BF)

    pl.loop(0, half // step)(functools.partial(back_two, half))
    ag_send(AR, ra, d, hi, 0, 1, to_x)
    pl.loop(0, half // step)(functools.partial(back_two, 0))
    ag_send(AR, ra, d, lo, 1, 2, to_y)
    ag_second(AR, ra)
    g_hop(GU2, 0, down=(0, 1))
    g_hop(GU0, 1)
    hid[...] = hid[...] + out_tile(d)
    for dd in (d, xn, yn, dg):
        make_z1(dd)
    ag_fwd(AR, ra)
    rs_pass(2, sb_b, bufs_b, "rs2")
    g_hop(GU0, 2)
    g_last(DOWN, gdown_ref)
    drain("w")
    drain("stage")
    ag_near(AR, ra)

    mcol = fs
    zero_tap = jnp.zeros((8, ch), F32)

    def back_conv(dd, acc):
        dy = dot_nt(ra[dd], wo[...])
        cur, one, two, _ = past(dd)
        q = dy * mbuf[dd, :, pl.ds(ch, ch)]
        mbuf[dd, :, pl.ds(ch, ch)] = q
        big[dd, :, pl.ds(mcol + ch, ch)] = (dy * convolve(cur, one, two)).astype(BF)
        return tuple(a + (q * v).reshape(tok // 8, 8, ch).sum(axis=0) for a, v in zip(acc, (cur, one, two)))

    taps = (zero_tap, zero_tap, zero_tap)
    for dd in (d, xn, yn):
        taps = back_conv(dd, taps)
    g_hop(GU1, 1)
    ag_far(AR, ra)
    taps = back_conv(dg, taps)
    head = 8
    send("halo", s > 0, lambda: mbuf.at[:, pl.ds(0, head), pl.ds(ch, ch)], lambda: halo_q, lambda: hs.at[1], lambda: hr.at[1], to_prev)

    g_hop(GU2, 0, up=False, down=(1, nz))

    @pl.when(s == 2 * nz - 1)
    def _():
        halo_q[...] = jnp.zeros_like(halo_q)

    lines = lax.broadcasted_iota(jnp.int32, (rows, ch), 0)
    tap_rows = jnp.zeros((rows, ch), F32)
    for k in range(3):
        tap_rows = jnp.where(lines == k, jnp.sum(taps[k], axis=0, keepdims=True), tap_rows)
    for q in range(2 * nz):
        first = (q * rows) // 128 * 128
        go[pl.ds(q * rows, rows), pl.ds(wid, 128)] = tap_rows[:, first : first + 128].astype(BF)
    go[:, pl.ds(0, wid)] = dot_tn(ybuf[...].reshape(4 * tok, ch), ra[...].reshape(4 * tok, wid)).astype(BF)
    g_pair(OUT)
    g_hop(GU1, 2)
    recv(s < 2 * nz - 1, lambda: halo_q, lambda: hr.at[1])

    @pl.loop(0, 4)
    def _(dd):
        q = mbuf[dd, :, pl.ds(ch, ch)]
        new = halo_q[dd]
        masks = ma[dd].astype(F32)
        one = jnp.where(row == tok - 1, new[0:1], pltpu.roll(q, tok - 1, 0)) * masks[:, 2:3]
        two = jnp.where(row == tok - 2, new[0:1], jnp.where(row == tok - 1, new[1:2], pltpu.roll(q, tok - 2, 0)))
        dp = gv[2:3, tap_cols] * q + gv[3:4, tap_cols] * one + gv[4:5, tap_cols] * (two * masks[:, 3:4])
        big[dd, :, pl.ds(mcol, ch)] = (dp * mbuf[dd, :, pl.ds(2 * ch, ch)]).astype(BF)
        big[dd, :, pl.ds(mcol + 2 * ch, ch)] = (dp * mbuf[dd, :, pl.ds(0, ch)]).astype(BF)

    drain("rs1")

    def dz1_tile(dd):
        return dot_nt(big[dd, :, pl.ds(mcol, uw)], unit_w(0, uw))

    def grad_in(p):
        left = big[:, :, zcol].reshape(4 * tok, wid)
        right = big[:, :, pl.ds(mcol + p * ch, ch)].reshape(4 * tok, ch)
        gw[:, :, :, :, pl.ds(p * ch, ch)] = dot_tn(left, right).astype(BF).reshape(4, nz, 2, rows, ch)

    grad_in(0)
    g_pair(IN_A)
    rs_run(3, sb_a, bufs_a, dz1_tile, "rs3")
    g_hop(IN_A, 0)
    grad_in(1)
    g_pair(IN_B)
    grad_in(2)
    g_pair(IN_C)
    g_hop(IN_B, 0)
    g_hop(IN_C, 0)
    g_hop(OUT, 0)
    g_hop(GU2, 1)
    rs_pass(3, sb_a, bufs_a, "rs3")
    g_rows(GU0)
    g_rows(GU1)
    g_hop(GU2, 2)
    g_hop(IN_A, 1)
    drain("ag")
    for unit in (DOWN, GU0):
        drain(("g", unit))
    rs_wait(2, bufs_b)

    @pl.loop(0, tok // step)
    def _(i):
        rr = pl.ds(pl.multiple_of(i * step, step), step)
        sb_b[d, rr, :] = (hid[rr, :] + rx_b[rr, :].astype(F32) + ry_b[rr, :].astype(F32)).astype(BF)

    result = pltpu.make_async_copy(sb_b.at[d], out_ref.at[0], ins.at[2 * count])
    result.start()
    hid[...] = dz1_tile(d)
    g_hop(IN_A, 2)
    g_hop(IN_B, 1)
    g_hop(IN_B, 2)
    g_rows(GU2)
    g_rows(IN_A)
    g_hop(IN_C, 1)
    g_hop(OUT, 1)
    g_rows(IN_B)
    drain("halo")
    drain("rs2")
    for unit in (GU1, GU2):
        drain(("g", unit))
    g_hop(IN_C, 2)
    rs_wait(3, bufs_a)

    @pl.loop(0, tok // step)
    def _(i):
        rr = pl.ds(pl.multiple_of(i * step, step), step)
        dz = hid[rr, :] + rx_a[rr, :].astype(F32) + ry_a[rr, :].astype(F32)
        xv = xa[d, rr, :].astype(F32)
        inv = norm_rows(xv)
        unit = xv * inv
        e = dz * gv[0:1, :]
        g = dh[rr, :] + inv * (e - unit * jnp.mean(e * unit, axis=1, keepdims=True))
        sb_a[d, rr, :] = g.astype(BF)

    grads = pltpu.make_async_copy(sb_a.at[d], gtok_ref.at[0], ins.at[2 * count + 1])
    grads.start()

    g_hop(OUT, 2)
    for unit in (GU0, GU1, GU2):
        g_rows_wait(unit)

    def gain_sum(first, n):
        acc = jnp.zeros((rows, 128), F32)
        for k in range(4):
            for q in range(n // 128):
                cc = pl.ds(first + q * 128, 128)
                acc = acc + stage[k, :, cc].astype(F32) * rbuf[k, :, cc].astype(F32)
        return acc

    def gain_out(k, first, n, gain):
        total = lax.dot_general(
            jnp.ones((8, 128), F32), gain_sum(first, n), (((1,), (1,)), ((), ())),
            precision=lax.Precision.HIGHEST, preferred_element_type=F32,
        )
        gsmall_ref[k : k + 1, 0:lanes] = total[0:1] / gain[...].astype(BF).astype(F32)

    g_rows(IN_C)
    gain_out(1, uw, 3 * uw, n2_ref)
    g_last(OUT, oacc)
    gout_ref[...] = oacc[:, pl.ds(0, wid)]
    gsmall_ref[pl.ds(8, 8), :] = pltpu.roll(oacc[0:16, pl.ds(wid, 128)], lax.rem(128 - lane0, 128), 1)[:8]
    for unit in PIECES:
        g_rows_wait(unit)
    gain_out(0, 0, uw, n1_ref)
    result.wait()
    grads.wait()
    drain()


def move_out(shape, *refs):
    lanes, ch, fs, cj, uw = shape
    out_in, tok_in, tile_in, go_in, gd_in, small, out_ref, tok_ref, in_ref, go_ref, gate_ref, up_ref, gd_ref = refs[:13]
    one_ref, two_ref, taps_ref, a, b, tile, e, f, gin, gate, up, sems, done = refs[13:]
    wid = 4 * ch
    tile_load = pltpu.make_async_copy(tile_in, tile, sems.at[0])
    tile_load.start()
    pairs = ((gd_in, f, gd_ref), (out_in, a, out_ref), (tok_in, b, tok_ref), (go_in, e, go_ref))
    loads = [pltpu.make_async_copy(p[0], p[1], sems.at[k + 1]) for k, p in enumerate(pairs)]
    stores = [pltpu.make_async_copy(p[1], p[2], done.at[k]) for k, p in enumerate(pairs)]
    for load in loads:
        load.start()
    one_ref[...] = small[0:1, 0:lanes]
    two_ref[...] = small[1:2, 0:lanes]
    taps_ref[...] = small[8:11, 0:lanes]
    tile_load.wait()
    for k in range(4):
        for p in range(3):
            first = (1 + p) * uw
            gate[:, pl.ds(k * fs + p * cj, cj)] = tile[k, :, pl.ds(first, cj)].astype(F32)
    stores.append(pltpu.make_async_copy(gate, gate_ref, done.at[4]))
    stores[-1].start()
    for load, store in zip(loads, stores):
        load.wait()
        store.start()
    for k in range(4):
        for p in range(3):
            first = (1 + p) * uw
            up[:, pl.ds(k * fs + p * cj, cj)] = tile[k, :, pl.ds(first + cj, cj)].astype(F32)
    stores.append(pltpu.make_async_copy(up, up_ref, done.at[5]))
    stores[-1].start()
    for k in range(4):
        for p in range(3):
            gin[:, pl.ds(p * wid + k * ch, ch)] = tile[k, :, pl.ds(p * ch, ch)].astype(F32)
    stores.append(pltpu.make_async_copy(gin, in_ref, done.at[6]))
    stores[-1].start()
    for store in stores:
        store.wait()


def fast_body(n_dp, n_seq, tokens, segments, cotangent, in_weight, out_weight, gate_weight, up_weight, down_weight, norm_one, norm_two, kernel):
    tok, wid = tokens.shape[1], tokens.shape[2]
    nz = n_seq // 2
    rows = in_weight.shape[0]
    drows = down_weight.shape[0]
    ch = wid // n_dp
    fs = gate_weight.shape[1] // n_dp
    uw = 3 * ch
    cj = uw // 2
    lanes = kernel.shape[1]

    dims = (tok, wid, nz, rows, ch, fs, cj, uw, drows)
    top = nz - 1
    vm = pltpu.VMEM
    dma = lambda n: pltpu.SemaphoreType.DMA((n,))
    plane = lambda w, t=BF: vm((n_dp, tok, w), t)
    rs_set = [vm((tok, wid), BF)] * 2 + [vm((tok // 2, wid), BF)] * 2
    came = lambda n: (vm((n, n_dp, rows, 4 * uw), BF), vm((n, drows, wid), BF), vm((n, rows, wid + 128), BF))
    scratch = [
        vm((n_dp, rows, 4 * uw), BF),
        vm((n_dp, nz, 2, rows, 4 * uw), BF),
        vm((ch, wid), BF),
        vm((fs, wid), BF),
        vm((n_dp, nz, 2, 16, 128), BF),
        vm((16, wid), F32),
        plane(wid), plane(128), plane(wid), plane(wid), plane(wid),
        plane(3 * fs),
        plane(uw, F32), plane(ch), plane(ch),
        vm((n_dp, 16, ch), BF),
        vm((n_dp, 8, ch), F32),
        plane(wid), plane(wid),
        *rs_set, *rs_set,
        vm((tok, wid), F32), vm((tok, wid), F32),
        vm((n_dp, nz, 2, rows, 4 * uw), BF), vm((fs, wid), BF), vm((ch, wid + 128), BF),
        *came(nz), *came(top), *came(top),
        vm((16, 128), F32), vm((1, tok + 256), jnp.int32), vm((n_dp, 16, tok), BF), vm((rows, wid + 128), F32), vm((n_dp, rows, uw), F32),
        vm(segments.shape, jnp.int32), vm((1, lanes), F32), vm((1, lanes), F32), vm(kernel.shape, F32), vm(out_weight.shape, F32),
        dma(7 * 13), dma(7 * 2 * nz), dma(12), dma(12), dma(3), dma(3), dma(3), dma(3), dma(2), dma(2),
        dma(24), dma(24), dma(24), dma(24), dma(10 * nz), dma(10 * nz),
        dma(10 * top), dma(10 * top), dma(10 * top), dma(10 * top), dma(21), dma(21), dma(8 * fs // uw + 8), dma(5),
    ]
    f32 = lambda a: jax.ShapeDtypeStruct(a.shape, F32)
    vspec, anywhere = pl.BlockSpec(memory_space=vm), pl.BlockSpec(memory_space=pl.ANY)
    res = pl.pallas_call(
        functools.partial(block_kernel, dims),
        out_shape=(
            jax.ShapeDtypeStruct(tokens.shape, BF), jax.ShapeDtypeStruct(tokens.shape, BF),
            jax.ShapeDtypeStruct((n_dp, rows, 4 * uw), BF), f32(out_weight), f32(down_weight),
            jax.ShapeDtypeStruct((16, 128), F32),
        ),
        in_specs=[anywhere] * 11,
        out_specs=(anywhere,) * 2 + (vspec,) * 4,
        scratch_shapes=scratch,
        compiler_params=pltpu.CompilerParams(collective_id=0, has_side_effects=True, vmem_limit_bytes=64 * 1024 * 1024),
    )(tokens, cotangent, segments, norm_one[None], norm_two[None], kernel, in_weight, out_weight, gate_weight, up_weight, down_weight)
    final = [jax.ShapeDtypeStruct(v.shape, v.dtype) for v in res[:2]]
    final += [f32(w) for w in (in_weight, out_weight, gate_weight, up_weight, down_weight)]
    final += [jax.ShapeDtypeStruct((k, lanes), F32) for k in (1, 1, 3)]
    moved = pl.pallas_call(
        functools.partial(move_out, (lanes, ch, fs, cj, uw)),
        out_shape=tuple(final),
        in_specs=[anywhere] * 5 + [vspec],
        out_specs=(anywhere,) * 7 + (vspec,) * 3,
        scratch_shapes=[vm(v.shape, v.dtype) for v in res[:5]]
        + [vm(w.shape, F32) for w in (in_weight, gate_weight, up_weight)] + [dma(5), dma(7)],
    )(*res)
    return (*moved[:7], moved[7][0], moved[8][0], moved[9])


def gather(value, axis=0):
    return lax.all_gather(value.astype(BF), ("dp", "seq"), axis=axis, tiled=True)


def norm_back(grad_unit, unit_rows, inverse):
    return inverse * (grad_unit - unit_rows * jnp.mean(grad_unit * unit_rows, axis=1, keepdims=True))


def from_behind(value, axis, steps):
    count = lax.axis_size(axis)
    leading, last = (max(0, -steps), min(count, count - steps))
    return lax.ppermute(value, axis, [(source, source + steps) for source in range(leading, last)])


def spread(value):
    n_dp, n_seq = lax.axis_size("dp"), lax.axis_size("seq")
    shaped = value.reshape((n_dp, n_seq, value.shape[0] // (n_dp * n_seq)) + value.shape[1:]).astype(BF)
    moved = lax.all_to_all(shaped, "seq", split_axis=1, concat_axis=1, tiled=True).astype(F32)
    summed = jnp.sum(moved, axis=1).astype(BF)
    owned = lax.psum_scatter(summed, "dp", scatter_dimension=0, tiled=True).astype(F32)
    return owned.reshape(owned.shape[1:])


def plain_body(tokens, segments, cotangent, in_weight, out_weight, gate_weight, up_weight, down_weight, norm_one, norm_two, kernel):
    width, count = tokens.shape[2], tokens.shape[1]
    in_mat, out_mat, gate_mat, up_mat, down_mat = map(gather, (in_weight, out_weight, gate_weight, up_weight, down_weight))
    gain_a, gain_b = gather(norm_one).astype(F32), gather(norm_two).astype(F32)
    taps = gather(kernel, 1).astype(F32)
    filler = jnp.full((2,), -1, jnp.int32)
    near = lax.dynamic_slice_in_dim(jnp.concatenate([filler, segments[0], filler]), lax.axis_index("seq") * count, count + 4)
    mid = near[2 : count + 2]
    same = lambda first: (mid == near[first : count + first]).astype(F32)[:, None]
    resident = tokens[0].astype(F32)
    inverse_a = lax.rsqrt(jnp.mean(resident * resident, axis=1, keepdims=True) + epsilon)
    unit_a = resident * inverse_a
    normed_a = (unit_a * gain_a).astype(BF)
    mixed = dot_nn(normed_a, in_mat)
    b_part, c_part, x_part = mixed[:, :width], mixed[:, width : 2 * width], mixed[:, 2 * width :]
    conv_in = (b_part * x_part).astype(BF)
    extended = jnp.concatenate([from_behind(conv_in[count - 2 :], "seq", 1), conv_in], axis=0).astype(F32)
    current, prev_one, prev_two = extended[2:], extended[1 : count + 1] * same(1), extended[0:count] * same(0)
    convolved = taps[0] * current + taps[1] * prev_one + taps[2] * prev_two
    gated = (c_part * convolved).astype(BF)
    hidden = resident + dot_nn(gated, out_mat)
    inverse_b = lax.rsqrt(jnp.mean(hidden * hidden, axis=1, keepdims=True) + epsilon)
    unit_b = hidden * inverse_b
    normed_b = (unit_b * gain_b).astype(BF)
    gate_pre, up_pre = dot_nn(normed_b, gate_mat), dot_nn(normed_b, up_mat)
    sig = jax.nn.sigmoid(gate_pre)
    swish = gate_pre * sig
    active = (swish * up_pre).astype(BF)
    output = hidden + dot_nn(active, down_mat)
    grad_low = cotangent[0]
    grad_active = dot_nt(grad_low, down_mat)
    grad_gate_pre = (grad_active * up_pre * sig * (1.0 + gate_pre * (1.0 - sig))).astype(BF)
    grad_up_pre = (grad_active * swish).astype(BF)
    grad_normed_b = dot_nt(grad_gate_pre, gate_mat) + dot_nt(grad_up_pre, up_mat)
    grad_hidden = grad_low.astype(F32) + norm_back(grad_normed_b * gain_b, unit_b, inverse_b)
    grad_branch = grad_hidden.astype(BF)
    grad_gated = dot_nt(grad_branch, out_mat)
    grad_conv = grad_gated * c_part
    ahead = jnp.concatenate([grad_conv, from_behind(grad_conv[:2], "seq", -1)], axis=0)
    grad_conv_in = taps[0] * grad_conv + taps[1] * (ahead[1 : count + 1] * same(3)) + taps[2] * (ahead[2 : count + 2] * same(4))
    grad_taps = jnp.stack([jnp.sum(grad_conv * part, axis=0) for part in (current, prev_one, prev_two)])
    grad_mixed = jnp.concatenate([grad_conv_in * x_part, grad_gated * convolved, grad_conv_in * b_part], axis=1).astype(BF)
    grad_normed_a = dot_nt(grad_mixed, in_mat)
    grad_resident = grad_hidden + norm_back(grad_normed_a * gain_a, unit_a, inverse_a)
    return (
        output.astype(BF)[None],
        grad_resident.astype(BF)[None],
        spread(dot_tn(normed_a, grad_mixed)),
        spread(dot_tn(gated, grad_branch)),
        spread(dot_tn(normed_b, grad_gate_pre)),
        spread(dot_tn(normed_b, grad_up_pre)),
        spread(dot_tn(active, grad_low)),
        spread(jnp.sum(grad_normed_a * unit_a, axis=0)),
        spread(jnp.sum(grad_normed_b * unit_b, axis=0)),
        jnp.transpose(spread(jnp.transpose(grad_taps))),
    )


def solution(mesh):
    n_dp, n_seq = mesh.shape["dp"], mesh.shape["seq"]

    def body(*args):
        tokens, in_weight, gate_weight, down_weight = args[0], args[3], args[5], args[7]
        width = tokens.shape[2]
        unit = 3 * width // max(n_dp, 1)
        fits = (
            n_dp == 4
            and n_seq % 2 == 0
            and tokens.shape[0] == 1
            and in_weight.shape[0] % 16 == 0
            and down_weight.shape[0] % 16 == 0
            and 128 % in_weight.shape[0] == 0
            and unit % 256 == 0
            and 2 * gate_weight.shape[1] == 3 * unit * n_dp
        )
        if fits:
            return fast_body(n_dp, n_seq, *args)
        return plain_body(*args)

    return jax.shard_map(
        body,
        mesh=mesh,
        in_specs=(
            P("dp", "seq", None),
            P("dp", None),
            P("dp", "seq", None),
            P(("dp", "seq"), None),
            P(("dp", "seq"), None),
            P(("dp", "seq"), None),
            P(("dp", "seq"), None),
            P(("dp", "seq"), None),
            P(("dp", "seq")),
            P(("dp", "seq")),
            P(None, ("dp", "seq")),
        ),
        out_specs=(
            P("dp", "seq", None),
            P("dp", "seq", None),
            P(("dp", "seq"), None),
            P(("dp", "seq"), None),
            P(("dp", "seq"), None),
            P(("dp", "seq"), None),
            P(("dp", "seq"), None),
            P(("dp", "seq")),
            P(("dp", "seq")),
            P(None, ("dp", "seq")),
        ),
        check_vma=False,
    )
```
